32 devices in a mesh: img: 8 (over z, y), ty: 2 (over x), tx: 2 (over core).
Axes of the slice: x: 2, y: 2, z: 4, core: 2. Of those that a mesh axis runs over, the one named last changes fastest.
Arguments:
- tokens: bfloat16 [8, 32, 32, 1152], P('img', 'ty', 'tx'), may hold values from -6 to 6
- cond: bfloat16 [8, 1152], P('img'), may hold values from -6 to 6
- live_count: int32 [8], P('img'), may hold values from 1 to 1, as said below
- w_qkv: bfloat16 [1152, 3456], P('img'), may hold values from -0.1875 to 0.1875
- w_out: bfloat16 [1152, 1152], P('img'), may hold values from -0.75 to 0.75
- w_gu: bfloat16 [1152, 6144], P('img'), may hold values from -0.1875 to 0.1875
- w_down: bfloat16 [3072, 1152], P('img'), may hold values from -0.109375 to 0.109375
- w_ada: bfloat16 [1152, 6912], P('img'), may hold values from -0.1875 to 0.1875
- ada_bias: float32 [6912], replicated, may hold values from -3 to 3
- q_gain: float32 [72], replicated, may hold values from 0.8 to 1.6
- k_gain: float32 [72], replicated, may hold values from 0.8 to 1.6
- cotangent: bfloat16 [8, 32, 32, 1152], P('img', 'ty', 'tx'), may hold values from -6 to 6
Outputs:
- output: bfloat16 [8, 32, 32, 1152], P('img', 'ty', 'tx')
- grad_tokens: bfloat16 [8, 32, 32, 1152], P('img', 'ty', 'tx')
- grad_cond: bfloat16 [8, 1152], P('img')
- grad_w_qkv: float32 [1152, 3456], P('img', ('ty', 'tx'))
- grad_w_out: float32 [1152, 1152], P('img', ('ty', 'tx'))
- grad_w_gu: float32 [1152, 6144], P('img', ('ty', 'tx'))
- grad_w_down: float32 [3072, 1152], P('img', ('ty', 'tx'))
- grad_w_ada: float32 [1152, 6912], P('img', ('ty', 'tx'))
- grad_q_gain: float32 [72], replicated
- grad_k_gain: float32 [72], replicated
- grad_ada_bias: float32 [6912], replicated
The draws below stay inside these ranges and needn't reach their ends.
Inputs may be any that keep to these rules, and one draw needn't show every extreme that they name: `live_count`: each index of img holds 1 to 1 live images, in its first slots; in every draw some index holds 1.
All inputs are finite; a program needn't handle non-finite values.
Results may differ from the reference program's by a relative error of at most 0.015.
Values may be sent and summed in bfloat16 or wider, within the bound.
No kernel may reach another device: no remote copies, remote signals or barrier semaphores. Data moves between devices by JAX's collectives and lax.ppermute only.
A program may use at most 320 MiB of HBM per device.

```python
import math
import jax
import jax.numpy as jnp
from jax import lax

D = 1152
HEADS = 16
HEAD = 72
FF = 3072
GRID = 32
SLOTS = 1
IMAGES = 8


def draw_live_count(key, part):
    key = jax.random.fold_in(key, 11)
    first_key, second_key = jax.random.split(key)
    devices_img = IMAGES // SLOTS
    spread = 64
    raw_draw = jax.random.randint(first_key, (devices_img,), 0, spread)
    counts = 1 + 3 * SLOTS * raw_draw * raw_draw // (2 * spread * spread)
    counts = jnp.minimum(counts, SLOTS)
    fullest = jax.random.randint(second_key, (), 0, devices_img)
    counts = jnp.where(jnp.arange(devices_img) == fullest, SLOTS, counts)
    return counts.astype(jnp.int32)


def shard_levels(own_key, dims, cuts, low, largest):
    factor_of = 1.0
    for position, parts in cuts:
        steps = jax.random.uniform(jax.random.fold_in(jax.random.fold_in(own_key, 6), position), (parts,), jnp.float32, low / len(cuts), largest / len(cuts))
        factor_of = factor_of * jnp.repeat(jnp.exp(steps), dims[position] // parts).reshape((-1,) + (1,) * (len(dims) - 1 - position))
    return factor_of


def centred(stream_key, extent, deviation, limit, cuts=(), kind=jnp.bfloat16):
    values = jax.random.normal(stream_key, extent, jnp.float32) * deviation
    if len(cuts) > 0:
        values = shard_levels(stream_key, extent, cuts, -0.22, 0.18) * values
    return jnp.clip(values, min=-limit, max=limit).astype(kind)


def setup_inputs(seed: int = 0) -> dict:
    key_list = jax.random.split(jax.random.key(seed), 13)
    return {
        "tokens": centred(key_list[0], (IMAGES, GRID, GRID, D), 1.0, 6.0, ((0, 8), (1, 2), (2, 2))),
        "cond": centred(key_list[1], (IMAGES, D), 1.0, 6.0, ((0, 8),)),
        "live_count": draw_live_count(jax.random.fold_in(key_list[12], 71), 0),
        "w_qkv": centred(key_list[3], (D, 3 * D), D ** -0.5, 0.1875, ((0, 8),)),
        "w_out": centred(key_list[4], (D, D), (D // 16) ** -0.5, 0.75, ((0, 8),)),
        "w_gu": centred(key_list[5], (D, 2 * FF), D ** -0.5, 0.1875, ((0, 8),)),
        "w_down": centred(key_list[6], (FF, D), FF ** -0.5, 0.109375, ((0, 8),)),
        "w_ada": centred(key_list[7], (D, 6 * D), D ** -0.5, 0.1875, ((0, 8),)),
        "ada_bias": centred(key_list[8], (6 * D,), 0.5, 3.0, (), jnp.float32),
        "q_gain": jnp.clip(jax.random.uniform(key_list[9], (HEAD,), jnp.float32, 0.8, 1.6), 0.8, 1.6),
        "k_gain": jnp.clip(jax.random.uniform(key_list[10], (HEAD,), jnp.float32, 0.8, 1.6), 0.8, 1.6),
        "cotangent": centred(key_list[11], (IMAGES, GRID, GRID, D), 1.0, 6.0, ((0, 8), (1, 2), (2, 2))),
    }


highest = lax.Precision.HIGHEST
epsilon = 1e-06

@jax.custom_vjp
def low(v):
    return lax.optimization_barrier(v.astype(jnp.bfloat16)).astype(jnp.float32)

@jax.custom_vjp
def low_back(v):
    return v

def low_keep(v):
    return (low(v), None)

def low_pass(kept, grad):
    return (grad,)

def back_keep(v):
    return (v, None)

def back_low(kept, grad):
    return (low(grad),)
low.defvjp(low_keep, low_pass)
low_back.defvjp(back_keep, back_low)

def matmul(left, right):
    return jnp.dot(left, right, precision=highest, preferred_element_type=jnp.float32)

def inverse_rms(values):
    return lax.rsqrt(lax.optimization_barrier(jnp.mean(values * values, axis=-1, keepdims=True)) + epsilon)

def rope_tables(row_pos, col_pos, quarter):
    freqs = 10000.0 ** (-jnp.arange(quarter, dtype=jnp.float32) / quarter)
    angles = jnp.stack([row_pos[:, None] * freqs, col_pos[:, None] * freqs], axis=1)
    return (jnp.cos(angles), jnp.sin(angles))

def rotate(values, cosine, sine):
    quarter = values.shape[-1] // 4
    shaped = values.reshape(values.shape[:-1] + (2, 2, quarter))
    first_half = shaped[..., 0, :]
    other_half = shaped[..., 1, :]
    cos_b = cosine[:, None]
    sin_b = sine[:, None]
    turned = jnp.stack([first_half * cos_b - other_half * sin_b, first_half * sin_b + other_half * cos_b], axis=-2)
    return turned.reshape(values.shape)

def one_image(x_img, modulation, live_flag, params, cosine, sine):
    w_qkv, w_out, w_gu, w_down, q_gain, k_gain = params
    shift_a, scale_a, gate_a, shift_b, scale_b, gate_b = jnp.split(modulation, 6)
    tok_count = x_img.shape[0]
    normed_a = x_img * inverse_rms(x_img)
    attn_in = low(normed_a * (1.0 + scale_a) + shift_a)
    qkv_proj = low_back(matmul(attn_in, w_qkv)).reshape(tok_count, 3, HEADS, HEAD)
    q_raw = qkv_proj[:, 0]
    k_raw = qkv_proj[:, 1]
    values_low = low(qkv_proj[:, 2])
    queries = low(rotate(q_raw * inverse_rms(q_raw) * q_gain, cosine, sine))
    keys_low = low(rotate(k_raw * inverse_rms(k_raw) * k_gain, cosine, sine))
    logits = low_back(jnp.einsum('qhd,khd->hqk', queries, keys_low, precision=highest) / math.sqrt(HEAD))
    probs_low = low(jax.nn.softmax(logits, axis=-1))
    mixed_low = low(low_back(jnp.einsum('hqk,khd->qhd', probs_low, values_low, precision=highest))).reshape(tok_count, D)
    attended = low_back(matmul(mixed_low, w_out))
    x_mid = x_img + gate_a * attended
    normed_b = x_mid * inverse_rms(x_mid)
    mlp_in = low(normed_b * (1.0 + scale_b) + shift_b)
    gate_up = low_back(matmul(mlp_in, w_gu))
    hidden_low = low(jax.nn.silu(gate_up[:, :FF]) * gate_up[:, FF:])
    branch = low_back(matmul(hidden_low, w_down))
    return live_flag * (x_mid + gate_b * branch)

def forward(x_all, cond_all, w_qkv, w_out, w_gu, w_down, w_ada, ada_bias, q_gain, k_gain, live_flags, cosine, sine):
    modulation = low_back(matmul(low(jax.nn.silu(cond_all)), w_ada) + ada_bias)
    params = (w_qkv, w_out, w_gu, w_down, q_gain, k_gain)

    def per_image(packed):
        return one_image(packed[0], packed[1], packed[2], params, cosine, sine)
    return lax.map(jax.checkpoint(per_image), (x_all, modulation, live_flags))

def reference(tokens, cond, live_count, w_qkv, w_out, w_gu, w_down, w_ada, ada_bias, q_gain, k_gain, cotangent):
    images = tokens.shape[0]
    image_ids = jnp.arange(images, dtype=jnp.int32)
    owners = (image_ids // SLOTS).astype(jnp.int32)
    live_flags = (image_ids % SLOTS < live_count[owners]).astype(jnp.float32)
    grid_ids = jnp.arange(GRID * GRID, dtype=jnp.int32)
    row_pos = (grid_ids // GRID).astype(jnp.float32)
    col_pos = (grid_ids % GRID).astype(jnp.float32)
    cosine, sine = rope_tables(row_pos, col_pos, HEAD // 4)
    x_all = tokens.astype(jnp.float32).reshape(images, GRID * GRID, D)
    primals = (x_all, cond.astype(jnp.float32), w_qkv.astype(jnp.float32), w_out.astype(jnp.float32), w_gu.astype(jnp.float32), w_down.astype(jnp.float32), w_ada.astype(jnp.float32), ada_bias.astype(jnp.float32), q_gain.astype(jnp.float32), k_gain.astype(jnp.float32))

    def wrapped(x_in, cond_in, qkv_in, out_in, gu_in, down_in, ada_in, bias_in, qgain_in, kgain_in):
        return forward(x_in, cond_in, qkv_in, out_in, gu_in, down_in, ada_in, bias_in, qgain_in, kgain_in, live_flags, cosine, sine)
    outputs, pullback = jax.vjp(wrapped, *primals)
    grads = pullback(cotangent.astype(jnp.float32).reshape(outputs.shape))
    grad_x, grad_cond, g_qkv, g_out, g_gu, g_down, g_ada, g_bias, g_qgain, g_kgain = grads
    return (outputs.reshape(tokens.shape).astype(jnp.bfloat16), grad_x.reshape(tokens.shape).astype(jnp.bfloat16), grad_cond.astype(jnp.bfloat16), g_qkv, g_out, g_gu, g_down, g_ada, g_qgain, g_kgain, g_bias)
```

```python
import functools
import math

import jax
import jax.numpy as jnp
import numpy as np
from jax import lax
from jax.experimental import pallas as pl
from jax.experimental.pallas import tpu as pltpu
from jax.sharding import PartitionSpec as P

HEADS = 16
HEAD = 72
FF = 3072
TILES = 4
OWN = HEADS // TILES
LANES = 128
COLS = OWN * HEAD
PADDED = OWN * LANES
WINDOW = 384
QUARTER = HEAD // 4
EPSILON = 1e-06
LOG2E = math.log2(math.e)
LN2 = math.log(2.0)
BF16 = jnp.bfloat16
F32 = jnp.float32


def head_lane(index):
    part, half, freq = index // 36, (index % 36) // QUARTER, index % QUARTER
    return half * 64 + part * QUARTER + freq


def spread_matrices():
    spread = np.zeros((4, WINDOW, PADDED), np.float32)
    for which in range(4):
        base = (COLS - 256) * which if which < 3 else 0
        for head in range(OWN):
            for index in range(HEAD):
                lane = index if which >= 2 else head_lane(index)
                spread[which, base + HEAD * head + index, LANES * head + lane] = 1.0
    return spread


def dot(left, right):
    return jnp.dot(left, right, preferred_element_type=F32)


def dot_nt(left, right):
    return lax.dot_general(left, right, (((1,), (1,)), ((), ())), preferred_element_type=F32)


def dot_tn(left, right):
    return lax.dot_general(left, right, (((0,), (0,)), ((), ())), preferred_element_type=F32)


def inverse_rms(values):
    return lax.rsqrt(jnp.mean(values * values, axis=-1, keepdims=True) + EPSILON)


def norm_back(grad_out, normed, inv_scale):
    return inv_scale * (grad_out - normed * jnp.mean(grad_out * normed, axis=-1, keepdims=True))


def swap(values, axis):
    return lax.ppermute(values, axis, [(0, 1), (1, 0)])


def gather_rows(values):
    pair = jnp.concatenate([values, swap(values, "ty")])
    return jnp.concatenate([pair, swap(pair, "tx")])


def scatter_rows(partial):
    half = partial.shape[0] // 2
    low = partial.astype(BF16)
    pair = partial[:half].astype(F32) + swap(low[half:], "tx").astype(F32)
    cut = half // 2
    return pair[:cut] + swap(pair[cut:].astype(BF16), "ty").astype(F32)


def sum_tiles(values):
    values = values + swap(values, "tx")
    return values + swap(values, "ty")


def absolute(pieces):
    ty, tx = lax.axis_index("ty"), lax.axis_index("tx")
    turned = [jnp.where(tx == 1, pieces[j ^ 2], pieces[j]) for j in range(4)]
    turned = [jnp.where(ty == 1, turned[j ^ 1], turned[j]) for j in range(4)]
    return [turned[((a & 1) << 1) | (a >> 1)] for a in range(4)]


def tile_at(j):
    return (lax.axis_index("ty") ^ (j & 1)) * 2 + (lax.axis_index("tx") ^ (j >> 1))


def exchange_tiles(piece_for):
    got = [piece_for(tile_at(0))]
    got.append(swap(piece_for(tile_at(1)), "ty"))
    got.append(swap(piece_for(tile_at(2)), "tx"))
    across = [(a * 2 + b, (1 - a) * 2 + 1 - b) for a in range(2) for b in range(2)]
    got.append(lax.ppermute(piece_for(tile_at(3)), ("ty", "tx"), across))
    return absolute(got)


def flip_perm(count, bit):
    return [(i, i ^ bit) for i in range(count)]


def flip_gather(values, count):
    bit = 1
    while bit < count:
        values = jnp.concatenate([values, lax.ppermute(values, "img", flip_perm(count, bit))])
        bit *= 2
    return values


def flip_scatter(values, count):
    bit = count // 2
    while bit >= 1:
        values = values[:bit] + lax.ppermute(values[bit:], "img", flip_perm(count, bit))
        bit //= 2
    return values


def tree_sum(values):
    while values.shape[0] > 1:
        values = values[0::2] + values[1::2]
    return values


def ring_order(count):
    return list(range(0, count, 2)) + list(range(count - 1, 0, -2))


def ring_perm(count, step):
    order = ring_order(count)
    return [(order[i], order[(i + step) % count]) for i in range(count)]


def ring_place(count):
    order = ring_order(count)
    places = np.argsort(np.array(order)).astype(np.int32)
    return jnp.asarray(places)[lax.axis_index("img")], jnp.asarray(np.array(order, np.int32))


def use_ring(count, rows):
    return 2 < count <= 16 and count % 2 == 0 and rows % 16 == 0


def split_rows(rows):
    return (rows // 2 + 15) // 16 * 16


def assemble_kernel(count, rows, cut, index_ref, *refs):
    own, pieces_a, pieces_b = refs[0], refs[1:count], refs[count : 2 * count - 1]
    out_ref, sems = refs[-2], refs[-1]
    copies = [(own, 0, rows)]
    copies += [(piece, 0, cut) for piece in pieces_a]
    copies += [(piece, cut, rows - cut) for piece in pieces_b]
    started = []
    for k, (src, offset, size) in enumerate(copies):
        start = pl.multiple_of(index_ref[k] * rows + offset, 16)
        copy = pltpu.make_async_copy(src, out_ref.at[pl.ds(start, size)], sems.at[k])
        copy.start()
        started.append(copy)
    for copy in started:
        copy.wait()


def gather_weight(own, count):
    rows = own.shape[0]
    if not use_ring(count, rows):
        return lax.all_gather(own, "img", axis=0, tiled=True)
    cut = split_rows(rows)
    a, b = own[:cut], own[cut:]
    pieces_a, pieces_b = [], []
    for _ in range(count - 1):
        a = lax.ppermute(a, "img", ring_perm(count, 1))
        b = lax.ppermute(b, "img", ring_perm(count, -1))
        pieces_a.append(a)
        pieces_b.append(b)
    place, order = ring_place(count)
    steps = jnp.arange(1, count, dtype=jnp.int32)
    index = jnp.concatenate(
        [
            lax.axis_index("img")[None],
            order[(place - steps) % count],
            order[(place + steps) % count],
        ]
    ).astype(jnp.int32)
    copies = 2 * count - 1
    return pl.pallas_call(
        functools.partial(assemble_kernel, count, rows, cut),
        out_shape=jax.ShapeDtypeStruct((count * rows, own.shape[1]), own.dtype),
        in_specs=[pl.BlockSpec(memory_space=pltpu.SMEM)]
        + [pl.BlockSpec(memory_space=pl.ANY)] * copies,
        out_specs=vmem(),
        scratch_shapes=[pltpu.SemaphoreType.DMA((copies,))],
        name="assemble",
    )(index, own, *pieces_a, *pieces_b)


def scatter_weight(grad, count, kind):
    rows = grad.shape[0] // count
    if kind == "call" or not use_ring(count, rows):
        return lax.psum_scatter(grad, "img", scatter_dimension=0, tiled=True).astype(F32)
    cut = split_rows(rows)
    place, order = ring_place(count)
    outs = []
    for sign, offset, size in ((1, 0, cut), (-1, cut, rows - cut)):

        def part(step, offset=offset, size=size, sign=sign):
            owner = order[(place - sign * step) % count]
            return lax.dynamic_slice_in_dim(grad, owner * rows + offset, size, 0)

        total = part(1)
        for step in range(2, count + 1):
            total = lax.ppermute(total, "img", ring_perm(count, sign))
            total = total.astype(F32) + part(step).astype(F32)
            if step < count:
                total = total.astype(BF16)
        outs.append(total)
    return jnp.concatenate(outs)


def vmem():
    return pl.BlockSpec(memory_space=pltpu.VMEM)


def lane_ids(rows):
    return lax.broadcasted_iota(jnp.int32, (rows, LANES), 1)


def three_parts(column):
    high = column.astype(BF16)
    rest = column - high.astype(F32)
    mid = rest.astype(BF16)
    return high, mid, (rest - mid.astype(F32)).astype(BF16)


def put_lanes(values, first, parts):
    lanes = lane_ids(values.shape[0])
    for k, part in enumerate(parts):
        values = jnp.where(lanes == first + k, part.astype(values.dtype), values)
    return values


QK_SPARE = 100
V_SPARE = HEAD


def attention_kernel(
    x_ref, shift_ref, scale_ref, w_ref, cos_ref, sin_ref, gq_ref, gk_ref, spread_ref,
    attn_ref, qraw_ref, kraw_ref, q_ref, k_ref, v_ref, mixedp_ref, mixed_ref, wpad_ref,
):
    tokens = x_ref.shape[0]
    block = 256
    factor = LOG2E / math.sqrt(HEAD)

    @pl.loop(0, w_ref.shape[0] // 128)
    def _(i):
        rows = pl.ds(pl.multiple_of(i * 128, 128), 128)
        for w in range(3):
            wpad_ref[rows, PADDED * w : PADDED * (w + 1)] = dot(
                w_ref[rows, 256 * w : 256 * w + WINDOW], spread_ref[w]
            ).astype(BF16)

    @pl.loop(0, tokens // block)
    def _(i):
        rows = pl.ds(pl.multiple_of(i * block, block), block)
        x = x_ref[rows, :].astype(F32)
        normed = x * inverse_rms(x)
        attn_in = (normed * (1.0 + scale_ref[...]) + shift_ref[...]).astype(BF16)
        attn_ref[rows, :] = attn_in
        cos, sin = cos_ref[rows, :], sin_ref[rows, :]
        lanes = lane_ids(block)
        spare = (lanes >= QK_SPARE) & (lanes < QK_SPARE + 3)
        for which, raw_ref, out_ref, gain_ref in (
            (0, qraw_ref, q_ref, gq_ref),
            (1, kraw_ref, k_ref, gk_ref),
        ):
            raw = dot(attn_in, wpad_ref[:, PADDED * which : PADDED * (which + 1)])
            raw_ref[rows, :] = raw
            for head in range(OWN):
                at = slice(LANES * head, LANES * (head + 1))
                part = raw[:, at]
                inv = lax.rsqrt(jnp.sum(part * part, axis=-1, keepdims=True) / HEAD + EPSILON)
                scaled = part * inv * gain_ref[...]
                turned = scaled * cos + pltpu.roll(scaled, 64, 1) * sin
                if which == 0:
                    out_ref[rows, at] = (turned * factor).astype(BF16)
                else:
                    out_ref[rows, at] = jnp.where(spare, 1.0, turned).astype(BF16)
        value = dot(attn_in, wpad_ref[:, PADDED * 2 : PADDED * 3])
        ones = (lanes >= V_SPARE) & (lanes < V_SPARE + 3)
        for head in range(OWN):
            at = slice(LANES * head, LANES * (head + 1))
            v_ref[rows, at] = jnp.where(ones, 1.0, value[:, at]).astype(BF16)

    @pl.loop(0, tokens // block)
    def _(i):
        rows = pl.ds(pl.multiple_of(i * block, block), block)
        for head in range(OWN):
            at = slice(LANES * head, LANES * (head + 1))
            query = q_ref[rows, at]
            logits = dot_nt(query, k_ref[:, at])
            terms = jnp.exp2(logits).astype(BF16)
            result = dot(terms, v_ref[:, at])
            total = result[:, V_SPARE : V_SPARE + 1]
            mixedp_ref[rows, at] = (result * (1.0 / total)).astype(BF16)
            q_ref[rows, at] = put_lanes(query, QK_SPARE, three_parts(-jnp.log2(total)))
        mixed_ref[rows, :] = dot_nt(mixedp_ref[rows, :], spread_ref[3]).astype(BF16)[:, :COLS]


def attention_forward(x, shift, scale, w, cos, sin, gq, gk, spread):
    tokens, width = x.shape
    return pl.pallas_call(
        attention_kernel,
        out_shape=[
            jax.ShapeDtypeStruct((tokens, width), BF16),
            jax.ShapeDtypeStruct((tokens, PADDED), F32),
            jax.ShapeDtypeStruct((tokens, PADDED), F32),
            jax.ShapeDtypeStruct((tokens, PADDED), BF16),
            jax.ShapeDtypeStruct((tokens, PADDED), BF16),
            jax.ShapeDtypeStruct((tokens, PADDED), BF16),
            jax.ShapeDtypeStruct((tokens, PADDED), BF16),
            jax.ShapeDtypeStruct((tokens, COLS), BF16),
        ],
        in_specs=[vmem()] * 9,
        out_specs=[vmem()] * 8,
        scratch_shapes=[pltpu.VMEM((width, 3 * PADDED), BF16)],
        compiler_params=pltpu.CompilerParams(vmem_limit_bytes=56 * 1024 * 1024),
        name="attention_forward",
    )(x, shift, scale, w, cos, sin, gq, gk, spread)


def attention_back_kernel(
    grad_ref, qraw_ref, kraw_ref, q_ref, k_ref, v_ref, mixedp_ref, cos_ref, sin_ref, gq_ref, gk_ref,
    spread_ref, out_ref, gains_ref, do_ref, dq_ref, dk_ref, pad_ref,
):
    tokens = grad_ref.shape[0]
    block = 256
    root = 1.0 / math.sqrt(HEAD)

    @pl.loop(0, tokens // block)
    def _(i):
        rows = pl.ds(pl.multiple_of(i * block, block), block)
        wide = dot(grad_ref[rows, :], spread_ref[3, :COLS, :])
        for head in range(OWN):
            at = slice(LANES * head, LANES * (head + 1))
            part = wide[:, at]
            row_dot = jnp.sum(part * mixedp_ref[rows, at].astype(F32), axis=-1, keepdims=True)
            do_ref[rows, at] = put_lanes(part.astype(BF16), V_SPARE, three_parts(-row_dot))

    for head in range(OWN):
        at = slice(LANES * head, LANES * (head + 1))
        dq_ref[at, :] = jnp.zeros((LANES, tokens), F32)

        @pl.loop(0, tokens // block)
        def _(i):
            rows = pl.ds(pl.multiple_of(i * block, block), block)
            query, grad = q_ref[:, at], do_ref[:, at]
            key = k_ref[rows, at]
            probs = jnp.exp2(dot_nt(key, query))
            slope = (probs * dot_nt(v_ref[rows, at], grad)).astype(BF16)
            pad_ref[rows, 2 * PADDED + LANES * head : 2 * PADDED + LANES * (head + 1)] = dot(
                probs.astype(BF16), grad
            ).astype(BF16)
            dk_ref[rows, at] = dot(slope, query) * LN2
            dq_ref[at, :] += dot(key.astype(F32).T.astype(BF16), slope)

    gains_ref[...] = jnp.zeros_like(gains_ref)

    @pl.loop(0, tokens // block)
    def _(i):
        rows = pl.ds(pl.multiple_of(i * block, block), block)
        cos, sin = cos_ref[rows, :], sin_ref[rows, :]
        for which, raw_ref, gain_ref in ((0, qraw_ref, gq_ref), (1, kraw_ref, gk_ref)):
            gained = jnp.zeros((1, LANES), F32)
            for head in range(OWN):
                at = slice(LANES * head, LANES * (head + 1))
                raw = raw_ref[rows, at]
                inv = lax.rsqrt(jnp.sum(raw * raw, axis=-1, keepdims=True) / HEAD + EPSILON)
                hat = raw * inv
                if which == 0:
                    grad = dq_ref[at, rows].T * root
                else:
                    grad = dk_ref[rows, at]
                turned = grad * cos - pltpu.roll(grad, 64, 1) * sin
                product = turned * hat
                gained += jnp.sum(product, axis=0, keepdims=True)
                mean = jnp.sum(product * gain_ref[...], axis=-1, keepdims=True) / HEAD
                pad_ref[rows, PADDED * which + LANES * head : PADDED * which + LANES * (head + 1)] = (
                    inv * (turned * gain_ref[...] - hat * mean)
                ).astype(BF16)
            gains_ref[which : which + 1, :] += gained
        compact = [
            dot_nt(pad_ref[rows, PADDED * w : PADDED * (w + 1)], spread_ref[w]).astype(BF16)
            for w in range(3)
        ]
        out_ref[rows, :] = jnp.concatenate(
            [
                compact[0][:, :256],
                compact[0][:, 256:] + compact[1][:, :128],
                compact[1][:, 128:256],
                compact[1][:, 256:] + compact[2][:, :128],
                compact[2][:, 128:],
            ],
            axis=1,
        )[:, : 3 * COLS]


def attention_backward(grad, qraw, kraw, q, k, v, mixedp, cos, sin, gq, gk, spread):
    tokens = grad.shape[0]
    return pl.pallas_call(
        attention_back_kernel,
        out_shape=[
            jax.ShapeDtypeStruct((tokens, 3 * COLS), BF16),
            jax.ShapeDtypeStruct((8, LANES), F32),
        ],
        in_specs=[vmem()] * 12,
        out_specs=[vmem()] * 2,
        scratch_shapes=[
            pltpu.VMEM((tokens, PADDED), BF16),
            pltpu.VMEM((PADDED, tokens), F32),
            pltpu.VMEM((tokens, PADDED), F32),
            pltpu.VMEM((tokens, 3 * PADDED), BF16),
        ],
        compiler_params=pltpu.CompilerParams(vmem_limit_bytes=56 * 1024 * 1024),
        name="attention_backward",
    )(grad, qraw, kraw, q, k, v, mixedp, cos, sin, gq, gk, spread)


def rope_lanes(tile_rows, tile_cols):
    freq = np.zeros((LANES,), np.float32)
    part = np.zeros((LANES,), np.int32)
    sign = np.zeros((LANES,), np.float32)
    for index in range(HEAD):
        lane = head_lane(index)
        part[lane] = index // 36
        sign[lane] = 1.0 if lane >= 64 else -1.0
    freqs = 10000.0 ** (-jnp.arange(QUARTER, dtype=F32) / QUARTER)
    half = jnp.concatenate([freqs, freqs, jnp.zeros((64 - 2 * QUARTER,), F32)])
    freq = jnp.concatenate([half, half])
    ids = np.arange(tile_rows * tile_cols)
    rows, cols = [], []
    for j in range(4):
        ty, tx = lax.axis_index("ty") ^ (j & 1), lax.axis_index("tx") ^ (j >> 1)
        rows.append(ty * tile_rows + jnp.asarray(ids // tile_cols, jnp.int32))
        cols.append(tx * tile_cols + jnp.asarray(ids % tile_cols, jnp.int32))
    rows = jnp.concatenate(rows).astype(F32)[:, None]
    cols = jnp.concatenate(cols).astype(F32)[:, None]
    angle = jnp.where(jnp.asarray(part)[None] == 0, rows, cols) * freq[None]
    live = jnp.asarray((sign != 0).astype(np.float32))[None]
    return jnp.cos(angle) * live, jnp.sin(angle) * jnp.asarray(sign)[None]


def gain_lanes(gain):
    parts = gain.reshape(2, 2, QUARTER).transpose(1, 0, 2).reshape(2, 2 * QUARTER)
    return jnp.pad(parts, ((0, 0), (0, 64 - 2 * QUARTER))).reshape(1, LANES)


def gain_back(lanes):
    parts = lanes.reshape(2, 64)[:, : 2 * QUARTER].reshape(2, 2, QUARTER)
    return parts.transpose(1, 0, 2).reshape(HEAD)


def body(
    count, tokens, cond, live_count, w_qkv, w_out, w_gu, w_down, w_ada, ada_bias, q_gain, k_gain, cotangent
):
    _, tile_rows, tile_cols, width = tokens.shape
    per_tile = tile_rows * tile_cols
    img, ty, tx = lax.axis_index("img"), lax.axis_index("ty"), lax.axis_index("tx")
    tile = ty * 2 + tx
    live = (live_count[0] > 0).astype(F32)
    shard = width // count
    ff_shard = FF // count
    ff_own = ff_shard // TILES
    hidden_own = FF // TILES
    spread = jnp.asarray(spread_matrices(), BF16)

    first = jnp.concatenate(
        [lax.dynamic_slice_in_dim(w_qkv, p * width + tile * COLS, COLS, 1) for p in range(3)]
        + [lax.dynamic_slice_in_dim(w_out, tile * (width // TILES), width // TILES, 1)],
        axis=1,
    )
    full_first = gather_weight(first, count)
    gu_own = lax.dynamic_slice_in_dim(w_gu.reshape(shard, 2 * count, ff_shard), tile * ff_own, ff_own, 2)
    full_gu = gather_weight(gu_own.reshape(shard, 2 * hidden_own), count)
    full_down = gather_weight(lax.dynamic_slice_in_dim(w_down, tile * ff_own, ff_own, 0), count)

    x_all = gather_rows(tokens.reshape(per_tile, width))
    dy_all = gather_rows(cotangent.reshape(per_tile, width))

    cond_float = cond.astype(F32)
    silu_all = flip_gather(jax.nn.silu(cond_float).astype(BF16), count)
    silu_rows = lax.dynamic_slice_in_dim(silu_all, img * shard, shard, 1)
    modulation = flip_scatter(dot(silu_rows, w_ada), count) + ada_bias
    shift_a, scale_a, gate_a, shift_b, scale_b, gate_b = [
        modulation[:, k * width : (k + 1) * width] for k in range(6)
    ]

    cos, sin = rope_lanes(tile_rows, tile_cols)
    gq, gk = gain_lanes(q_gain), gain_lanes(k_gain)
    attn_in, qraw, kraw, queries, keys, values, mixedp, mixed = attention_forward(
        x_all, shift_a, scale_a, full_first, cos, sin, gq, gk, spread
    )

    def turn(v, flip):
        blocks = [v[per_tile * b : per_tile * (b + 1)] for b in range(4)]
        return jnp.concatenate([blocks[b ^ flip] for b in range(4)])

    mixed_pair = jnp.concatenate([mixed, turn(swap(mixed, "ty"), 1)], axis=1)
    mixed_all = jnp.concatenate([mixed_pair, turn(swap(mixed_pair, "tx"), 2)], axis=1)

    out_cols = full_first[:, 3 * COLS :]
    out_pair = swap(out_cols, "ty")
    pieces = [out_cols, out_pair, swap(out_cols, "tx"), swap(out_pair, "tx")]
    out_abs = jnp.concatenate(absolute(pieces), axis=1)
    full_out = jnp.concatenate(
        [lax.dynamic_slice_in_dim(out_abs, tile_at(j) * COLS, COLS, 0) for j in range(4)]
    )

    x_float = x_all.astype(F32)
    attended = dot(mixed_all, full_out)
    x_mid = x_float + gate_a * attended
    inv_b = inverse_rms(x_mid)
    normed_b = x_mid * inv_b
    mlp_in = (normed_b * (1.0 + scale_b) + shift_b).astype(BF16)
    gate_up = dot(mlp_in, full_gu)
    gate, up = gate_up[:, :hidden_own], gate_up[:, hidden_own:]
    sigmoid = jax.nn.sigmoid(gate)
    silu_g = gate * sigmoid
    hidden = (silu_g * up).astype(BF16)
    branch = scatter_rows(dot(hidden, full_down))
    x_mid_own = x_mid[:per_tile]
    output = (live * (x_mid_own + gate_b * branch)).astype(BF16)

    dy = live * dy_all.astype(F32)
    dy_own = dy[:per_tile]
    grad_gate_b = jnp.sum(dy_own * branch, axis=0, keepdims=True)
    grad_branch = (gate_b * dy).astype(BF16)
    g_down = dot_tn(hidden, grad_branch).astype(BF16)
    grad_hidden = dot_nt(grad_branch, full_down)
    grad_gu = jnp.concatenate(
        [grad_hidden * up * sigmoid * (1.0 + gate * (1.0 - sigmoid)), grad_hidden * silu_g], axis=1
    ).astype(BF16)
    g_gu = dot_tn(mlp_in, grad_gu).astype(BF16)
    grad_mlp_in = scatter_rows(dot_nt(grad_gu, full_gu))
    normed_own = normed_b[:per_tile]
    grad_scale_b = jnp.sum(grad_mlp_in * normed_own, axis=0, keepdims=True)
    grad_shift_b = jnp.sum(grad_mlp_in, axis=0, keepdims=True)
    grad_mid = dy_own + norm_back(grad_mlp_in * (1.0 + scale_b), normed_own, inv_b[:per_tile])
    grad_gate_a = jnp.sum(grad_mid * attended[:per_tile], axis=0, keepdims=True)
    grad_att = gather_rows((gate_a * grad_mid).astype(BF16))

    out_width = width // TILES
    g_out = dot_tn(mixed_all, lax.dynamic_slice_in_dim(grad_att, tile * out_width, out_width, 1))
    g_out = jnp.concatenate(
        absolute([g_out[COLS * j : COLS * (j + 1)].astype(BF16) for j in range(4)])
    )
    grad_mixed = dot_nt(grad_att, full_out[:COLS]).astype(BF16)
    grad_qkv, gains = attention_backward(
        grad_mixed, qraw, kraw, queries, keys, values, mixedp, cos, sin, gq, gk, spread
    )
    g_qkv = dot_tn(attn_in, grad_qkv).astype(BF16)
    grad_attn_in = scatter_rows(dot_nt(grad_qkv, full_first[:, : 3 * COLS]))
    x_own = x_float[:per_tile]
    inv_a = inverse_rms(x_own)
    normed_a = x_own * inv_a
    grad_scale_a = jnp.sum(grad_attn_in * normed_a, axis=0, keepdims=True)
    grad_shift_a = jnp.sum(grad_attn_in, axis=0, keepdims=True)
    grad_tokens = (grad_mid + norm_back(grad_attn_in * (1.0 + scale_a), normed_a, inv_a)).astype(BF16)

    grad_mod = jnp.concatenate(
        [grad_shift_a, grad_scale_a, grad_gate_a, grad_shift_b, grad_scale_b, grad_gate_b], axis=1
    )
    grad_mod = sum_tiles(grad_mod)
    gain_sums = sum_tiles(gains[:2])
    gain_sums = tree_sum(flip_gather(gain_sums.reshape(1, 2 * LANES), count))
    mod_all = flip_gather(grad_mod.astype(BF16), count)
    grad_bias = tree_sum(mod_all.astype(F32)).reshape(-1)
    ada_cols = mod_all.shape[1] // TILES
    grad_ada = dot_tn(silu_rows, lax.dynamic_slice_in_dim(mod_all, tile * ada_cols, ada_cols, 1))
    grad_silu = flip_gather(dot_nt(mod_all, w_ada).reshape(1, count * shard), count)
    grad_silu = grad_silu.reshape(count, count, shard)
    flips = jnp.arange(count) ^ img
    grad_silu = grad_silu[flips, flips].reshape(1, width)
    sigmoid_c = jax.nn.sigmoid(cond_float)
    grad_cond = (grad_silu * sigmoid_c * (1.0 + cond_float * (1.0 - sigmoid_c))).astype(BF16)

    s_down = scatter_weight(g_down, count, "ring").astype(BF16)
    s_gu = scatter_weight(g_gu, count, "ring").astype(BF16)
    s_out = scatter_weight(g_out, count, "ring")
    s_qkv = scatter_weight(g_qkv, count, "ring").astype(BF16)

    down_cols = width // TILES
    grad_down = jnp.concatenate(
        exchange_tiles(lambda t: lax.dynamic_slice_in_dim(s_down, t * down_cols, down_cols, 1))
    ).astype(F32)
    gu_cols = 2 * hidden_own // TILES
    got = exchange_tiles(lambda t: lax.dynamic_slice_in_dim(s_gu, t * gu_cols, gu_cols, 1))
    groups = gu_cols // ff_own
    grad_w_gu = jnp.concatenate(
        [got[s][:, ff_own * g : ff_own * (g + 1)] for g in range(groups) for s in range(4)], axis=1
    ).astype(F32)
    units = jnp.stack([s_qkv[:, COLS * p : COLS * (p + 1)] for p in range(3)])

    def unit(table):
        return lax.dynamic_index_in_dim(units, jnp.asarray(table, jnp.int32)[tile], 0, keepdims=False)

    kept = unit([0, 1, 1, 2])
    from_tx = swap(unit([1, 0, 2, 1]), "tx")
    from_ty = swap(unit([2, 2, 0, 0]), "ty")
    slots = jnp.stack([kept, from_tx, from_ty])
    places = jnp.asarray([[0, 1, 2], [2, 1, 0], [0, 1, 2], [2, 1, 0]], jnp.int32)[tile]
    grad_w_qkv = jnp.concatenate(
        [lax.dynamic_index_in_dim(slots, places[k], 0, keepdims=False) for k in range(3)], axis=1
    ).astype(F32)

    return (
        output.reshape(tokens.shape),
        grad_tokens.reshape(tokens.shape),
        grad_cond,
        grad_w_qkv,
        s_out,
        grad_w_gu,
        grad_down,
        grad_ada,
        gain_back(gain_sums[0, :LANES]),
        gain_back(gain_sums[0, LANES:]),
        grad_bias,
    )


def solution(mesh):
    tiled = P("img", "ty", "tx", None)
    rows = P("img", None)
    cut = P("img", ("ty", "tx"))
    in_specs = (tiled, rows, P("img"), rows, rows, rows, rows, rows, P(), P(), P(), tiled)
    out_specs = (tiled, tiled, rows, cut, cut, cut, cut, cut, P(), P(), P())
    return jax.shard_map(
        functools.partial(body, mesh.shape["img"]),
        mesh=mesh,
        in_specs=in_specs,
        out_specs=out_specs,
        check_vma=False,
    )
```

```python
import functools
import math

import jax
import jax.numpy as jnp
import numpy as np
from jax import lax
from jax.experimental import pallas as pl
from jax.experimental.pallas import tpu as pltpu
from jax.sharding import PartitionSpec as P

HEADS = 16
HEAD = 72
FF = 3072
TILES = 4
OWN = HEADS // TILES
LANES = 128
COLS = OWN * HEAD
PADDED = OWN * LANES
WINDOW = 384
QUARTER = HEAD // 4
EPSILON = 1e-06
LOG2E = math.log2(math.e)
LN2 = math.log(2.0)
BF16 = jnp.bfloat16
F32 = jnp.float32


def head_lane(index):
    part, half, freq = index // 36, (index % 36) // QUARTER, index % QUARTER
    return half * 64 + part * QUARTER + freq


def spread_matrices():
    spread = np.zeros((4, WINDOW, PADDED), np.float32)
    for which in range(4):
        base = (COLS - 256) * which if which < 3 else 0
        for head in range(OWN):
            for index in range(HEAD):
                lane = index if which >= 2 else head_lane(index)
                spread[which, base + HEAD * head + index, LANES * head + lane] = 1.0
    return spread


def dot(left, right):
    return jnp.dot(left, right, preferred_element_type=F32)


def dot_nt(left, right):
    return lax.dot_general(left, right, (((1,), (1,)), ((), ())), preferred_element_type=F32)


def dot_tn(left, right):
    return lax.dot_general(left, right, (((0,), (0,)), ((), ())), preferred_element_type=F32)


def inverse_rms(values):
    return lax.rsqrt(jnp.mean(values * values, axis=-1, keepdims=True) + EPSILON)


def norm_back(grad_out, normed, inv_scale):
    return inv_scale * (grad_out - normed * jnp.mean(grad_out * normed, axis=-1, keepdims=True))


def swap(values, axis):
    return lax.ppermute(values, axis, [(0, 1), (1, 0)])


FLIPS = (2, 3, 0, 1)


def tile_at(flip):
    return (lax.axis_index("ty") ^ (flip >> 1)) * 2 + (lax.axis_index("tx") ^ (flip & 1))


def gather_tiles(values):
    far = swap(values, "ty")
    return [far, swap(far, "tx"), values, swap(values, "tx")]


def sum_tiles(values):
    values = values + swap(values, "tx")
    return values + swap(values, "ty")


def absolute(pieces):
    ty, tx = lax.axis_index("ty"), lax.axis_index("tx")
    turned = [jnp.where(tx == 1, pieces[f ^ 1], pieces[f]) for f in range(4)]
    return [jnp.where(ty == 1, turned[f ^ 2], turned[f]) for f in range(4)]


def exchange_tiles(piece_for):
    across = [(a * 2 + b, (1 - a) * 2 + 1 - b) for a in range(2) for b in range(2)]
    return absolute(
        [
            piece_for(tile_at(0)),
            swap(piece_for(tile_at(1)), "tx"),
            swap(piece_for(tile_at(2)), "ty"),
            lax.ppermute(piece_for(tile_at(3)), ("ty", "tx"), across),
        ]
    )


def flip_perm(count, bit):
    return [(i, i ^ bit) for i in range(count)]


def flip_exchange(values, count, bits):
    rows = [values[k : k + 1] for k in range(count)]
    for bit in bits:
        sent = jnp.concatenate([rows[k] for k in range(count) if k & bit])
        got = lax.ppermute(sent, "img", flip_perm(count, bit))
        moved = [k for k in range(count) if k & bit]
        for place, k in enumerate(moved):
            rows[k] = got[place : place + 1]
    return jnp.concatenate(rows)


def ring_perm(count, step):
    order = list(range(0, count, 2)) + list(range(count - 1, 0, -2))
    return [(order[i], order[(i + step) % count]) for i in range(count)]


def ring_place(count):
    index = lax.axis_index("img")
    return jnp.where(index % 2 == 0, index // 2, count - 1 - index // 2)


def ring_owner(count, place):
    place = (place + count) % count
    return jnp.where(place < count // 2, 2 * place, 2 * (count - 1 - place) + 1)


def use_ring(count, rows):
    return 2 < count <= 16 and count % 2 == 0 and rows % 16 == 0


def split_rows(rows):
    return (rows // 2 + 15) // 16 * 16


def out_share(pick, first):
    return dot_nt(pick, first[:, first.shape[1] - WINDOW :]).astype(BF16)


def ring_gather(own, count, beside):
    cut = split_rows(own.shape[0])
    a, b = own[:cut], own[cut:]
    pieces, value = [], None
    for hop in range(count - 1):
        a = lax.ppermute(a, "img", ring_perm(count, 1))
        b = lax.ppermute(b, "img", ring_perm(count, -1))
        if hop < len(beside):
            value = beside[hop](value)
            a, b, value = lax.optimization_barrier((a, b, value))
        pieces.append((a, b))
    for step in beside[count - 1 :]:
        value = step(value)
    return pieces, value


def assemble_kernel(count, total, plan, shared, index_ref, pick_ref, *refs):
    cut = split_rows(total)
    own, pieces_a, pieces_b = refs[0], refs[1:count], refs[count : 2 * count - 1]
    outs, sems = refs[2 * count - 1 : -1], refs[-1]
    started = []
    for k, (src, first, size) in enumerate(
        [(own, 0, total)]
        + [(piece, 0, cut) for piece in pieces_a]
        + [(piece, cut, total - cut) for piece in pieces_b]
    ):
        for out, rows, base, count_rows, to_row, from_lane, to_lane, lanes in plan:
            low, high = max(first, base), min(first + size, base + count_rows)
            if low < high:
                start = pl.multiple_of(index_ref[k] * rows + to_row + low - base, 16)
                copy = pltpu.make_async_copy(
                    src.at[pl.ds(low - first, high - low), pl.ds(from_lane, lanes)],
                    outs[out].at[pl.ds(start, high - low), pl.ds(to_lane, lanes)],
                    sems.at[len(started)],
                )
                copy.start()
                started.append(copy)
    for copy in started:
        copy.wait()
    if shared:
        outs[-1][...] = out_share(pick_ref[...], outs[0])


def assemble(own, pieces, shapes, plan, count, shared):
    place = ring_place(count)
    steps = jnp.asarray([0] + [-k for k in range(1, count)] + list(range(1, count)), jnp.int32)
    index = ring_owner(count, place + steps).astype(jnp.int32)
    copies = 2 * count - 1
    shapes = [jax.ShapeDtypeStruct(shape, own.dtype) for shape in shapes]
    return pl.pallas_call(
        functools.partial(assemble_kernel, count, own.shape[0], plan, shared),
        out_shape=shapes,
        in_specs=[smem(), vmem()] + [pl.BlockSpec(memory_space=pltpu.HBM)] * copies,
        out_specs=[vmem() for _ in shapes],
        scratch_shapes=[pltpu.SemaphoreType.DMA((2 * len(plan) * copies,))],
        compiler_params=limit(58),
        cost_estimate=cost(5),
        name="assemble_first" if shared else "assemble_gu",
    )(index, out_pick(), own, *[a for a, _ in pieces], *[b for _, b in pieces])


def out_pick():
    pick = np.zeros((COLS, WINDOW), np.float32)
    pick[np.arange(COLS), WINDOW - COLS + np.arange(COLS)] = 1.0
    return jnp.asarray(pick, BF16)


def after(value, *others):
    return lax.optimization_barrier((value, others))[0]


def ring_scatter(grads, count, beside):
    sizes = [grad.shape[0] // count for grad in grads]
    total = sum(sizes)
    cut = split_rows(total)
    place = ring_place(count)
    value = None

    def part(sign, step):
        owner = ring_owner(count, place - sign * step)
        first, last = (0, cut) if sign > 0 else (cut, total)
        found, base = [], 0
        for grad, rows in zip(grads, sizes):
            low, high = max(first, base), min(last, base + rows)
            if low < high:
                found.append(lax.dynamic_slice_in_dim(grad, owner * rows + low - base, high - low, 0))
            base += rows
        return jnp.concatenate(found)

    sums = [part(1, 1), part(-1, 1)]
    for step in range(2, count + 1):
        kind = BF16 if step < count else F32
        got = [lax.ppermute(sums[k], "img", ring_perm(count, sign)) for k, sign in enumerate((1, -1))]
        if step - 2 < len(beside) and beside[step - 2]:
            value = beside[step - 2](value)
            got, value = lax.optimization_barrier((got, value))
        for k, sign in enumerate((1, -1)):
            sums[k] = (got[k].astype(F32) + part(sign, step).astype(F32)).astype(kind)
    for step in beside[count - 1 :]:
        value = step(value)
    return sums, value


def vmem():
    return pl.BlockSpec(memory_space=pltpu.VMEM)


def limit(megabytes):
    return pltpu.CompilerParams(vmem_limit_bytes=megabytes * 1024 * 1024)


def cost(microseconds):
    return pl.CostEstimate(
        flops=int(microseconds * 1.1e9), bytes_accessed=int(microseconds * 3e6), transcendentals=0
    )


def lane_ids(rows):
    return lax.broadcasted_iota(jnp.int32, (rows, LANES), 1)


def three_parts(column):
    high = column.astype(BF16)
    rest = column - high.astype(F32)
    mid = rest.astype(BF16)
    return high, mid, (rest - mid.astype(F32)).astype(BF16)


def put_lanes(values, first, parts):
    lanes = lane_ids(values.shape[0])
    for k, part in enumerate(parts):
        values = jnp.where(lanes == first + k, part.astype(values.dtype), values)
    return values


QK_SPARE = 100
V_SPARE = HEAD


PAIRS = OWN // 2
PAIR = 2 * LANES
PAIR_COLS = 2 * HEAD


def project_kernel(
    x0_ref, x1_ref, x2_ref, x3_ref, mod_ref, w_ref, cos_ref, sin_ref, gq_ref, gk_ref, spread_ref,
    attn_ref, qraw_ref, kraw_ref, q0_ref, q1_ref, k0_ref, k1_ref, v0_ref, v1_ref, wpad_ref,
):
    block = x0_ref.shape[0]
    tokens = 4 * block
    factor = LOG2E / math.sqrt(HEAD)

    for place, x_ref in enumerate((x0_ref, x1_ref, x2_ref, x3_ref)):
        x = x_ref[...].astype(F32)
        normed = x * inverse_rms(x)
        attn_ref[block * place : block * (place + 1), :] = (
            normed * (1.0 + mod_ref[1:2, :]) + mod_ref[0:1, :]
        ).astype(BF16)

    @pl.loop(0, w_ref.shape[0] // 128)
    def _(i):
        rows = pl.ds(pl.multiple_of(i * 128, 128), 128)
        for w in range(3):
            wpad_ref[rows, PADDED * w : PADDED * (w + 1)] = dot(
                w_ref[rows, 256 * w : 256 * w + WINDOW], spread_ref[w]
            ).astype(BF16)

    @pl.loop(0, tokens // block)
    def _(i):
        rows = pl.ds(pl.multiple_of(i * block, block), block)
        attn_in = attn_ref[rows, :]
        cos, sin = cos_ref[rows, :], sin_ref[rows, :]
        lanes = lane_ids(block)
        spare = (lanes >= QK_SPARE) & (lanes < QK_SPARE + 3)
        for which, raw_ref, out_refs, gain_ref in (
            (0, qraw_ref, (q0_ref, q1_ref), gq_ref),
            (1, kraw_ref, (k0_ref, k1_ref), gk_ref),
        ):
            raw = dot(attn_in, wpad_ref[:, PADDED * which : PADDED * (which + 1)])
            raw_ref[rows, :] = raw
            for head in range(OWN):
                part = raw[:, LANES * head : LANES * (head + 1)]
                inv = lax.rsqrt(jnp.sum(part * part, axis=-1, keepdims=True) / HEAD + EPSILON)
                scaled = part * inv * gain_ref[...]
                turned = scaled * cos + pltpu.roll(scaled, 64, 1) * sin
                turned = turned * factor if which == 0 else jnp.where(spare, 1.0, turned)
                at = slice(LANES * (head % 2), LANES * (head % 2 + 1))
                out_refs[head // 2][rows, at] = turned.astype(BF16)
        value = dot(attn_in, wpad_ref[:, PADDED * 2 : PADDED * 3])
        ones = (lanes >= V_SPARE) & (lanes < V_SPARE + 3)
        for head in range(OWN):
            at = slice(LANES * (head % 2), LANES * (head % 2 + 1))
            part = value[:, LANES * head : LANES * (head + 1)]
            (v0_ref, v1_ref)[head // 2][rows, at] = jnp.where(ones, 1.0, part).astype(BF16)


def project(x_tiles, mod, w, cos, sin, gq, gk, spread):
    width = w.shape[0]
    tokens = cos.shape[0]
    return pl.pallas_call(
        project_kernel,
        out_shape=[
            jax.ShapeDtypeStruct((tokens, width), BF16),
            jax.ShapeDtypeStruct((tokens, PADDED), F32),
            jax.ShapeDtypeStruct((tokens, PADDED), F32),
        ]
        + [jax.ShapeDtypeStruct((tokens, PAIR), BF16)] * 6,
        in_specs=[vmem()] * 11,
        out_specs=[vmem()] * 9,
        scratch_shapes=[pltpu.VMEM((width, 3 * PADDED), BF16)],
        cost_estimate=cost(16),
        compiler_params=limit(34),
        name="project",
    )(*x_tiles, mod, w, cos, sin, gq, gk, spread)


def attend_kernel(qin_ref, k_ref, v_ref, spread_ref, q_ref, mixedp_ref, mixed_ref):
    tokens = qin_ref.shape[0]
    block = 256

    @pl.loop(0, tokens // block)
    def _(i):
        rows = pl.ds(pl.multiple_of(i * block, block), block)
        for head in range(2):
            at = slice(LANES * head, LANES * (head + 1))
            query = qin_ref[rows, at]
            terms = jnp.exp2(dot_nt(query, k_ref[:, at])).astype(BF16)
            result = dot(terms, v_ref[:, at])
            total = result[:, V_SPARE : V_SPARE + 1]
            mixedp_ref[rows, at] = (result * (1.0 / total)).astype(BF16)
            q_ref[rows, at] = put_lanes(query, QK_SPARE, three_parts(-jnp.log2(total)))
        mixed_ref[:, rows] = dot_nt(spread_ref[3, :PAIR_COLS, :PAIR], mixedp_ref[rows, :]).astype(BF16)


def attend(q, k, v, spread):
    tokens = q.shape[0]
    return pl.pallas_call(
        attend_kernel,
        out_shape=[
            jax.ShapeDtypeStruct((tokens, PAIR), BF16),
            jax.ShapeDtypeStruct((tokens, PAIR), BF16),
            jax.ShapeDtypeStruct((PAIR_COLS, tokens), BF16),
        ],
        in_specs=[vmem()] * 4,
        out_specs=[vmem()] * 3,
        cost_estimate=cost(4.1),
        compiler_params=limit(20),
        name="attend",
    )(q, k, v, spread)


def attention_back_kernel(
    g0_ref, g1_ref, g2_ref, g3_ref, wout_ref, qraw_ref, kraw_ref, q0_ref, q1_ref, k0_ref, k1_ref, v0_ref, v1_ref,
    m0_ref, m1_ref, cos_ref, sin_ref, gq_ref, gk_ref, spread_ref, out_ref, gains_ref, do_ref, dq_ref, dk_ref, pad_ref,
):
    block = g0_ref.shape[0]
    tokens = 4 * block
    root = 1.0 / math.sqrt(HEAD)

    for place, g_ref in enumerate((g0_ref, g1_ref, g2_ref, g3_ref)):
        rows = slice(block * place, block * (place + 1))
        grad_mixed = dot(g_ref[...], wout_ref[...]).astype(BF16)
        wide = dot(grad_mixed, spread_ref[3, :COLS, :])
        for head in range(OWN):
            at = slice(LANES * head, LANES * (head + 1))
            part = wide[:, at]
            pair_at = slice(LANES * (head % 2), LANES * (head % 2 + 1))
            mixed = (m0_ref, m1_ref)[head // 2][rows, pair_at].astype(F32)
            row_dot = jnp.sum(part * mixed, axis=-1, keepdims=True)
            do_ref[rows, at] = put_lanes(part.astype(BF16), V_SPARE, three_parts(-row_dot))

    for head in range(OWN):
        at = slice(LANES * head, LANES * (head + 1))
        pair_at = slice(LANES * (head % 2), LANES * (head % 2 + 1))
        q_ref, k_ref, v_ref = ((q0_ref, k0_ref, v0_ref), (q1_ref, k1_ref, v1_ref))[head // 2]
        dq_ref[at, :] = jnp.zeros((LANES, tokens), F32)

        @pl.loop(0, tokens // block)
        def _(i, at=at, pair_at=pair_at, q_ref=q_ref, k_ref=k_ref, v_ref=v_ref, head=head):
            rows = pl.ds(pl.multiple_of(i * block, block), block)
            query, grad = q_ref[:, pair_at], do_ref[:, at]
            key = k_ref[rows, pair_at]
            probs = jnp.exp2(dot_nt(key, query))
            slope = (probs * dot_nt(v_ref[rows, pair_at], grad)).astype(BF16)
            pad_ref[rows, 2 * PADDED + LANES * head : 2 * PADDED + LANES * (head + 1)] = dot(
                probs.astype(BF16), grad
            ).astype(BF16)
            dk_ref[rows, at] = dot(slope, query) * LN2
            dq_ref[at, :] += dot(key.astype(F32).T.astype(BF16), slope)

    gains_ref[...] = jnp.zeros_like(gains_ref)

    @pl.loop(0, tokens // block)
    def _(i):
        rows = pl.ds(pl.multiple_of(i * block, block), block)
        cos, sin = cos_ref[rows, :], sin_ref[rows, :]
        for which, raw_ref, gain_ref in ((0, qraw_ref, gq_ref), (1, kraw_ref, gk_ref)):
            gained = jnp.zeros((1, LANES), F32)
            for head in range(OWN):
                at = slice(LANES * head, LANES * (head + 1))
                raw = raw_ref[rows, at]
                inv = lax.rsqrt(jnp.sum(raw * raw, axis=-1, keepdims=True) / HEAD + EPSILON)
                hat = raw * inv
                if which == 0:
                    grad = dq_ref[at, rows].T * root
                else:
                    grad = dk_ref[rows, at]
                turned = grad * cos - pltpu.roll(grad, 64, 1) * sin
                product = turned * hat
                gained += jnp.sum(product, axis=0, keepdims=True)
                mean = jnp.sum(product * gain_ref[...], axis=-1, keepdims=True) / HEAD
                pad_ref[rows, PADDED * which + LANES * head : PADDED * which + LANES * (head + 1)] = (
                    inv * (turned * gain_ref[...] - hat * mean)
                ).astype(BF16)
            gains_ref[which : which + 1, :] += gained
        compact = [
            dot_nt(pad_ref[rows, PADDED * w : PADDED * (w + 1)], spread_ref[w]).astype(BF16)
            for w in range(3)
        ]
        out_ref[rows, :] = jnp.concatenate(
            [
                compact[0][:, :256],
                compact[0][:, 256:] + compact[1][:, :128],
                compact[1][:, 128:256],
                compact[1][:, 256:] + compact[2][:, :128],
                compact[2][:, 128:],
            ],
            axis=1,
        )[:, : 3 * COLS]


def attention_backward(grads, w_rows, qraw, kraw, q, k, v, mixedp, cos, sin, gq, gk, spread):
    tokens = cos.shape[0]
    return pl.pallas_call(
        attention_back_kernel,
        out_shape=[
            jax.ShapeDtypeStruct((tokens, 3 * COLS), BF16),
            jax.ShapeDtypeStruct((8, LANES), F32),
        ],
        in_specs=[vmem()] * 20,
        out_specs=[vmem()] * 2,
        scratch_shapes=[
            pltpu.VMEM((tokens, PADDED), BF16),
            pltpu.VMEM((PADDED, tokens), F32),
            pltpu.VMEM((tokens, PADDED), F32),
            pltpu.VMEM((tokens, 3 * PADDED), BF16),
        ],
        cost_estimate=cost(32),
        compiler_params=limit(58),
        name="attention_backward",
    )(*grads, w_rows, qraw, kraw, *q, *k, *v, *mixedp, cos, sin, gq, gk, spread)


def smem():
    return pl.BlockSpec(memory_space=pltpu.SMEM)


def out_weight_kernel(tile_ref, p0_ref, p1_ref, p2_ref, p3_ref, out_ref, own_ref):
    for place, piece in enumerate((p0_ref, p1_ref, p2_ref, p3_ref)):
        start = pl.multiple_of((tile_ref[0] ^ FLIPS[place]) * COLS, 16)
        out_ref[pl.ds(start, COLS), :] = piece[...]
    for tile in range(4):

        @pl.when(tile_ref[0] == tile)
        def _(tile=tile):
            own_ref[...] = out_ref[:, COLS * tile : COLS * (tile + 1)]


def out_weight(tile, pieces):
    width = pieces[0].shape[1]
    return pl.pallas_call(
        out_weight_kernel,
        out_shape=[
            jax.ShapeDtypeStruct((width, width), BF16),
            jax.ShapeDtypeStruct((width, COLS), BF16),
        ],
        in_specs=[smem()] + [vmem()] * 4,
        out_specs=[vmem()] * 2,
        cost_estimate=cost(3.8),
        compiler_params=limit(12),
        name="out_weight",
    )(tile, *pieces)


def mlp_kernel(places, tile_ref, mod_ref, wout_ref, wgu_ref, wdown_ref, *refs):
    number = len(places)
    x_refs, dy_refs, mixed_refs = refs[:number], refs[number : 2 * number], refs[2 * number : 2 * number + 4 * PAIRS]
    refs = refs[-(4 + 2 * number + (2 in places) + 1) :]
    mlp_ref, hidden_ref, ggu_ref, gbranch_ref = refs[:4]
    branch_refs, gmlp_refs, mixed_ref = refs[4 : 4 + number], refs[4 + number : 4 + 2 * number], refs[-1]
    block = x_refs[0].shape[0]
    half = wgu_ref.shape[1] // 2
    for k, m_ref in enumerate(mixed_refs):
        pair, source = k // 4, k % 4
        start = pl.multiple_of((tile_ref[0] ^ FLIPS[source]) * COLS + PAIR_COLS * pair, 16)
        for n, place in enumerate(places):
            at = block * (place ^ FLIPS[source])
            mixed_ref[pl.ds(start, PAIR_COLS), block * n : block * (n + 1)] = m_ref[:, at : at + block]
    for n, (place, x_ref, dy_ref, branch_ref, gmlp_ref) in enumerate(
        zip(places, x_refs, dy_refs, branch_refs, gmlp_refs)
    ):
        here = slice(block * n, block * (n + 1))
        attended = lax.dot_general(
            mixed_ref[:, here], wout_ref[...], (((0,), (1,)), ((), ())), preferred_element_type=F32
        )
        if place == 2:
            refs[-2][...] = attended
        x_mid = x_ref[...].astype(F32) + mod_ref[2:3, :] * attended
        normed = x_mid * inverse_rms(x_mid)
        mlp_in = (normed * (1.0 + mod_ref[4:5, :]) + mod_ref[3:4, :]).astype(BF16)
        mlp_ref[here, :] = mlp_in
        grad_branch = (mod_ref[5:6, :] * (mod_ref[6:7, :] * dy_ref[...].astype(F32))).astype(BF16)
        gbranch_ref[here, :] = grad_branch
        gate = dot(mlp_in, wgu_ref[:, :half])
        up = dot(mlp_in, wgu_ref[:, half:])
        grad_hidden = dot_nt(grad_branch, wdown_ref[...])
        sigmoid = jax.nn.sigmoid(gate)
        silu = gate * sigmoid
        hidden = (silu * up).astype(BF16)
        hidden_ref[here, :] = hidden
        branch_ref[...] = dot(hidden, wdown_ref[...]).astype(BF16)
        grad_gate = (grad_hidden * up * (sigmoid * (1.0 + gate * (1.0 - sigmoid)))).astype(BF16)
        grad_up = (grad_hidden * silu).astype(BF16)
        ggu_ref[here, :half] = grad_gate
        ggu_ref[here, half:] = grad_up
        gmlp_ref[...] = (
            dot_nt(grad_gate, wgu_ref[:, :half]) + dot_nt(grad_up, wgu_ref[:, half:])
        ).astype(BF16)


def mlp(places, tile, mod, w_out, w_gu, w_down, x_tiles, dy_tiles, mixed, kept):
    number = len(places)
    block, width = x_tiles[0].shape
    hidden = w_down.shape[0]
    one = pl.Buffered(1)
    row_block = lambda cols: pl.BlockSpec(
        (number * block, cols), lambda i: (places[0] // number, 0), pipeline_mode=one
    )
    whole = lambda rows, cols: pl.BlockSpec((rows, cols), lambda i: (0, 0), pipeline_mode=one)
    args = [mod, w_out, w_gu, w_down]
    args += [x_tiles[p] for p in places] + [dy_tiles[p] for p in places] + list(mixed)
    in_specs = [smem()] + [whole(*arg.shape) for arg in args]
    args = [tile] + args
    aliases = {}
    for k, array in enumerate(kept):
        aliases[len(args)] = k
        args.append(array)
        in_specs.append(pl.BlockSpec(memory_space=pl.ANY))
    shapes = [(4 * block, width), (4 * block, hidden), (4 * block, 2 * hidden), (4 * block, width)]
    attended = [jax.ShapeDtypeStruct((block, width), F32)] if 2 in places else []
    return pl.pallas_call(
        functools.partial(mlp_kernel, places),
        grid=(1,),
        out_shape=[jax.ShapeDtypeStruct(shape, BF16) for shape in shapes]
        + [jax.ShapeDtypeStruct((block, width), BF16)] * (2 * number)
        + attended,
        in_specs=in_specs,
        out_specs=[row_block(shape[1]) for shape in shapes]
        + [whole(block, width)] * (2 * number + len(attended)),
        scratch_shapes=[pltpu.VMEM((width, number * block), BF16)],
        input_output_aliases=aliases,
        compiler_params=limit(44),
        cost_estimate=cost(7 * number),
        name="mlp",
    )(*args)


def middle_kernel(a_ref, b_ref, c0_ref, c1_ref, attended_ref, x_ref, dy_ref, mod_ref, gatt_ref, gmid_ref, sums_ref):
    far = jnp.concatenate([c0_ref[...], c1_ref[...]]).astype(F32)
    grad_in = a_ref[...].astype(F32) + b_ref[...].astype(F32) + far
    attended = attended_ref[...]
    x_mid = x_ref[...].astype(F32) + mod_ref[2:3, :] * attended
    inv = inverse_rms(x_mid)
    normed = x_mid * inv
    product = grad_in * normed
    grad_mid = mod_ref[6:7, :] * dy_ref[...].astype(F32) + inv * (
        grad_in * (1.0 + mod_ref[4:5, :])
        - normed * jnp.mean(product * (1.0 + mod_ref[4:5, :]), axis=-1, keepdims=True)
    )
    gmid_ref[...] = grad_mid
    gatt_ref[...] = (mod_ref[2:3, :] * grad_mid).astype(BF16)
    sums_ref[...] = jnp.zeros_like(sums_ref)
    sums_ref[0:1, :] = jnp.sum(grad_mid * attended, axis=0, keepdims=True)
    sums_ref[1:2, :] = jnp.sum(grad_in, axis=0, keepdims=True)
    sums_ref[2:3, :] = jnp.sum(product, axis=0, keepdims=True)


def middle(parts, attended, x, dy, mod):
    block, width = x.shape
    return pl.pallas_call(
        middle_kernel,
        out_shape=[
            jax.ShapeDtypeStruct((block, width), BF16),
            jax.ShapeDtypeStruct((block, width), F32),
            jax.ShapeDtypeStruct((8, width), F32),
        ],
        in_specs=[vmem()] * 8,
        out_specs=[vmem()] * 3,
        cost_estimate=cost(4.6),
        compiler_params=limit(14),
        name="middle",
    )(*parts, attended, x, dy, mod)


def output_kernel(a_ref, b_ref, c_ref, attended_ref, x_ref, dy_ref, mod_ref, out_ref, sums_ref):
    branch = a_ref[...].astype(F32) + b_ref[...].astype(F32) + c_ref[...].astype(F32)
    x_mid = x_ref[...].astype(F32) + mod_ref[2:3, :] * attended_ref[...]
    live = mod_ref[6:7, :]
    out_ref[...] = (live * (x_mid + mod_ref[5:6, :] * branch)).astype(BF16)
    sums_ref[...] = jnp.zeros_like(sums_ref)
    sums_ref[0:1, :] = jnp.sum(live * dy_ref[...].astype(F32) * branch, axis=0, keepdims=True)


def output_tile(parts, attended, x, dy, mod):
    block, width = x.shape
    return pl.pallas_call(
        output_kernel,
        out_shape=[
            jax.ShapeDtypeStruct((block, width), BF16),
            jax.ShapeDtypeStruct((8, width), F32),
        ],
        in_specs=[vmem()] * 7,
        out_specs=[vmem()] * 2,
        cost_estimate=cost(3.5),
        compiler_params=limit(12),
        name="output_tile",
    )(*parts, attended, x, dy, mod)


def tokens_kernel(a_ref, b_ref, c_ref, x_ref, gmid_ref, mod_ref, out_ref, sums_ref):
    grad_in = a_ref[...].astype(F32) + b_ref[...].astype(F32) + c_ref[...].astype(F32)
    x = x_ref[...].astype(F32)
    inv = inverse_rms(x)
    normed = x * inv
    product = grad_in * normed
    scale = 1.0 + mod_ref[1:2, :]
    out_ref[...] = (
        gmid_ref[...] + inv * (grad_in * scale - normed * jnp.mean(product * scale, axis=-1, keepdims=True))
    ).astype(BF16)
    sums_ref[...] = jnp.zeros_like(sums_ref)
    sums_ref[0:1, :] = jnp.sum(grad_in, axis=0, keepdims=True)
    sums_ref[1:2, :] = jnp.sum(product, axis=0, keepdims=True)


def tokens_back(parts, x, grad_mid, mod):
    block, width = x.shape
    return pl.pallas_call(
        tokens_kernel,
        out_shape=[
            jax.ShapeDtypeStruct((block, width), BF16),
            jax.ShapeDtypeStruct((8, width), F32),
        ],
        in_specs=[vmem()] * 6,
        out_specs=[vmem()] * 2,
        cost_estimate=cost(3.6),
        compiler_params=limit(14),
        name="tokens_back",
    )(*parts, x, grad_mid, mod)


def first_grad_kernel(tile_ref, g0_ref, g1_ref, g2_ref, g3_ref, *refs):
    mixed_refs, (attn_ref, qkv_ref, out_ref, cols_ref) = refs[: 4 * PAIRS], refs[4 * PAIRS :]
    block = g0_ref.shape[0]
    wide = qkv_ref.shape[1]
    for tile in range(4):

        @pl.when(tile_ref[0] == tile)
        def _(tile=tile):
            for place, g_ref in enumerate((g0_ref, g1_ref, g2_ref, g3_ref)):
                cols_ref[block * place : block * (place + 1), :] = g_ref[:, COLS * tile : COLS * (tile + 1)]

    for k in range(attn_ref.shape[1] // LANES):
        at = slice(LANES * k, LANES * (k + 1))
        out_ref[at, :wide] = dot_tn(attn_ref[:, at], qkv_ref[...]).astype(BF16)
    for k, m_ref in enumerate(mixed_refs):
        pair, source = k // 4, k % 4
        total = None
        for place in range(4):
            at = block * (place ^ FLIPS[source])
            term = dot(m_ref[:, at : at + block], cols_ref[block * place : block * (place + 1), :])
            total = term if total is None else total + term
        start = pl.multiple_of((tile_ref[0] ^ FLIPS[source]) * COLS + PAIR_COLS * pair, 16)
        out_ref[pl.ds(start, PAIR_COLS), wide:] = total.astype(BF16)


def first_grad(tile, grads, mixed, attn_in, grad_qkv):
    width = attn_in.shape[1]
    return pl.pallas_call(
        first_grad_kernel,
        out_shape=jax.ShapeDtypeStruct((width, grad_qkv.shape[1] + COLS), BF16),
        in_specs=[smem()] + [vmem()] * (6 + 4 * PAIRS),
        out_specs=vmem(),
        scratch_shapes=[pltpu.VMEM((grad_qkv.shape[0], COLS), BF16)],
        compiler_params=limit(24),
        cost_estimate=cost(8),
        name="first_grad",
    )(tile, *grads, *mixed, attn_in, grad_qkv)


def weight_grad_kernel(left_ref, right_ref, out_ref):
    for k in range(left_ref.shape[1] // LANES):
        at = slice(LANES * k, LANES * (k + 1))
        out_ref[at, :] = dot_tn(left_ref[:, at], right_ref[...]).astype(BF16)


def weight_grad(left, right, microseconds):
    return pl.pallas_call(
        weight_grad_kernel,
        out_shape=jax.ShapeDtypeStruct((left.shape[1], right.shape[1]), BF16),
        in_specs=[vmem()] * 2,
        out_specs=vmem(),
        compiler_params=limit(24),
        cost_estimate=cost(microseconds),
        name="weight_grad",
    )(left, right)


GU_AFTER = 4
TO_TX = (1, 0, 2, 1)
TO_TY = (2, 2, 0, 0)
KEPT = (0, 1, 1, 2)
SLOTS = ((0, 1, 2), (2, 1, 0), (0, 1, 2), (2, 1, 0))


def pack_kernel(shard, ff_own, tile_ref, a_ref, b_ref, sgu_ref, tx_ref, ty_ref, gu_ref, down_ref, unit_ref, out_ref):
    cut = a_ref.shape[0]
    share = sgu_ref.shape[1] // 4

    def rows(first, last, lanes):
        pieces = []
        if first < cut:
            pieces.append(a_ref[first : min(last, cut), lanes])
        if last > cut:
            pieces.append(b_ref[max(first, cut) - cut : last - cut, lanes])
        return pieces[0] if len(pieces) == 1 else jnp.concatenate(pieces)

    def gu(tile):
        return sgu_ref[:, share * tile : share * (tile + 1)]

    def down(tile):
        return rows(shard, shard + ff_own, slice(COLS * tile, COLS * (tile + 1)))

    def unit(part):
        return rows(0, shard, slice(COLS * part, COLS * (part + 1)))

    out_ref[...] = unit(3)
    for tile in range(4):

        @pl.when(tile_ref[0] == tile)
        def _(tile=tile):
            at = 0
            for ref, pieces in (
                (tx_ref, (gu(tile ^ 1), gu(tile ^ 3), down(tile ^ 1), down(tile ^ 3), unit(TO_TX[tile]))),
                (ty_ref, (gu(tile ^ 2), down(tile ^ 2), unit(TO_TY[tile]))),
            ):
                at = 0
                for piece in pieces:
                    ref[at : at + piece.shape[0], : piece.shape[1]] = piece.astype(BF16)
                    at += piece.shape[0]
            gu_ref[...] = gu(tile).astype(F32)
            down_ref[...] = down(tile)
            unit_ref[...] = unit(KEPT[tile])


def pack(tile, sums, sum_gu, shard, ff_own):
    share = sum_gu.shape[1] // 4
    both = 3 * shard + 2 * ff_own
    one = 2 * shard + ff_own
    return pl.pallas_call(
        functools.partial(pack_kernel, shard, ff_own),
        out_shape=[
            jax.ShapeDtypeStruct((both, share), BF16),
            jax.ShapeDtypeStruct((one, share), BF16),
            jax.ShapeDtypeStruct((shard, share), F32),
            jax.ShapeDtypeStruct((ff_own, COLS), F32),
            jax.ShapeDtypeStruct((shard, COLS), F32),
            jax.ShapeDtypeStruct((shard, COLS), F32),
        ],
        in_specs=[smem()] + [vmem()] * 3,
        out_specs=[vmem()] * 6,
        compiler_params=limit(12),
        cost_estimate=cost(2),
        name="pack",
    )(tile, *sums, sum_gu)


def unpack_kernel(shard, ff_own, tile_ref, tx_ref, ty_ref, gu_ref, down_ref, unit_ref, wgu_ref, wdown_ref, wqkv_ref):
    one = 2 * shard + ff_own
    share = gu_ref.shape[1]
    groups = share // ff_own
    gus = [
        gu_ref[...],
        tx_ref[0:shard, :].astype(F32),
        ty_ref[0:shard, :].astype(F32),
        ty_ref[one : one + shard, :].astype(F32),
    ]
    downs = [
        down_ref[...],
        tx_ref[2 * shard : 2 * shard + ff_own, :COLS].astype(F32),
        ty_ref[shard : shard + ff_own, :COLS].astype(F32),
        ty_ref[one + shard : one + shard + ff_own, :COLS].astype(F32),
    ]
    units = [
        unit_ref[...],
        tx_ref[2 * shard + 2 * ff_own :, :COLS].astype(F32),
        ty_ref[shard + ff_own : one, :COLS].astype(F32),
    ]
    for tile in range(4):

        @pl.when(tile_ref[0] == tile)
        def _(tile=tile):
            for source in range(4):
                flip = source ^ tile
                wdown_ref[ff_own * source : ff_own * (source + 1), :] = downs[flip]
                for group in range(groups):
                    at = share * group + ff_own * source
                    wgu_ref[:, at : at + ff_own] = gus[flip][:, ff_own * group : ff_own * (group + 1)]
            for k in range(3):
                wqkv_ref[:, COLS * k : COLS * (k + 1)] = units[SLOTS[tile][k]]


def unpack(tile, from_tx, from_ty, kept, shard, ff_own):
    share = kept[0].shape[1]
    return pl.pallas_call(
        functools.partial(unpack_kernel, shard, ff_own),
        out_shape=[
            jax.ShapeDtypeStruct((shard, 4 * share), F32),
            jax.ShapeDtypeStruct((4 * ff_own, COLS), F32),
            jax.ShapeDtypeStruct((shard, 3 * COLS), F32),
        ],
        in_specs=[smem()] + [vmem()] * 5,
        out_specs=[vmem()] * 3,
        compiler_params=limit(12),
        cost_estimate=cost(2),
        name="unpack",
    )(tile, from_tx, from_ty, *kept)


def ada_kernel(tile_ref, mod_ref, w_ref, silu_ref, ada_ref, bias_ref, cond_ref):
    count, wide = mod_ref.shape
    width = w_ref.shape[1]
    share = width // 4
    for tile in range(4):

        @pl.when(tile_ref[0] == tile)
        def _(tile=tile):
            ada_ref[...] = dot_tn(silu_ref[...], mod_ref[:, share * tile : share * (tile + 1)])

    rows = [mod_ref[k : k + 1, :].astype(F32) for k in range(count)]
    while len(rows) > 1:
        rows = [rows[k] + rows[k + 1] for k in range(0, len(rows), 2)]
    bias_ref[...] = rows[0]
    cond_ref[...] = dot_nt(mod_ref[:, :width], w_ref[...])


def ada_back(tile, mod_all, w_ada, silu_rows):
    count, wide = mod_all.shape
    shard, width = w_ada.shape
    return pl.pallas_call(
        ada_kernel,
        out_shape=[
            jax.ShapeDtypeStruct((shard, width // 4), F32),
            jax.ShapeDtypeStruct((1, wide), F32),
            jax.ShapeDtypeStruct((count, shard), F32),
        ],
        in_specs=[smem()] + [vmem()] * 3,
        out_specs=[vmem()] * 3,
        cost_estimate=cost(3.5),
        compiler_params=limit(12),
        name="ada_back",
    )(tile, mod_all, w_ada, silu_rows)


def reorder_kernel(index_ref, rows_ref, out_ref):
    for k in range(rows_ref.shape[0]):
        out_ref[k : k + 1, :] = rows_ref[pl.ds(index_ref[k], 1), :]


def reorder(index, rows):
    return pl.pallas_call(
        reorder_kernel,
        out_shape=jax.ShapeDtypeStruct(rows.shape, rows.dtype),
        in_specs=[smem(), vmem()],
        out_specs=vmem(),
        cost_estimate=cost(1.3),
        compiler_params=limit(4),
        name="reorder",
    )(index, rows)


def lane_matrix():
    matrix = np.zeros((HEAD, LANES), np.float32)
    for index in range(HEAD):
        matrix[index, head_lane(index)] = 1.0
    return matrix


def rope_lanes(tile_rows, tile_cols):
    freqs = (10000.0 ** (-np.arange(QUARTER, dtype=np.float64) / QUARTER)).astype(np.float32)
    freq = np.zeros((LANES,), np.float32)
    part = np.zeros((LANES,), np.int32)
    sign = np.zeros((LANES,), np.float32)
    for index in range(HEAD):
        lane = head_lane(index)
        freq[lane] = freqs[index % QUARTER]
        part[lane] = index // 36
        sign[lane] = 1.0 if lane >= 64 else -1.0
    per_tile = tile_rows * tile_cols
    ids = np.arange(4 * per_tile)
    flips = np.array(FLIPS)[ids // per_tile]
    ty = lax.axis_index("ty") ^ jnp.asarray(flips >> 1, jnp.int32)
    tx = lax.axis_index("tx") ^ jnp.asarray(flips & 1, jnp.int32)
    rows = (ty * tile_rows + jnp.asarray(ids % per_tile // tile_cols, jnp.int32)).astype(F32)
    cols = (tx * tile_cols + jnp.asarray(ids % tile_cols, jnp.int32)).astype(F32)
    angle = jnp.where(jnp.asarray(part)[None] == 0, rows[:, None], cols[:, None]) * jnp.asarray(freq)[None]
    live = jnp.asarray((sign != 0).astype(np.float32))[None]
    return jnp.cos(angle) * live, jnp.sin(angle) * jnp.asarray(sign)[None]


def gain_lanes(gain):
    return jnp.sum(jnp.asarray(lane_matrix()) * gain[:, None], axis=0, keepdims=True)


def gain_back(lanes):
    return jnp.sum(jnp.asarray(lane_matrix()) * lanes[None, :], axis=1)


def tile_pair(far):
    return (far[0].astype(F32) + swap(far[1], "tx").astype(F32)).astype(BF16)


def tile_sum_parts(pair, near):
    return near[0], swap(near[1], "tx"), swap(pair, "ty")


def body(
    count, tokens, cond, live_count, w_qkv, w_out, w_gu, w_down, w_ada, ada_bias, q_gain, k_gain, cotangent
):
    _, tile_rows, tile_cols, width = tokens.shape
    per_tile = tile_rows * tile_cols
    img, ty, tx = lax.axis_index("img"), lax.axis_index("ty"), lax.axis_index("tx")
    tile = ty * 2 + tx
    tile_word = tile[None].astype(jnp.int32)
    live = (live_count[0] > 0).astype(F32)
    shard = width // count
    ff_shard = FF // count
    ff_own = ff_shard // TILES
    hidden_own = FF // TILES
    out_width = width // TILES
    spread = jnp.asarray(spread_matrices(), BF16)

    first = jnp.concatenate(
        [lax.dynamic_slice_in_dim(w_qkv, p * width + tile * COLS, COLS, 1) for p in range(3)]
        + [lax.dynamic_slice_in_dim(w_out, tile * out_width, out_width, 1)],
        axis=1,
    )
    down_own = lax.dynamic_slice_in_dim(w_down, tile * ff_own, ff_own, 0)
    gu_own = lax.dynamic_slice_in_dim(w_gu.reshape(shard, 2 * count, ff_shard), tile * ff_own, ff_own, 2)
    gu_own = gu_own.reshape(shard, 2 * hidden_own)

    x_own = tokens.reshape(per_tile, width)
    dy_own = cotangent.reshape(per_tile, width)
    x_tiles = gather_tiles(x_own)
    dy_tiles = gather_tiles(dy_own)

    cond_float = cond.astype(F32)
    bits = [1 << k for k in range(count.bit_length() - 1)]
    store = {}

    def gather_step(v, bit):
        return jnp.concatenate([v, lax.ppermute(v, "img", flip_perm(count, bit))])

    def scatter_step(v, bit):
        return v[:bit] + lax.ppermute(v[bit:], "img", flip_perm(count, bit))

    silu_some = jax.nn.silu(cond_float).astype(BF16)
    for bit in bits[:-1]:
        silu_some = gather_step(silu_some, bit)

    def rows_step(_):
        store["silu_rows"] = lax.dynamic_slice_in_dim(gather_step(silu_some, bits[-1]), img * shard, shard, 1)
        return store["silu_rows"]

    beside = [rows_step, lambda v: scatter_step(dot(v, w_ada), bits[-1])]
    beside += [lambda v, bit=bit: scatter_step(v, bit) for bit in bits[-2::-1]]
    early, late = beside[1], beside[2]
    beside[1] = lambda v: after(early(v), x_tiles[0])
    beside[2] = lambda v: after(late(v), dy_tiles[0], x_tiles)

    ring = use_ring(count, math.gcd(shard, ff_own))
    if ring:
        own = after(jnp.concatenate([first, down_own]), silu_some)
        pieces, modulation = ring_gather(own, count, beside)
        full_first, full_down, out_own = assemble(
            own,
            pieces,
            [(width, width), (hidden_own, width), (COLS, width)],
            [(0, shard, 0, shard, 0, 0, 0, width), (1, ff_own, shard, ff_own, 0, 0, 0, width)],
            count,
            True,
        )
        full_gu = lax.all_gather(after(gu_own, pieces[GU_AFTER]), "img", axis=0, tiled=True)
    else:
        full_first, full_down, full_gu = [
            lax.all_gather(a, "img", axis=0, tiled=True) for a in (first, down_own, gu_own)
        ]
        out_own = out_share(out_pick(), full_first)
        modulation = None
        for step in beside:
            modulation = step(modulation)
    silu_rows = store["silu_rows"]
    modulation = modulation + ada_bias
    mod = jnp.concatenate([modulation.reshape(6, width), jnp.broadcast_to(live, (2, width))])

    cos, sin = rope_lanes(tile_rows, tile_cols)
    gq, gk = gain_lanes(q_gain), gain_lanes(k_gain)
    attn_in, qraw, kraw, q0, q1, k0, k1, v0, v1 = project(
        x_tiles, mod, full_first, cos, sin, gq, gk, spread
    )
    out_far = swap(out_own, "ty")
    out_far = after(out_far, attn_in)
    full_out, out_rows = out_weight(
        tile_word, [out_far, swap(out_far, "tx"), out_own, swap(out_own, "tx")]
    )
    q0, mixedp0, mixed0 = attend(q0, k0, v0, spread)
    mixed = gather_tiles(mixed0)
    q1, mixedp1, mixed1 = attend(after(q1, full_out, mixed0), k1, v1, spread)
    mixed += gather_tiles(mixed1)

    weights = (tile_word, mod, full_out, full_gu, full_down, x_tiles, dy_tiles, mixed)
    far = mlp((0, 1), *weights, ())
    grad_pair = tile_pair(far[6:8])
    cut = per_tile // 2
    part_0, part_1 = swap(grad_pair[:cut], "ty"), swap(grad_pair[cut:], "ty")
    beside_tile = mlp((3,), *weights, after(far[:4], grad_pair))
    own_tile = mlp((2,), *weights, after(beside_tile[:4], part_0))
    mlp_in, hidden, grad_gu, grad_branch = own_tile[:4]
    attended = own_tile[6]

    grad_att, grad_mid, mid_sums = middle(
        (own_tile[5], swap(beside_tile[5], "tx"), part_0, part_1), attended, x_own, dy_own, mod
    )
    g_gu = weight_grad(mlp_in, after(grad_gu, grad_att), 5)
    g_down = weight_grad(hidden, after(grad_branch, g_gu), 3)
    att_far = after(swap(grad_att, "ty"), g_gu, g_down)
    grad_att_tiles = [att_far, swap(att_far, "tx"), grad_att, swap(grad_att, "tx")]

    grad_qkv, gains = attention_backward(
        grad_att_tiles, out_rows, qraw, kraw, (q0, q1), (k0, k1), (v0, v1), (mixedp0, mixedp1),
        cos, sin, gq, gk, spread,
    )
    branch_parts = tile_sum_parts(tile_pair(far[4:6]), (own_tile[4], beside_tile[4]))
    output, out_sums = output_tile(after(branch_parts, grad_qkv), attended, x_own, dy_own, mod)
    w_back = full_first[:, : 3 * COLS]
    back_far = dot_nt(grad_qkv[: 2 * per_tile], w_back).astype(BF16)
    halves = lambda rows: (rows[:per_tile], rows[per_tile:])
    back_pair = tile_pair(halves(back_far))
    late_qkv = after(grad_qkv, back_pair)
    back_near = dot_nt(late_qkv[2 * per_tile :], w_back).astype(BF16)
    g_first = first_grad(tile_word, grad_att_tiles, mixed, attn_in, late_qkv)

    wide = 6 * width

    def token_step():
        parts = tile_sum_parts(back_pair, halves(back_near))
        store["grad_tokens"], tok_sums = tokens_back(parts, x_own, grad_mid, mod)
        return jnp.concatenate(
            [tok_sums[0], tok_sums[1], mid_sums[0], mid_sums[1], mid_sums[2], out_sums[0], gains[0], gains[1]]
        )[None]

    def low_step(grad_mod):
        return jnp.concatenate([grad_mod[:, :wide].astype(BF16), *three_parts(grad_mod[:, wide:])], axis=1)

    def ada_step(mod_all):
        store["grad_ada"], store["sums"], grad_silu = ada_back(tile_word, mod_all, w_ada, silu_rows)
        return grad_silu

    steps = [None, lambda _: token_step(), lambda v: low_step(sum_tiles(v))]
    steps += [lambda v, bit=bit: gather_step(v, bit) for bit in bits]
    steps.append(lambda v: flip_exchange(ada_step(v), count, bits[-1:]))
    steps.append(lambda v: flip_exchange(v, count, bits[-2::-1]))

    if ring:
        s_gu = lax.psum_scatter(g_gu, "img", scatter_dimension=0, tiled=True)
        s_all, grad_silu = ring_scatter([g_first, g_down], count, steps)
    else:
        grad_silu = None
        for step in steps:
            grad_silu = step(grad_silu) if step else None
    grad_tokens, grad_ada, sums = store["grad_tokens"], store["grad_ada"], store["sums"]
    grad_bias = sums[0, :wide]
    gain_sums = (sums[:, wide : wide + 256] + sums[:, wide + 256 : wide + 512]) + sums[:, wide + 512 :]
    flips = (jnp.arange(count, dtype=jnp.int32) ^ img).astype(jnp.int32)
    grad_silu = reorder(flips, grad_silu).reshape(1, width)
    sigmoid_c = jax.nn.sigmoid(cond_float)
    grad_cond = (grad_silu * sigmoid_c * (1.0 + cond_float * (1.0 - sigmoid_c))).astype(BF16)
    if ring:
        to_tx, to_ty, *kept, grad_w_out = pack(tile_word, s_all, s_gu, shard, ff_own)
        from_tx = swap(to_tx, "tx")
        to_ty = jnp.concatenate(
            [to_ty, from_tx[shard : 2 * shard], from_tx[2 * shard + ff_own : 2 * shard + 2 * ff_own]]
        )
        grad_w_gu, grad_down, grad_w_qkv = unpack(tile_word, from_tx, swap(to_ty, "ty"), kept, shard, ff_own)
    else:
        sums_of = lambda grad: lax.psum_scatter(grad, "img", scatter_dimension=0, tiled=True)
        s_first, s_down, s_gu = sums_of(g_first).astype(F32), sums_of(g_down), sums_of(g_gu)
        gu_cols = 2 * hidden_own // TILES
        got = exchange_tiles(lambda t: lax.dynamic_slice_in_dim(s_gu, t * gu_cols, gu_cols, 1))
        grad_w_out = s_first[:, 3 * COLS :].astype(F32)
        s_qkv = s_first.astype(BF16)

        grad_down = jnp.concatenate(
            exchange_tiles(lambda t: lax.dynamic_slice_in_dim(s_down, t * out_width, out_width, 1))
        ).astype(F32)
        grad_w_gu = jnp.concatenate(
            [got[s][:, ff_own * g : ff_own * (g + 1)] for g in range(gu_cols // ff_own) for s in range(4)],
            axis=1,
        ).astype(F32)
        units = [s_qkv[:, COLS * p : COLS * (p + 1)] for p in range(3)]

        def choose(options, table):
            result = options[table[0]]
            for t in range(1, 4):
                if table[t] != table[0]:
                    result = jnp.where(tile == t, options[table[t]], result)
            return result

        slots = [
            choose(units, KEPT),
            swap(choose(units, TO_TX), "tx"),
            swap(choose(units, TO_TY), "ty"),
        ]
        grad_w_qkv = jnp.concatenate(
            [choose(slots, [SLOTS[t][k] for t in range(4)]) for k in range(3)], axis=1
        ).astype(F32)

    return (
        output.reshape(tokens.shape),
        grad_tokens.reshape(tokens.shape),
        grad_cond,
        grad_w_qkv,
        grad_w_out,
        grad_w_gu,
        grad_down,
        grad_ada,
        gain_back(gain_sums[0, :LANES]),
        gain_back(gain_sums[0, LANES:]),
        grad_bias,
    )


def solution(mesh):
    tiled = P("img", "ty", "tx", None)
    rows = P("img", None)
    cut = P("img", ("ty", "tx"))
    in_specs = (tiled, rows, P("img"), rows, rows, rows, rows, rows, P(), P(), P(), tiled)
    out_specs = (tiled, tiled, rows, cut, cut, cut, cut, cut, P(), P(), P())
    return jax.shard_map(
        functools.partial(body, mesh.shape["img"]),
        mesh=mesh,
        in_specs=in_specs,
        out_specs=out_specs,
        check_vma=False,
    )
```

```python
import functools
import math

import jax
import jax.numpy as jnp
import numpy as np
from jax import lax
from jax.experimental import pallas as pl
from jax.experimental.pallas import tpu as pltpu
from jax.sharding import PartitionSpec as P

HEADS = 16
HEAD = 72
FF = 3072
TILES = 4
OWN = HEADS // TILES
LANES = 128
COLS = OWN * HEAD
PADDED = OWN * LANES
WINDOW = 384
QUARTER = HEAD // 4
EPSILON = 1e-06
LOG2E = math.log2(math.e)
LN2 = math.log(2.0)
BF16 = jnp.bfloat16
F32 = jnp.float32


def head_lane(index):
    part, half, freq = index // 36, (index % 36) // QUARTER, index % QUARTER
    return half * 64 + part * QUARTER + freq


def spread_matrices():
    spread = np.zeros((4, WINDOW, PADDED), np.float32)
    for which in range(4):
        base = (COLS - 256) * which if which < 3 else 0
        for head in range(OWN):
            for index in range(HEAD):
                lane = index if which >= 2 else head_lane(index)
                spread[which, base + HEAD * head + index, LANES * head + lane] = 1.0
    return spread


def dot(left, right):
    return jnp.dot(left, right, preferred_element_type=F32)


def dot_nt(left, right):
    return lax.dot_general(left, right, (((1,), (1,)), ((), ())), preferred_element_type=F32)


def dot_tn(left, right):
    return lax.dot_general(left, right, (((0,), (0,)), ((), ())), preferred_element_type=F32)


def inverse_rms(values):
    return lax.rsqrt(jnp.mean(values * values, axis=-1, keepdims=True) + EPSILON)


def norm_back(grad_out, normed, inv_scale):
    return inv_scale * (grad_out - normed * jnp.mean(grad_out * normed, axis=-1, keepdims=True))


def swap(values, axis):
    return lax.ppermute(values, axis, [(0, 1), (1, 0)])


FLIPS = (2, 3, 0, 1)


def tile_at(flip):
    return (lax.axis_index("ty") ^ (flip >> 1)) * 2 + (lax.axis_index("tx") ^ (flip & 1))


def gather_tiles(values):
    far = swap(values, "ty")
    return [far, swap(far, "tx"), values, swap(values, "tx")]


def sum_tiles(values):
    values = values + swap(values, "tx")
    return values + swap(values, "ty")


def absolute(pieces):
    ty, tx = lax.axis_index("ty"), lax.axis_index("tx")
    turned = [jnp.where(tx == 1, pieces[f ^ 1], pieces[f]) for f in range(4)]
    return [jnp.where(ty == 1, turned[f ^ 2], turned[f]) for f in range(4)]


def exchange_tiles(piece_for):
    across = [(a * 2 + b, (1 - a) * 2 + 1 - b) for a in range(2) for b in range(2)]
    return absolute(
        [
            piece_for(tile_at(0)),
            swap(piece_for(tile_at(1)), "tx"),
            swap(piece_for(tile_at(2)), "ty"),
            lax.ppermute(piece_for(tile_at(3)), ("ty", "tx"), across),
        ]
    )


def flip_perm(count, bit):
    return [(i, i ^ bit) for i in range(count)]


def flip_exchange(values, count, bits):
    rows = [values[k : k + 1] for k in range(count)]
    for bit in bits:
        sent = jnp.concatenate([rows[k] for k in range(count) if k & bit])
        got = lax.ppermute(sent, "img", flip_perm(count, bit))
        moved = [k for k in range(count) if k & bit]
        for place, k in enumerate(moved):
            rows[k] = got[place : place + 1]
    return jnp.concatenate(rows)


def ring_perm(count, step):
    order = list(range(0, count, 2)) + list(range(count - 1, 0, -2))
    return [(order[i], order[(i + step) % count]) for i in range(count)]


def ring_place(count):
    index = lax.axis_index("img")
    return jnp.where(index % 2 == 0, index // 2, count - 1 - index // 2)


def ring_owner(count, place):
    place = (place + count) % count
    return jnp.where(place < count // 2, 2 * place, 2 * (count - 1 - place) + 1)


def use_ring(count, rows):
    return 2 < count <= 16 and count % 2 == 0 and rows % 16 == 0


def split_rows(rows):
    return (rows // 2 + 15) // 16 * 16


def out_share(pick, first):
    return dot_nt(pick, first[:, first.shape[1] - WINDOW :]).astype(BF16)


def ring_gather(own, count, beside):
    cut = split_rows(own.shape[0])
    a, b = own[:cut], own[cut:]
    pieces, value = [], None
    for hop in range(count - 1):
        a = lax.ppermute(a, "img", ring_perm(count, 1))
        b = lax.ppermute(b, "img", ring_perm(count, -1))
        if hop < len(beside):
            value = beside[hop](value)
            a, b, value = lax.optimization_barrier((a, b, value))
        pieces.append((a, b))
    for step in beside[count - 1 :]:
        value = step(value)
    return pieces, value


def assemble_kernel(count, total, plan, shared, index_ref, pick_ref, *refs):
    cut = split_rows(total)
    own, pieces_a, pieces_b = refs[0], refs[1:count], refs[count : 2 * count - 1]
    outs, sems = refs[2 * count - 1 : -1], refs[-1]
    started = []
    for k, (src, first, size) in enumerate(
        [(own, 0, total)]
        + [(piece, 0, cut) for piece in pieces_a]
        + [(piece, cut, total - cut) for piece in pieces_b]
    ):
        for out, rows, base, count_rows, to_row, from_lane, to_lane, lanes in plan:
            low, high = max(first, base), min(first + size, base + count_rows)
            if low < high:
                start = pl.multiple_of(index_ref[k] * rows + to_row + low - base, 16)
                copy = pltpu.make_async_copy(
                    src.at[pl.ds(low - first, high - low), pl.ds(from_lane, lanes)],
                    outs[out].at[pl.ds(start, high - low), pl.ds(to_lane, lanes)],
                    sems.at[len(started)],
                )
                copy.start()
                started.append(copy)
    for copy in started:
        copy.wait()
    if shared:
        outs[-1][...] = out_share(pick_ref[...], outs[0])


def assemble(own, pieces, shapes, plan, count, shared):
    place = ring_place(count)
    steps = jnp.asarray([0] + [-k for k in range(1, count)] + list(range(1, count)), jnp.int32)
    index = ring_owner(count, place + steps).astype(jnp.int32)
    copies = 2 * count - 1
    shapes = [jax.ShapeDtypeStruct(shape, own.dtype) for shape in shapes]
    return pl.pallas_call(
        functools.partial(assemble_kernel, count, own.shape[0], plan, shared),
        out_shape=shapes,
        in_specs=[smem(), vmem()] + [pl.BlockSpec(memory_space=pltpu.HBM)] * copies,
        out_specs=[vmem() for _ in shapes],
        scratch_shapes=[pltpu.SemaphoreType.DMA((2 * len(plan) * copies,))],
        compiler_params=limit(58),
        cost_estimate=cost(5),
        name="assemble_first" if shared else "assemble_gu",
    )(index, out_pick(), own, *[a for a, _ in pieces], *[b for _, b in pieces])


def out_pick():
    pick = np.zeros((COLS, WINDOW), np.float32)
    pick[np.arange(COLS), WINDOW - COLS + np.arange(COLS)] = 1.0
    return jnp.asarray(pick, BF16)


def after(value, *others):
    return lax.optimization_barrier((value, others))[0]


def ring_scatter(grads, count, beside):
    sizes = [grad.shape[0] // count for grad in grads]
    total = sum(sizes)
    cut = split_rows(total)
    place = ring_place(count)
    value = None

    def part(sign, step):
        owner = ring_owner(count, place - sign * step)
        first, last = (0, cut) if sign > 0 else (cut, total)
        found, base = [], 0
        for grad, rows in zip(grads, sizes):
            low, high = max(first, base), min(last, base + rows)
            if low < high:
                found.append(lax.dynamic_slice_in_dim(grad, owner * rows + low - base, high - low, 0))
            base += rows
        return jnp.concatenate(found)

    sums = [part(1, 1), part(-1, 1)]
    for step in range(2, count + 1):
        kind = BF16 if step < count else F32
        got = [lax.ppermute(sums[k], "img", ring_perm(count, sign)) for k, sign in enumerate((1, -1))]
        if step - 2 < len(beside) and beside[step - 2]:
            value = beside[step - 2](value)
            got, value = lax.optimization_barrier((got, value))
        for k, sign in enumerate((1, -1)):
            sums[k] = (got[k].astype(F32) + part(sign, step).astype(F32)).astype(kind)
    for step in beside[count - 1 :]:
        value = step(value)
    return sums, value


def vmem():
    return pl.BlockSpec(memory_space=pltpu.VMEM)


def limit(megabytes):
    return pltpu.CompilerParams(vmem_limit_bytes=megabytes * 1024 * 1024)


def cost(microseconds):
    return pl.CostEstimate(
        flops=int(microseconds * 1.1e9), bytes_accessed=int(microseconds * 3e6), transcendentals=0
    )


def hbm():
    return pl.BlockSpec(memory_space=pltpu.HBM)


def lane_ids(rows):
    return lax.broadcasted_iota(jnp.int32, (rows, LANES), 1)


def three_parts(column):
    high = column.astype(BF16)
    rest = column - high.astype(F32)
    mid = rest.astype(BF16)
    return high, mid, (rest - mid.astype(F32)).astype(BF16)


def head_sums(values):
    lanes = values.shape[1]
    row = lax.broadcasted_iota(jnp.int32, (PAIR, PAIR), 0) // LANES
    col = lax.broadcasted_iota(jnp.int32, (PAIR, PAIR), 1) // LANES
    ones = jnp.where(row == col, 1.0, 0.0).astype(BF16)
    high = values.astype(BF16)
    rest = (values - high.astype(F32)).astype(BF16)
    return jnp.concatenate(
        [
            dot(high[:, at : at + PAIR], ones) + dot(rest[:, at : at + PAIR], ones)
            for at in range(0, lanes, PAIR)
        ],
        axis=1,
    )


def put_lanes(values, first, parts):
    lanes = lane_ids(values.shape[0])
    for k, part in enumerate(parts):
        values = jnp.where(lanes == first + k, part.astype(values.dtype), values)
    return values


QK_SPARE = 100
V_SPARE = HEAD


PAIRS = OWN // 2
PAIR = 2 * LANES
PAIR_COLS = 2 * HEAD


def project_kernel(
    x0_ref, x1_ref, x2_ref, x3_ref, mod_ref, w_ref, cos_ref, sin_ref, gq_ref, gk_ref, spread_ref,
    attn_ref, qraw_ref, kraw_ref, q0_ref, q1_ref, k0_ref, k1_ref, v0_ref, v1_ref, wpad_ref,
):
    block = x0_ref.shape[0]
    tokens = 4 * block
    factor = LOG2E / math.sqrt(HEAD)

    for place, x_ref in enumerate((x0_ref, x1_ref, x2_ref, x3_ref)):
        x = x_ref[...].astype(F32)
        normed = x * inverse_rms(x)
        attn_ref[block * place : block * (place + 1), :] = (
            normed * (1.0 + mod_ref[1:2, :]) + mod_ref[0:1, :]
        ).astype(BF16)

    @pl.loop(0, w_ref.shape[0] // 128)
    def _(i):
        rows = pl.ds(pl.multiple_of(i * 128, 128), 128)
        for w in range(3):
            wpad_ref[rows, PADDED * w : PADDED * (w + 1)] = dot(
                w_ref[rows, 256 * w : 256 * w + WINDOW], spread_ref[w]
            ).astype(BF16)

    @pl.loop(0, tokens // block)
    def _(i):
        rows = pl.ds(pl.multiple_of(i * block, block), block)
        attn_in = attn_ref[rows, :]
        cos, sin = cos_ref[rows, :], sin_ref[rows, :]
        lanes = lane_ids(block)
        spare = (lanes >= QK_SPARE) & (lanes < QK_SPARE + 3)
        for which, raw_ref, out_refs, gain_ref in (
            (0, qraw_ref, (q0_ref, q1_ref), gq_ref),
            (1, kraw_ref, (k0_ref, k1_ref), gk_ref),
        ):
            raw = dot(attn_in, wpad_ref[:, PADDED * which : PADDED * (which + 1)])
            raw_ref[rows, :] = raw
            for head in range(OWN):
                part = raw[:, LANES * head : LANES * (head + 1)]
                inv = lax.rsqrt(jnp.sum(part * part, axis=-1, keepdims=True) / HEAD + EPSILON)
                scaled = part * inv * gain_ref[...]
                turned = scaled * cos + pltpu.roll(scaled, 64, 1) * sin
                turned = turned * factor if which == 0 else jnp.where(spare, 1.0, turned)
                at = slice(LANES * (head % 2), LANES * (head % 2 + 1))
                out_refs[head // 2][rows, at] = turned.astype(BF16)
        value = dot(attn_in, wpad_ref[:, PADDED * 2 : PADDED * 3])
        ones = (lanes >= V_SPARE) & (lanes < V_SPARE + 3)
        for head in range(OWN):
            at = slice(LANES * (head % 2), LANES * (head % 2 + 1))
            part = value[:, LANES * head : LANES * (head + 1)]
            (v0_ref, v1_ref)[head // 2][rows, at] = jnp.where(ones, 1.0, part).astype(BF16)


def project(x_tiles, mod, w, cos, sin, gq, gk, spread):
    width = w.shape[0]
    tokens = cos.shape[0]
    return pl.pallas_call(
        project_kernel,
        out_shape=[
            jax.ShapeDtypeStruct((tokens, width), BF16),
            jax.ShapeDtypeStruct((tokens, PADDED), F32),
            jax.ShapeDtypeStruct((tokens, PADDED), F32),
        ]
        + [jax.ShapeDtypeStruct((tokens, PAIR), BF16)] * 6,
        in_specs=[vmem()] * 11,
        out_specs=[vmem()] * 9,
        scratch_shapes=[pltpu.VMEM((width, 3 * PADDED), BF16)],
        cost_estimate=cost(16),
        compiler_params=limit(34),
        name="project",
    )(*x_tiles, mod, w, cos, sin, gq, gk, spread)


def attend_kernel(qin_ref, k_ref, v_ref, spread_ref, q_ref, mixedp_ref, mixed_ref):
    tokens = qin_ref.shape[0]
    block = 256
    for i in range(tokens // block):
        rows = slice(block * i, block * (i + 1))
        for head in range(2):
            at = slice(LANES * head, LANES * (head + 1))
            query = qin_ref[rows, at]
            terms = jnp.exp2(dot_nt(query, k_ref[:, at])).astype(BF16)
            result = dot(terms, v_ref[:, at])
            total = result[:, V_SPARE : V_SPARE + 1]
            mixedp_ref[rows, at] = (result * (1.0 / total)).astype(BF16)
            q_ref[rows, at] = put_lanes(query, QK_SPARE, three_parts(-jnp.log2(total)))
        mixed_ref[:, rows] = dot_nt(spread_ref[3, :PAIR_COLS, :PAIR], mixedp_ref[rows, :]).astype(BF16)


def attend(q, k, v, spread):
    tokens = q.shape[0]
    return pl.pallas_call(
        attend_kernel,
        out_shape=[
            jax.ShapeDtypeStruct((tokens, PAIR), BF16),
            jax.ShapeDtypeStruct((tokens, PAIR), BF16),
            jax.ShapeDtypeStruct((PAIR_COLS, tokens), BF16),
        ],
        in_specs=[vmem()] * 4,
        out_specs=[vmem()] * 3,
        cost_estimate=cost(4.1),
        compiler_params=limit(20),
        name="attend",
    )(q, k, v, spread)


def attention_back_kernel(
    g0_ref, g1_ref, g2_ref, g3_ref, wout_ref, qraw_ref, kraw_ref, q0_ref, q1_ref, k0_ref, k1_ref, v0_ref, v1_ref,
    m0_ref, m1_ref, cos_ref, sin_ref, gq_ref, gk_ref, spread_ref, out_ref, gains_ref, do_ref, dq_ref, dk_ref, pad_ref,
    *scratch
):
    sems = scratch[-1]
    late = (q0_ref, k0_ref, v0_ref, q1_ref, k1_ref, v1_ref, cos_ref, sin_ref, qraw_ref, kraw_ref)
    copies = [pltpu.make_async_copy(src, dst, sems.at[n]) for n, (src, dst) in enumerate(zip(late, scratch))]
    for copy in copies:
        copy.start()
    q0_ref, k0_ref, v0_ref, q1_ref, k1_ref, v1_ref, cos_ref, sin_ref, qraw_ref, kraw_ref = scratch[:-1]
    block = g0_ref.shape[0]
    tokens = 4 * block
    root = 1.0 / math.sqrt(HEAD)

    for place, g_ref in enumerate((g0_ref, g1_ref, g2_ref, g3_ref)):
        rows = slice(block * place, block * (place + 1))
        grad_mixed = dot(g_ref[...], wout_ref[...]).astype(BF16)
        wide = dot(grad_mixed, spread_ref[3, :COLS, :])
        mixed = jnp.concatenate([m0_ref[rows, :], m1_ref[rows, :]], axis=1).astype(F32)
        row_dot = head_sums(wide * mixed)
        for head in range(OWN):
            at = slice(LANES * head, LANES * (head + 1))
            do_ref[rows, at] = put_lanes(wide[:, at].astype(BF16), V_SPARE, three_parts(-row_dot[:, at]))

    for head in range(OWN):
        at = slice(LANES * head, LANES * (head + 1))
        pair_at = slice(LANES * (head % 2), LANES * (head % 2 + 1))
        q_ref, k_ref, v_ref = ((q0_ref, k0_ref, v0_ref), (q1_ref, k1_ref, v1_ref))[head // 2]
        if head % 2 == 0:
            for copy in copies[3 * (head // 2) : 3 * (head // 2) + 3]:
                copy.wait()
        dq_ref[at, :] = jnp.zeros((LANES, tokens), F32)

        for i in range(tokens // block):
            rows = slice(block * i, block * (i + 1))
            query, grad = q_ref[:, pair_at], do_ref[:, at]
            key = k_ref[rows, pair_at]
            probs = jnp.exp2(dot_nt(key, query))
            slope = (probs * dot_nt(v_ref[rows, pair_at], grad)).astype(BF16)
            pad_ref[rows, 2 * PADDED + LANES * head : 2 * PADDED + LANES * (head + 1)] = dot(
                probs.astype(BF16), grad
            ).astype(BF16)
            dk_ref[rows, at] = dot(slope, query) * LN2
            dq_ref[at, :] += dot(key.astype(F32).T.astype(BF16), slope)

    for copy in copies[6:]:
        copy.wait()
    gains_ref[...] = jnp.zeros_like(gains_ref)

    @pl.loop(0, tokens // block)
    def _(i):
        rows = pl.ds(pl.multiple_of(i * block, block), block)
        cos, sin = cos_ref[rows, :], sin_ref[rows, :]
        for which, raw_ref, gain_ref in ((0, qraw_ref, gq_ref), (1, kraw_ref, gk_ref)):
            raw = raw_ref[rows, :]
            inv = lax.rsqrt(head_sums(raw * raw) / HEAD + EPSILON)
            hat = raw * inv
            turned = []
            for head in range(OWN):
                at = slice(LANES * head, LANES * (head + 1))
                grad = dq_ref[at, rows].T * root if which == 0 else dk_ref[rows, at]
                turned.append(grad * cos - pltpu.roll(grad, 64, 1) * sin)
            gain = jnp.concatenate([gain_ref[...]] * OWN, axis=1)
            product = jnp.concatenate(turned, axis=1) * hat
            gained = jnp.sum(product, axis=0, keepdims=True)
            gains_ref[which : which + 1, :] += sum(
                gained[:, LANES * head : LANES * (head + 1)] for head in range(OWN)
            )
            mean = head_sums(product * gain) / HEAD
            pad_ref[rows, PADDED * which : PADDED * (which + 1)] = (
                inv * (jnp.concatenate(turned, axis=1) * gain - hat * mean)
            ).astype(BF16)
        compact = [
            dot_nt(pad_ref[rows, PADDED * w : PADDED * (w + 1)], spread_ref[w]).astype(BF16)
            for w in range(3)
        ]
        out_ref[rows, :] = jnp.concatenate(
            [
                compact[0][:, :256],
                compact[0][:, 256:] + compact[1][:, :128],
                compact[1][:, 128:256],
                compact[1][:, 256:] + compact[2][:, :128],
                compact[2][:, 128:],
            ],
            axis=1,
        )[:, : 3 * COLS]


def attention_backward(grads, w_rows, qraw, kraw, q, k, v, mixedp, cos, sin, gq, gk, spread):
    tokens = cos.shape[0]
    return pl.pallas_call(
        attention_back_kernel,
        out_shape=[
            jax.ShapeDtypeStruct((tokens, 3 * COLS), BF16),
            jax.ShapeDtypeStruct((8, LANES), F32),
        ],
        in_specs=[vmem()] * 5 + [hbm()] * 8 + [vmem()] * 2 + [hbm()] * 2 + [vmem()] * 3,
        out_specs=[vmem()] * 2,
        scratch_shapes=[
            pltpu.VMEM((tokens, PADDED), BF16),
            pltpu.VMEM((PADDED, tokens), F32),
            pltpu.VMEM((tokens, PADDED), F32),
            pltpu.VMEM((tokens, 3 * PADDED), BF16),
        ]
        + [pltpu.VMEM((tokens, PAIR), BF16)] * 6
        + [pltpu.VMEM((tokens, LANES), F32)] * 2
        + [pltpu.VMEM((tokens, PADDED), F32)] * 2
        + [pltpu.SemaphoreType.DMA((10,))],
        cost_estimate=cost(K5_COST),
        compiler_params=limit(58),
        name="attention_backward",
    )(*grads, w_rows, qraw, kraw, *q, *k, *v, *mixedp, cos, sin, gq, gk, spread)


def smem():
    return pl.BlockSpec(memory_space=pltpu.SMEM)


def out_weight_kernel(tile_ref, p0_ref, p1_ref, p2_ref, p3_ref, out_ref, own_ref):
    for place, piece in enumerate((p0_ref, p1_ref, p2_ref, p3_ref)):
        start = pl.multiple_of((tile_ref[0] ^ FLIPS[place]) * COLS, 16)
        out_ref[pl.ds(start, COLS), :] = piece[...]
    for tile in range(4):

        @pl.when(tile_ref[0] == tile)
        def _(tile=tile):
            own_ref[...] = out_ref[:, COLS * tile : COLS * (tile + 1)]


def out_weight(tile, pieces):
    width = pieces[0].shape[1]
    return pl.pallas_call(
        out_weight_kernel,
        out_shape=[
            jax.ShapeDtypeStruct((width, width), BF16),
            jax.ShapeDtypeStruct((width, COLS), BF16),
        ],
        in_specs=[smem()] + [vmem()] * 4,
        out_specs=[vmem()] * 2,
        cost_estimate=cost(3.8),
        compiler_params=limit(12),
        name="out_weight",
    )(tile, *pieces)


def mlp_kernel(places, tile_ref, mod_ref, wout_ref, wgu_ref, wdown_ref, *refs):
    number = len(places)
    x_refs, dy_refs, mixed_refs = refs[:number], refs[number : 2 * number], refs[2 * number : 2 * number + 4 * PAIRS]
    refs = refs[-(4 + 2 * number + (2 in places) + 1) :]
    mlp_ref, hidden_ref, ggu_ref, gbranch_ref = refs[:4]
    branch_refs, gmlp_refs, mixed_ref = refs[4 : 4 + number], refs[4 + number : 4 + 2 * number], refs[-1]
    block = x_refs[0].shape[0]
    half = wgu_ref.shape[1] // 2
    for k, m_ref in enumerate(mixed_refs):
        pair, source = k // 4, k % 4
        start = pl.multiple_of((tile_ref[0] ^ FLIPS[source]) * COLS + PAIR_COLS * pair, 16)
        for n, place in enumerate(places):
            at = block * (place ^ FLIPS[source])
            mixed_ref[pl.ds(start, PAIR_COLS), block * n : block * (n + 1)] = m_ref[:, at : at + block]
    for n, (place, x_ref, dy_ref, branch_ref, gmlp_ref) in enumerate(
        zip(places, x_refs, dy_refs, branch_refs, gmlp_refs)
    ):
        at = slice(block * n, block * (n + 1))
        here = slice(0, block) if number == 1 else slice(block * place, block * (place + 1))
        attended = lax.dot_general(
            mixed_ref[:, at], wout_ref[...], (((0,), (1,)), ((), ())), preferred_element_type=F32
        )
        if place == 2:
            refs[-2][...] = attended
        x_mid = x_ref[...].astype(F32) + mod_ref[2:3, :] * attended
        normed = x_mid * inverse_rms(x_mid)
        mlp_in = (normed * (1.0 + mod_ref[4:5, :]) + mod_ref[3:4, :]).astype(BF16)
        mlp_ref[here, :] = mlp_in
        grad_branch = (mod_ref[5:6, :] * (mod_ref[6:7, :] * dy_ref[...].astype(F32))).astype(BF16)
        gbranch_ref[here, :] = grad_branch
        gate = dot(mlp_in, wgu_ref[:, :half])
        up = dot(mlp_in, wgu_ref[:, half:])
        grad_hidden = dot_nt(grad_branch, wdown_ref[...])
        sigmoid = jax.nn.sigmoid(gate)
        silu = gate * sigmoid
        hidden = (silu * up).astype(BF16)
        hidden_ref[here, :] = hidden
        branch_ref[...] = dot(hidden, wdown_ref[...]).astype(BF16)
        grad_gate = (grad_hidden * up * (sigmoid * (1.0 + gate * (1.0 - sigmoid)))).astype(BF16)
        grad_up = (grad_hidden * silu).astype(BF16)
        ggu_ref[here, :half] = grad_gate
        ggu_ref[here, half:] = grad_up
        gmlp_ref[...] = (
            dot_nt(grad_gate, wgu_ref[:, :half]) + dot_nt(grad_up, wgu_ref[:, half:])
        ).astype(BF16)


def mlp(places, tile, mod, w_out, w_gu, w_down, x_tiles, dy_tiles, mixed, kept):
    number = len(places)
    block, width = x_tiles[0].shape
    hidden = w_down.shape[0]
    one = pl.Buffered(1)
    if number == 1:
        row_block = lambda cols: pl.BlockSpec((block, cols), lambda i: (places[0], 0), pipeline_mode=one)
    else:
        row_block = lambda cols: pl.BlockSpec((4 * block, cols), lambda i: (0, 0), pipeline_mode=one)
    whole = lambda rows, cols: pl.BlockSpec((rows, cols), lambda i: (0, 0), pipeline_mode=one)
    args = [mod, w_out, w_gu, w_down]
    args += [x_tiles[p] for p in places] + [dy_tiles[p] for p in places] + list(mixed)
    in_specs = [smem()] + [whole(*arg.shape) for arg in args]
    args = [tile] + args
    aliases = {}
    for k, array in enumerate(kept):
        aliases[len(args)] = k
        args.append(array)
        in_specs.append(hbm())
    shapes = [(4 * block, width), (4 * block, hidden), (4 * block, 2 * hidden), (4 * block, width)]
    attended = [jax.ShapeDtypeStruct((block, width), F32)] if 2 in places else []
    return pl.pallas_call(
        functools.partial(mlp_kernel, places),
        grid=(1,),
        out_shape=[jax.ShapeDtypeStruct(shape, BF16) for shape in shapes]
        + [jax.ShapeDtypeStruct((block, width), BF16)] * (2 * number)
        + attended,
        in_specs=in_specs,
        out_specs=[row_block(shape[1]) for shape in shapes]
        + [whole(block, width)] * (2 * number + len(attended)),
        scratch_shapes=[pltpu.VMEM((width, number * block), BF16)],
        input_output_aliases=aliases,
        compiler_params=limit(58),
        cost_estimate=cost(7 * number),
        name="mlp",
    )(*args)


def middle_kernel(a_ref, b_ref, c_ref, attended_ref, x_ref, dy_ref, mod_ref, gatt_ref, gmid_ref, sums_ref):
    grad_in = a_ref[...].astype(F32) + b_ref[...].astype(F32) + c_ref[...].astype(F32)
    attended = attended_ref[...]
    x_mid = x_ref[...].astype(F32) + mod_ref[2:3, :] * attended
    inv = inverse_rms(x_mid)
    normed = x_mid * inv
    product = grad_in * normed
    grad_mid = mod_ref[6:7, :] * dy_ref[...].astype(F32) + inv * (
        grad_in * (1.0 + mod_ref[4:5, :])
        - normed * jnp.mean(product * (1.0 + mod_ref[4:5, :]), axis=-1, keepdims=True)
    )
    gmid_ref[...] = grad_mid
    gatt_ref[...] = (mod_ref[2:3, :] * grad_mid).astype(BF16)
    sums_ref[...] = jnp.zeros_like(sums_ref)
    sums_ref[0:1, :] = jnp.sum(grad_mid * attended, axis=0, keepdims=True)
    sums_ref[1:2, :] = jnp.sum(grad_in, axis=0, keepdims=True)
    sums_ref[2:3, :] = jnp.sum(product, axis=0, keepdims=True)


def middle(parts, attended, x, dy, mod):
    block, width = x.shape
    return pl.pallas_call(
        middle_kernel,
        out_shape=[
            jax.ShapeDtypeStruct((block, width), BF16),
            jax.ShapeDtypeStruct((block, width), F32),
            jax.ShapeDtypeStruct((8, width), F32),
        ],
        in_specs=[vmem()] * 7,
        out_specs=[vmem()] * 3,
        cost_estimate=cost(4.6),
        compiler_params=limit(14),
        name="middle",
    )(*parts, attended, x, dy, mod)


def output_kernel(a_ref, b_ref, c_ref, attended_ref, x_ref, dy_ref, mod_ref, out_ref, sums_ref):
    branch = a_ref[...].astype(F32) + b_ref[...].astype(F32) + c_ref[...].astype(F32)
    x_mid = x_ref[...].astype(F32) + mod_ref[2:3, :] * attended_ref[...]
    live = mod_ref[6:7, :]
    out_ref[...] = (live * (x_mid + mod_ref[5:6, :] * branch)).astype(BF16)
    sums_ref[...] = jnp.zeros_like(sums_ref)
    sums_ref[0:1, :] = jnp.sum(live * dy_ref[...].astype(F32) * branch, axis=0, keepdims=True)


def output_tile(parts, attended, x, dy, mod):
    block, width = x.shape
    return pl.pallas_call(
        output_kernel,
        out_shape=[
            jax.ShapeDtypeStruct((block, width), BF16),
            jax.ShapeDtypeStruct((8, width), F32),
        ],
        in_specs=[vmem()] * 7,
        out_specs=[vmem()] * 2,
        cost_estimate=cost(3.5),
        compiler_params=limit(12),
        name="output_tile",
    )(*parts, attended, x, dy, mod)


def tokens_kernel(a_ref, b_ref, c_ref, x_ref, gmid_ref, mod_ref, out_ref, sums_ref):
    grad_in = a_ref[...].astype(F32) + b_ref[...].astype(F32) + c_ref[...].astype(F32)
    x = x_ref[...].astype(F32)
    inv = inverse_rms(x)
    normed = x * inv
    product = grad_in * normed
    scale = 1.0 + mod_ref[1:2, :]
    out_ref[...] = (
        gmid_ref[...] + inv * (grad_in * scale - normed * jnp.mean(product * scale, axis=-1, keepdims=True))
    ).astype(BF16)
    sums_ref[...] = jnp.zeros_like(sums_ref)
    sums_ref[0:1, :] = jnp.sum(grad_in, axis=0, keepdims=True)
    sums_ref[1:2, :] = jnp.sum(product, axis=0, keepdims=True)


def tokens_back(parts, x, grad_mid, mod):
    block, width = x.shape
    return pl.pallas_call(
        tokens_kernel,
        out_shape=[
            jax.ShapeDtypeStruct((block, width), BF16),
            jax.ShapeDtypeStruct((8, width), F32),
        ],
        in_specs=[vmem()] * 6,
        out_specs=[vmem()] * 2,
        cost_estimate=cost(3.6),
        compiler_params=limit(14),
        name="tokens_back",
    )(*parts, x, grad_mid, mod)


def first_grad_kernel(tile_ref, g0_ref, g1_ref, g2_ref, g3_ref, *refs):
    mixed_refs, (attn_ref, qkv_ref, out_ref, cols_ref) = refs[: 4 * PAIRS], refs[4 * PAIRS :]
    block = g0_ref.shape[0]
    wide = qkv_ref.shape[1]
    for tile in range(4):

        @pl.when(tile_ref[0] == tile)
        def _(tile=tile):
            for place, g_ref in enumerate((g0_ref, g1_ref, g2_ref, g3_ref)):
                cols_ref[block * place : block * (place + 1), :] = g_ref[:, COLS * tile : COLS * (tile + 1)]

    for k in range(attn_ref.shape[1] // LANES):
        at = slice(LANES * k, LANES * (k + 1))
        out_ref[at, :wide] = dot_tn(attn_ref[:, at], qkv_ref[...]).astype(BF16)
    for k, m_ref in enumerate(mixed_refs):
        pair, source = k // 4, k % 4
        total = None
        for place in range(4):
            at = block * (place ^ FLIPS[source])
            term = dot(m_ref[:, at : at + block], cols_ref[block * place : block * (place + 1), :])
            total = term if total is None else total + term
        start = pl.multiple_of((tile_ref[0] ^ FLIPS[source]) * COLS + PAIR_COLS * pair, 16)
        out_ref[pl.ds(start, PAIR_COLS), wide:] = total.astype(BF16)


def first_grad(tile, grads, mixed, attn_in, grad_qkv):
    width = attn_in.shape[1]
    return pl.pallas_call(
        first_grad_kernel,
        out_shape=jax.ShapeDtypeStruct((width, grad_qkv.shape[1] + COLS), BF16),
        in_specs=[smem()] + [vmem()] * (6 + 4 * PAIRS),
        out_specs=vmem(),
        scratch_shapes=[pltpu.VMEM((grad_qkv.shape[0], COLS), BF16)],
        compiler_params=limit(24),
        cost_estimate=cost(8),
        name="first_grad",
    )(tile, *grads, *mixed, attn_in, grad_qkv)


def weight_grad_kernel(left_ref, right_ref, out_ref):
    for k in range(left_ref.shape[1] // LANES):
        at = slice(LANES * k, LANES * (k + 1))
        out_ref[at, :] = dot_tn(left_ref[:, at], right_ref[...]).astype(BF16)


def weight_grad(left, right, microseconds):
    return pl.pallas_call(
        weight_grad_kernel,
        out_shape=jax.ShapeDtypeStruct((left.shape[1], right.shape[1]), BF16),
        in_specs=[vmem()] * 2,
        out_specs=vmem(),
        compiler_params=limit(24),
        cost_estimate=cost(microseconds),
        name="weight_grad",
    )(left, right)


GU_AFTER = 5
K5_COST = 32
GU_BY = 3
TO_TX = (1, 0, 2, 1)
TO_TY = (2, 2, 0, 0)
KEPT = (0, 1, 1, 2)
SLOTS = ((0, 1, 2), (2, 1, 0), (0, 1, 2), (2, 1, 0))


def pack_kernel(shard, ff_own, tile_ref, a_ref, b_ref, tx_ref, ty_ref, down_ref, unit_ref, out_ref):
    cut = a_ref.shape[0]

    def rows(first, last, lanes):
        pieces = []
        if first < cut:
            pieces.append(a_ref[first : min(last, cut), lanes])
        if last > cut:
            pieces.append(b_ref[max(first, cut) - cut : last - cut, lanes])
        return pieces[0] if len(pieces) == 1 else jnp.concatenate(pieces)

    def down(tile):
        return rows(shard, shard + ff_own, slice(COLS * tile, COLS * (tile + 1)))

    def unit(part):
        return rows(0, shard, slice(COLS * part, COLS * (part + 1)))

    out_ref[...] = unit(3)
    for tile in range(4):

        @pl.when(tile_ref[0] == tile)
        def _(tile=tile):
            for ref, pieces in (
                (tx_ref, (down(tile ^ 1), down(tile ^ 3), unit(TO_TX[tile]))),
                (ty_ref, (down(tile ^ 2), unit(TO_TY[tile]))),
            ):
                at = 0
                for piece in pieces:
                    ref[at : at + piece.shape[0], :COLS] = piece.astype(BF16)
                    at += piece.shape[0]
            down_ref[...] = down(tile)
            unit_ref[...] = unit(KEPT[tile])


def pack(tile, sums, shard, ff_own):
    return pl.pallas_call(
        functools.partial(pack_kernel, shard, ff_own),
        out_shape=[
            jax.ShapeDtypeStruct((shard + 2 * ff_own, WINDOW), BF16),
            jax.ShapeDtypeStruct((shard + ff_own, WINDOW), BF16),
            jax.ShapeDtypeStruct((ff_own, COLS), F32),
            jax.ShapeDtypeStruct((shard, COLS), F32),
            jax.ShapeDtypeStruct((shard, COLS), F32),
        ],
        in_specs=[smem()] + [vmem()] * 2,
        out_specs=[vmem()] * 5,
        compiler_params=limit(12),
        cost_estimate=cost(2),
        name="pack",
    )(tile, *sums)


def unpack_kernel(
    shard, ff_own, tile_ref, tx_ref, ty_ref, on_ref, down_ref, unit_ref, sgu_ref, gutx_ref, guty_ref,
    wgu_ref, wdown_ref, wqkv_ref,
):
    share = sgu_ref.shape[1] // 4
    groups = share // ff_own
    gus = [None, gutx_ref[:shard, :], guty_ref[:shard, :], guty_ref[shard:, :]]
    downs = [
        down_ref[...],
        tx_ref[:ff_own, :COLS].astype(F32),
        ty_ref[:ff_own, :COLS].astype(F32),
        on_ref[:, :COLS].astype(F32),
    ]
    units = [unit_ref[...], tx_ref[2 * ff_own :, :COLS].astype(F32), ty_ref[ff_own:, :COLS].astype(F32)]
    for tile in range(4):

        @pl.when(tile_ref[0] == tile)
        def _(tile=tile):
            for source in range(4):
                flip = source ^ tile
                wdown_ref[ff_own * source : ff_own * (source + 1), :] = downs[flip]
                piece = sgu_ref[:, share * tile : share * (tile + 1)] if flip == 0 else gus[flip]
                for group in range(groups):
                    at = share * group + ff_own * source
                    wgu_ref[:, at : at + ff_own] = piece[:, ff_own * group : ff_own * (group + 1)].astype(F32)
            for k in range(3):
                wqkv_ref[:, COLS * k : COLS * (k + 1)] = units[SLOTS[tile][k]]


def unpack(tile, from_tx, from_ty, passed_on, kept, gus, shard, ff_own):
    return pl.pallas_call(
        functools.partial(unpack_kernel, shard, ff_own),
        out_shape=[
            jax.ShapeDtypeStruct(gus[0].shape, F32),
            jax.ShapeDtypeStruct((4 * ff_own, COLS), F32),
            jax.ShapeDtypeStruct((shard, 3 * COLS), F32),
        ],
        in_specs=[smem()] + [vmem()] * 8,
        out_specs=[vmem()] * 3,
        compiler_params=limit(12),
        cost_estimate=cost(2),
        name="unpack",
    )(tile, from_tx, from_ty, passed_on, *kept, *gus)


def ada_kernel(tile_ref, mod_ref, w_ref, silu_ref, ada_ref, bias_ref, cond_ref):
    count, wide = mod_ref.shape
    width = w_ref.shape[1]
    share = width // 4
    for tile in range(4):

        @pl.when(tile_ref[0] == tile)
        def _(tile=tile):
            ada_ref[...] = dot_tn(silu_ref[...], mod_ref[:, share * tile : share * (tile + 1)])

    rows = [mod_ref[k : k + 1, :].astype(F32) for k in range(count)]
    while len(rows) > 1:
        rows = [rows[k] + rows[k + 1] for k in range(0, len(rows), 2)]
    bias_ref[...] = rows[0]
    cond_ref[...] = dot_nt(mod_ref[:, :width], w_ref[...])


def ada_back(tile, mod_all, w_ada, silu_rows):
    count, wide = mod_all.shape
    shard, width = w_ada.shape
    return pl.pallas_call(
        ada_kernel,
        out_shape=[
            jax.ShapeDtypeStruct((shard, width // 4), F32),
            jax.ShapeDtypeStruct((1, wide), F32),
            jax.ShapeDtypeStruct((count, shard), F32),
        ],
        in_specs=[smem()] + [vmem()] * 3,
        out_specs=[vmem()] * 3,
        cost_estimate=cost(3.5),
        compiler_params=limit(12),
        name="ada_back",
    )(tile, mod_all, w_ada, silu_rows)


def reorder_kernel(index_ref, rows_ref, out_ref):
    for k in range(rows_ref.shape[0]):
        out_ref[k : k + 1, :] = rows_ref[pl.ds(index_ref[k], 1), :]


def reorder(index, rows):
    return pl.pallas_call(
        reorder_kernel,
        out_shape=jax.ShapeDtypeStruct(rows.shape, rows.dtype),
        in_specs=[smem(), vmem()],
        out_specs=vmem(),
        cost_estimate=cost(1.3),
        compiler_params=limit(4),
        name="reorder",
    )(index, rows)


def lane_matrix():
    matrix = np.zeros((HEAD, LANES), np.float32)
    for index in range(HEAD):
        matrix[index, head_lane(index)] = 1.0
    return matrix


def rope_lanes(tile_rows, tile_cols):
    freqs = (10000.0 ** (-np.arange(QUARTER, dtype=np.float64) / QUARTER)).astype(np.float32)
    freq = np.zeros((LANES,), np.float32)
    part = np.zeros((LANES,), np.int32)
    sign = np.zeros((LANES,), np.float32)
    for index in range(HEAD):
        lane = head_lane(index)
        freq[lane] = freqs[index % QUARTER]
        part[lane] = index // 36
        sign[lane] = 1.0 if lane >= 64 else -1.0
    per_tile = tile_rows * tile_cols
    ids = np.arange(4 * per_tile)
    flips = np.array(FLIPS)[ids // per_tile]
    ty = lax.axis_index("ty") ^ jnp.asarray(flips >> 1, jnp.int32)
    tx = lax.axis_index("tx") ^ jnp.asarray(flips & 1, jnp.int32)
    rows = (ty * tile_rows + jnp.asarray(ids % per_tile // tile_cols, jnp.int32)).astype(F32)
    cols = (tx * tile_cols + jnp.asarray(ids % tile_cols, jnp.int32)).astype(F32)
    angle = jnp.where(jnp.asarray(part)[None] == 0, rows[:, None], cols[:, None]) * jnp.asarray(freq)[None]
    live = jnp.asarray((sign != 0).astype(np.float32))[None]
    return jnp.cos(angle) * live, jnp.sin(angle) * jnp.asarray(sign)[None]


def gain_lanes(gain):
    return jnp.sum(jnp.asarray(lane_matrix()) * gain[:, None], axis=0, keepdims=True)


def gain_back(lanes):
    return jnp.sum(jnp.asarray(lane_matrix()) * lanes[None, :], axis=1)


def tile_pair(far):
    return (far[0].astype(F32) + swap(far[1], "tx").astype(F32)).astype(BF16)


def tile_sum_parts(pair, near):
    return near[0], swap(near[1], "tx"), swap(pair, "ty")


def body(
    count, tokens, cond, live_count, w_qkv, w_out, w_gu, w_down, w_ada, ada_bias, q_gain, k_gain, cotangent
):
    _, tile_rows, tile_cols, width = tokens.shape
    per_tile = tile_rows * tile_cols
    img, ty, tx = lax.axis_index("img"), lax.axis_index("ty"), lax.axis_index("tx")
    tile = ty * 2 + tx
    tile_word = tile[None].astype(jnp.int32)
    live = (live_count[0] > 0).astype(F32)
    shard = width // count
    ff_shard = FF // count
    ff_own = ff_shard // TILES
    hidden_own = FF // TILES
    out_width = width // TILES
    spread = jnp.asarray(spread_matrices(), BF16)

    first = jnp.concatenate(
        [lax.dynamic_slice_in_dim(w_qkv, p * width + tile * COLS, COLS, 1) for p in range(3)]
        + [lax.dynamic_slice_in_dim(w_out, tile * out_width, out_width, 1)],
        axis=1,
    )
    down_own = lax.dynamic_slice_in_dim(w_down, tile * ff_own, ff_own, 0)
    gu_own = lax.dynamic_slice_in_dim(w_gu.reshape(shard, 2 * count, ff_shard), tile * ff_own, ff_own, 2)
    gu_own = gu_own.reshape(shard, 2 * hidden_own)

    x_own = tokens.reshape(per_tile, width)
    dy_own = cotangent.reshape(per_tile, width)
    x_tiles = gather_tiles(x_own)
    dy_tiles = gather_tiles(dy_own)

    cond_float = cond.astype(F32)
    bits = [1 << k for k in range(count.bit_length() - 1)]
    store = {}

    def gather_step(v, bit):
        return jnp.concatenate([v, lax.ppermute(v, "img", flip_perm(count, bit))])

    def scatter_step(v, bit):
        return v[:bit] + lax.ppermute(v[bit:], "img", flip_perm(count, bit))

    silu_some = jax.nn.silu(cond_float).astype(BF16)
    for bit in bits[:-1]:
        silu_some = gather_step(silu_some, bit)

    def rows_step(_):
        store["silu_rows"] = lax.dynamic_slice_in_dim(gather_step(silu_some, bits[-1]), img * shard, shard, 1)
        return store["silu_rows"]

    beside = [rows_step, lambda v: scatter_step(dot(v, w_ada), bits[-1])]
    beside += [lambda v, bit=bit: scatter_step(v, bit) for bit in bits[-2::-1]]
    early = beside[2]
    beside[2] = lambda v: after(early(v), x_tiles)
    beside.append(lambda v: after(v, dy_tiles))

    ring = use_ring(count, math.gcd(shard, ff_own))
    if ring:
        own = after(jnp.concatenate([first, down_own]), silu_some)
        pieces, modulation = ring_gather(own, count, beside)
        full_first, full_down, out_own = assemble(
            own,
            pieces,
            [(width, width), (hidden_own, width), (COLS, width)],
            [(0, shard, 0, shard, 0, 0, 0, width), (1, ff_own, shard, ff_own, 0, 0, 0, width)],
            count,
            True,
        )
        full_gu = lax.all_gather(after(gu_own, pieces[GU_AFTER]), "img", axis=0, tiled=True)
    else:
        full_first, full_down, full_gu = [
            lax.all_gather(a, "img", axis=0, tiled=True) for a in (first, down_own, gu_own)
        ]
        out_own = out_share(out_pick(), full_first)
        modulation = None
        for step in beside:
            modulation = step(modulation)
    silu_rows = store["silu_rows"]
    modulation = modulation + ada_bias
    mod = jnp.concatenate([modulation.reshape(6, width), jnp.broadcast_to(live, (2, width))])

    cos, sin = rope_lanes(tile_rows, tile_cols)
    gq, gk = gain_lanes(q_gain), gain_lanes(k_gain)
    attn_in, qraw, kraw, q0, q1, k0, k1, v0, v1 = project(
        x_tiles, mod, full_first, cos, sin, gq, gk, spread
    )
    out_far = swap(out_own, "ty")
    out_far = after(out_far, attn_in)
    full_out, out_rows = out_weight(
        tile_word, [out_far, swap(out_far, "tx"), out_own, swap(out_own, "tx")]
    )
    q0, mixedp0, mixed0 = attend(q0, k0, v0, spread)
    mixed = gather_tiles(mixed0)
    q1, mixedp1, mixed1 = attend(after(q1, full_out, mixed0), k1, v1, spread)
    mixed += gather_tiles(mixed1)

    weights = (tile_word, mod, full_out, full_gu, full_down, x_tiles, dy_tiles, mixed)
    others = mlp((1, 0, 3), *weights, ())
    grad_pair = tile_pair((others[8], others[7]))
    grad_far = swap(grad_pair, "ty")
    own_tile = mlp((2,), *weights, after(others[:4], grad_pair))
    mlp_in, hidden, grad_gu, grad_branch = own_tile[:4]
    attended = own_tile[6]

    grad_att, grad_mid, mid_sums = middle(
        (own_tile[5], swap(others[9], "tx"), grad_far), attended, x_own, dy_own, mod
    )
    g_gu = weight_grad(mlp_in, after(grad_gu, grad_att), 5)
    g_down = weight_grad(hidden, after(grad_branch, g_gu), 3)
    att_far = after(swap(grad_att, "ty"), g_gu, g_down)
    grad_att_tiles = [att_far, swap(att_far, "tx"), grad_att, swap(grad_att, "tx")]

    grad_qkv, gains = attention_backward(
        grad_att_tiles, out_rows, qraw, kraw, (q0, q1), (k0, k1), (v0, v1), (mixedp0, mixedp1),
        cos, sin, gq, gk, spread,
    )
    branch_parts = tile_sum_parts(tile_pair((others[5], others[4])), (own_tile[4], others[6]))
    grad_qkv = after(grad_qkv, branch_parts)
    w_back = full_first[:, : 3 * COLS]
    back_far = dot_nt(grad_qkv[: 2 * per_tile], w_back).astype(BF16)
    halves = lambda rows: (rows[:per_tile], rows[per_tile:])
    back_pair = tile_pair(halves(back_far))
    late_qkv = after(grad_qkv, back_pair)
    back_near = dot_nt(late_qkv[2 * per_tile :], w_back).astype(BF16)
    g_first = first_grad(tile_word, grad_att_tiles, mixed, attn_in, late_qkv)

    wide = 6 * width

    def output_step():
        store["output"], store["out_sums"] = output_tile(
            branch_parts, attended, x_own, dy_own, mod
        )
        return store["out_sums"]

    def token_step():
        parts = tile_sum_parts(back_pair, halves(back_near))
        store["grad_tokens"], tok_sums = tokens_back(parts, x_own, grad_mid, mod)
        return jnp.concatenate(
            [tok_sums[0], tok_sums[1], mid_sums[0], mid_sums[1], mid_sums[2], store["out_sums"][0], gains[0], gains[1]]
        )[None]

    def low_step(grad_mod):
        return jnp.concatenate([grad_mod[:, :wide].astype(BF16), *three_parts(grad_mod[:, wide:])], axis=1)

    def ada_step(mod_all):
        store["grad_ada"], store["sums"], grad_silu = ada_back(tile_word, mod_all, w_ada, silu_rows)
        return grad_silu

    steps = [lambda _: output_step(), lambda _: token_step(), lambda v: low_step(sum_tiles(v))]
    steps += [lambda v, bit=bit: gather_step(v, bit) for bit in bits]
    steps.append(lambda v: flip_exchange(ada_step(v), count, bits[-1:]))

    if ring:
        s_gu = lax.psum_scatter(g_gu, "img", scatter_dimension=0, tiled=True)
        gu_cols = 2 * hidden_own // TILES

        def gu_piece(flip):
            return lax.dynamic_slice_in_dim(s_gu, tile_at(flip) * gu_cols, gu_cols, 1)

        def gu_tx_step(v):
            store["gu_tx"] = swap(jnp.concatenate([gu_piece(1), gu_piece(3)]), "tx")
            return after(v, store["gu_tx"])

        def gu_ty_step(v):
            store["gu_ty"] = swap(jnp.concatenate([gu_piece(2), store["gu_tx"][shard:]]), "ty")
            return after(v, store["gu_ty"])

        first_half, second_half = steps[GU_BY], steps[GU_BY + 1]
        steps[GU_BY] = lambda v: gu_tx_step(first_half(v))
        steps[GU_BY + 1] = lambda v: gu_ty_step(second_half(v))
        s_all, grad_silu = ring_scatter([g_first, g_down], count, steps)
    else:
        grad_silu = None
        for step in steps:
            grad_silu = step(grad_silu) if step else None
    grad_tokens, grad_ada, sums = store["grad_tokens"], store["grad_ada"], store["sums"]
    grad_bias = sums[0, :wide]
    gain_sums = (sums[:, wide : wide + 256] + sums[:, wide + 256 : wide + 512]) + sums[:, wide + 512 :]
    if ring:
        to_tx, to_ty, *kept, grad_w_out = pack(tile_word, s_all, shard, ff_own)
        from_tx = swap(to_tx, "tx")
        passed_on = swap(from_tx[ff_own : 2 * ff_own], "ty")
        from_ty = swap(to_ty, "ty")
        grad_w_gu, grad_down, grad_w_qkv = unpack(
            tile_word, from_tx, from_ty, passed_on, kept, (s_gu, store["gu_tx"], store["gu_ty"]), shard, ff_own
        )
        grad_silu = after(grad_silu, from_tx)
    else:
        sums_of = lambda grad: lax.psum_scatter(grad, "img", scatter_dimension=0, tiled=True)
        s_first, s_down, s_gu = sums_of(g_first).astype(F32), sums_of(g_down), sums_of(g_gu)
        gu_cols = 2 * hidden_own // TILES
        got = exchange_tiles(lambda t: lax.dynamic_slice_in_dim(s_gu, t * gu_cols, gu_cols, 1))
        grad_w_out = s_first[:, 3 * COLS :].astype(F32)
        s_qkv = s_first.astype(BF16)

        grad_down = jnp.concatenate(
            exchange_tiles(lambda t: lax.dynamic_slice_in_dim(s_down, t * out_width, out_width, 1))
        ).astype(F32)
        grad_w_gu = jnp.concatenate(
            [got[s][:, ff_own * g : ff_own * (g + 1)] for g in range(gu_cols // ff_own) for s in range(4)],
            axis=1,
        ).astype(F32)
        units = [s_qkv[:, COLS * p : COLS * (p + 1)] for p in range(3)]

        def choose(options, table):
            result = options[table[0]]
            for t in range(1, 4):
                if table[t] != table[0]:
                    result = jnp.where(tile == t, options[table[t]], result)
            return result

        slots = [
            choose(units, KEPT),
            swap(choose(units, TO_TX), "tx"),
            swap(choose(units, TO_TY), "ty"),
        ]
        grad_w_qkv = jnp.concatenate(
            [choose(slots, [SLOTS[t][k] for t in range(4)]) for k in range(3)], axis=1
        ).astype(F32)

    flips = (jnp.arange(count, dtype=jnp.int32) ^ img).astype(jnp.int32)
    grad_silu = flip_exchange(grad_silu, count, bits[-2::-1])
    grad_silu = reorder(flips, grad_silu).reshape(1, width)
    sigmoid_c = jax.nn.sigmoid(cond_float)
    grad_cond = (grad_silu * sigmoid_c * (1.0 + cond_float * (1.0 - sigmoid_c))).astype(BF16)

    return (
        store["output"].reshape(tokens.shape),
        grad_tokens.reshape(tokens.shape),
        grad_cond,
        grad_w_qkv,
        grad_w_out,
        grad_w_gu,
        grad_down,
        grad_ada,
        gain_back(gain_sums[0, :LANES]),
        gain_back(gain_sums[0, LANES:]),
        grad_bias,
    )


def solution(mesh):
    tiled = P("img", "ty", "tx", None)
    rows = P("img", None)
    cut = P("img", ("ty", "tx"))
    in_specs = (tiled, rows, P("img"), rows, rows, rows, rows, rows, P(), P(), P(), tiled)
    out_specs = (tiled, tiled, rows, cut, cut, cut, cut, cut, P(), P(), P())
    return jax.shard_map(
        functools.partial(body, mesh.shape["img"]),
        mesh=mesh,
        in_specs=in_specs,
        out_specs=out_specs,
        check_vma=False,
    )
```

```python
import functools
import math

import jax
import jax.numpy as jnp
import numpy as np
from jax import lax
from jax.experimental import pallas as pl
from jax.experimental.pallas import tpu as pltpu
from jax.sharding import PartitionSpec as P

HEADS = 16
HEAD = 72
FF = 3072
TILES = 4
OWN = HEADS // TILES
LANES = 128
COLS = OWN * HEAD
PADDED = OWN * LANES
WINDOW = 384
QUARTER = HEAD // 4
EPSILON = 1e-06
LOG2E = math.log2(math.e)
LN2 = math.log(2.0)
BF16 = jnp.bfloat16
F32 = jnp.float32


def head_lane(index):
    part, half, freq = index // 36, (index % 36) // QUARTER, index % QUARTER
    return half * 64 + part * QUARTER + freq


def spread_matrices():
    spread = np.zeros((4, WINDOW, PADDED), np.float32)
    for which in range(4):
        base = (COLS - 256) * which if which < 3 else 0
        for head in range(OWN):
            for index in range(HEAD):
                lane = index if which >= 2 else head_lane(index)
                spread[which, base + HEAD * head + index, LANES * head + lane] = 1.0
    return spread


def dot(left, right):
    return jnp.dot(left, right, preferred_element_type=F32)


def dot_nt(left, right):
    return lax.dot_general(left, right, (((1,), (1,)), ((), ())), preferred_element_type=F32)


def dot_tn(left, right):
    return lax.dot_general(left, right, (((0,), (0,)), ((), ())), preferred_element_type=F32)


def inverse_rms(values):
    return lax.rsqrt(jnp.mean(values * values, axis=-1, keepdims=True) + EPSILON)


def norm_back(grad_out, normed, inv_scale):
    return inv_scale * (grad_out - normed * jnp.mean(grad_out * normed, axis=-1, keepdims=True))


def swap(values, axis):
    return lax.ppermute(values, axis, [(0, 1), (1, 0)])


FLIPS = (2, 3, 0, 1)


def tile_at(flip):
    return (lax.axis_index("ty") ^ (flip >> 1)) * 2 + (lax.axis_index("tx") ^ (flip & 1))


def gather_tiles(values):
    far = swap(values, "ty")
    return [far, swap(far, "tx"), values, swap(values, "tx")]


def sum_tiles(values):
    values = values + swap(values, "tx")
    return values + swap(values, "ty")


def absolute(pieces):
    ty, tx = lax.axis_index("ty"), lax.axis_index("tx")
    turned = [jnp.where(tx == 1, pieces[f ^ 1], pieces[f]) for f in range(4)]
    return [jnp.where(ty == 1, turned[f ^ 2], turned[f]) for f in range(4)]


def exchange_tiles(piece_for):
    across = [(a * 2 + b, (1 - a) * 2 + 1 - b) for a in range(2) for b in range(2)]
    return absolute(
        [
            piece_for(tile_at(0)),
            swap(piece_for(tile_at(1)), "tx"),
            swap(piece_for(tile_at(2)), "ty"),
            lax.ppermute(piece_for(tile_at(3)), ("ty", "tx"), across),
        ]
    )


def flip_perm(count, bit):
    return [(i, i ^ bit) for i in range(count)]


def flip_exchange(values, count, bits):
    rows = [values[k : k + 1] for k in range(count)]
    for bit in bits:
        sent = jnp.concatenate([rows[k] for k in range(count) if k & bit])
        got = lax.ppermute(sent, "img", flip_perm(count, bit))
        moved = [k for k in range(count) if k & bit]
        for place, k in enumerate(moved):
            rows[k] = got[place : place + 1]
    return jnp.concatenate(rows)


def ring_perm(count, step):
    order = list(range(0, count, 2)) + list(range(count - 1, 0, -2))
    return [(order[i], order[(i + step) % count]) for i in range(count)]


def ring_place(count):
    index = lax.axis_index("img")
    return jnp.where(index % 2 == 0, index // 2, count - 1 - index // 2)


def ring_owner(count, place):
    place = (place + count) % count
    return jnp.where(place < count // 2, 2 * place, 2 * (count - 1 - place) + 1)


def use_ring(count, rows):
    return 2 < count <= 16 and count % 2 == 0 and rows % 16 == 0


def split_rows(rows):
    return (rows // 2 + 15) // 16 * 16


def out_share(pick, first):
    return dot_nt(pick, first[:, first.shape[1] - WINDOW :]).astype(BF16)


def ring_gather(own, count, beside):
    cut = split_rows(own.shape[0])
    a, b = own[:cut], own[cut:]
    pieces, value = [], None
    for hop in range(count - 1):
        a = lax.ppermute(a, "img", ring_perm(count, 1))
        b = lax.ppermute(b, "img", ring_perm(count, -1))
        if hop < len(beside):
            value = beside[hop](value)
            a, b, value = lax.optimization_barrier((a, b, value))
        pieces.append((a, b))
    for step in beside[count - 1 :]:
        value = step(value)
    return pieces, value


def assemble_kernel(count, total, plan, shared, index_ref, pick_ref, *refs):
    cut = split_rows(total)
    own, pieces_a, pieces_b = refs[0], refs[1:count], refs[count : 2 * count - 1]
    outs, sems = refs[2 * count - 1 : -1], refs[-1]
    started = []
    for k, (src, first, size) in enumerate(
        [(own, 0, total)]
        + [(piece, 0, cut) for piece in pieces_a]
        + [(piece, cut, total - cut) for piece in pieces_b]
    ):
        for out, rows, base, count_rows, to_row, from_lane, to_lane, lanes in plan:
            low, high = max(first, base), min(first + size, base + count_rows)
            if low < high:
                start = pl.multiple_of(index_ref[k] * rows + to_row + low - base, 16)
                copy = pltpu.make_async_copy(
                    src.at[pl.ds(low - first, high - low), pl.ds(from_lane, lanes)],
                    outs[out].at[pl.ds(start, high - low), pl.ds(to_lane, lanes)],
                    sems.at[len(started)],
                )
                copy.start()
                started.append(copy)
    for copy in started:
        copy.wait()
    if shared:
        outs[-1][...] = out_share(pick_ref[...], outs[0])


def assemble(own, pieces, shapes, plan, count, shared):
    place = ring_place(count)
    steps = jnp.asarray([0] + [-k for k in range(1, count)] + list(range(1, count)), jnp.int32)
    index = ring_owner(count, place + steps).astype(jnp.int32)
    copies = 2 * count - 1
    shapes = [jax.ShapeDtypeStruct(shape, own.dtype) for shape in shapes]
    return pl.pallas_call(
        functools.partial(assemble_kernel, count, own.shape[0], plan, shared),
        out_shape=shapes,
        in_specs=[smem(), vmem()] + [pl.BlockSpec(memory_space=pltpu.HBM)] * copies,
        out_specs=[vmem() for _ in shapes],
        scratch_shapes=[pltpu.SemaphoreType.DMA((2 * len(plan) * copies,))],
        compiler_params=limit(58),
        cost_estimate=cost(5),
        name="assemble_first" if shared else "assemble_gu",
    )(index, out_pick(), own, *[a for a, _ in pieces], *[b for _, b in pieces])


def out_pick():
    pick = np.zeros((COLS, WINDOW), np.float32)
    pick[np.arange(COLS), WINDOW - COLS + np.arange(COLS)] = 1.0
    return jnp.asarray(pick, BF16)


def after(value, *others):
    return lax.optimization_barrier((value, others))[0]


def ring_scatter(grads, count, beside):
    sizes = [grad.shape[0] // count for grad in grads]
    total = sum(sizes)
    cut = split_rows(total)
    place = ring_place(count)
    value = None

    def part(sign, step):
        owner = ring_owner(count, place - sign * step)
        first, last = (0, cut) if sign > 0 else (cut, total)
        found, base = [], 0
        for grad, rows in zip(grads, sizes):
            low, high = max(first, base), min(last, base + rows)
            if low < high:
                found.append(lax.dynamic_slice_in_dim(grad, owner * rows + low - base, high - low, 0))
            base += rows
        return jnp.concatenate(found)

    sums = [part(1, 1), part(-1, 1)]
    for step in range(2, count + 1):
        kind = BF16 if step < count else F32
        got = [lax.ppermute(sums[k], "img", ring_perm(count, sign)) for k, sign in enumerate((1, -1))]
        if step - 2 < len(beside) and beside[step - 2]:
            value = beside[step - 2](value)
            got, value = lax.optimization_barrier((got, value))
        for k, sign in enumerate((1, -1)):
            sums[k] = (got[k].astype(F32) + part(sign, step).astype(F32)).astype(kind)
    for step in beside[count - 1 :]:
        value = step(value)
    return sums, value


def vmem():
    return pl.BlockSpec(memory_space=pltpu.VMEM)


def limit(megabytes):
    return pltpu.CompilerParams(vmem_limit_bytes=megabytes * 1024 * 1024)


def cost(microseconds):
    return pl.CostEstimate(
        flops=int(microseconds * 1.1e9), bytes_accessed=int(microseconds * 3e6), transcendentals=0
    )


def hbm():
    return pl.BlockSpec(memory_space=pltpu.HBM)


def lane_ids(rows):
    return lax.broadcasted_iota(jnp.int32, (rows, LANES), 1)


def three_parts(column):
    high = column.astype(BF16)
    rest = column - high.astype(F32)
    mid = rest.astype(BF16)
    return high, mid, (rest - mid.astype(F32)).astype(BF16)


def head_sums(values):
    lanes = values.shape[1]
    row = lax.broadcasted_iota(jnp.int32, (PAIR, PAIR), 0) // LANES
    col = lax.broadcasted_iota(jnp.int32, (PAIR, PAIR), 1) // LANES
    ones = jnp.where(row == col, 1.0, 0.0).astype(BF16)
    high = values.astype(BF16)
    rest = (values - high.astype(F32)).astype(BF16)
    return jnp.concatenate(
        [
            dot(high[:, at : at + PAIR], ones) + dot(rest[:, at : at + PAIR], ones)
            for at in range(0, lanes, PAIR)
        ],
        axis=1,
    )


def put_lanes(values, first, parts):
    lanes = lane_ids(values.shape[0])
    for k, part in enumerate(parts):
        values = jnp.where(lanes == first + k, part.astype(values.dtype), values)
    return values


QK_SPARE = 100
V_SPARE = HEAD


PAIRS = OWN // 2
PAIR = 2 * LANES
PAIR_COLS = 2 * HEAD


def project_kernel(
    x0_ref, x1_ref, x2_ref, x3_ref, mod_ref, w_ref, cos_ref, sin_ref, gq_ref, gk_ref, spread_ref,
    attn_ref, qraw_ref, kraw_ref, q0_ref, q1_ref, k0_ref, k1_ref, v0_ref, v1_ref, wpad_ref,
):
    block = x0_ref.shape[0]
    tokens = 4 * block
    factor = LOG2E / math.sqrt(HEAD)

    for place, x_ref in enumerate((x0_ref, x1_ref, x2_ref, x3_ref)):
        x = x_ref[...].astype(F32)
        normed = x * inverse_rms(x)
        attn_ref[block * place : block * (place + 1), :] = (
            normed * (1.0 + mod_ref[1:2, :]) + mod_ref[0:1, :]
        ).astype(BF16)

    @pl.loop(0, w_ref.shape[0] // 128)
    def _(i):
        rows = pl.ds(pl.multiple_of(i * 128, 128), 128)
        for w in range(3):
            wpad_ref[rows, PADDED * w : PADDED * (w + 1)] = dot(
                w_ref[rows, 256 * w : 256 * w + WINDOW], spread_ref[w]
            ).astype(BF16)

    @pl.loop(0, tokens // block)
    def _(i):
        rows = pl.ds(pl.multiple_of(i * block, block), block)
        attn_in = attn_ref[rows, :]
        cos, sin = cos_ref[rows, :], sin_ref[rows, :]
        lanes = lane_ids(block)
        spare = (lanes >= QK_SPARE) & (lanes < QK_SPARE + 3)
        for which, raw_ref, out_refs, gain_ref in (
            (0, qraw_ref, (q0_ref, q1_ref), gq_ref),
            (1, kraw_ref, (k0_ref, k1_ref), gk_ref),
        ):
            raw = dot(attn_in, wpad_ref[:, PADDED * which : PADDED * (which + 1)])
            raw_ref[rows, :] = raw
            for head in range(OWN):
                part = raw[:, LANES * head : LANES * (head + 1)]
                inv = lax.rsqrt(jnp.sum(part * part, axis=-1, keepdims=True) / HEAD + EPSILON)
                scaled = part * inv * gain_ref[...]
                turned = scaled * cos + pltpu.roll(scaled, 64, 1) * sin
                turned = turned * factor if which == 0 else jnp.where(spare, 1.0, turned)
                at = slice(LANES * (head % 2), LANES * (head % 2 + 1))
                out_refs[head // 2][rows, at] = turned.astype(BF16)
        value = dot(attn_in, wpad_ref[:, PADDED * 2 : PADDED * 3])
        ones = (lanes >= V_SPARE) & (lanes < V_SPARE + 3)
        for head in range(OWN):
            at = slice(LANES * (head % 2), LANES * (head % 2 + 1))
            part = value[:, LANES * head : LANES * (head + 1)]
            (v0_ref, v1_ref)[head // 2][rows, at] = jnp.where(ones, 1.0, part).astype(BF16)


def project(x_tiles, mod, w, cos, sin, gq, gk, spread):
    width = w.shape[0]
    tokens = cos.shape[0]
    return pl.pallas_call(
        project_kernel,
        out_shape=[
            jax.ShapeDtypeStruct((tokens, width), BF16),
            jax.ShapeDtypeStruct((tokens, PADDED), F32),
            jax.ShapeDtypeStruct((tokens, PADDED), F32),
        ]
        + [jax.ShapeDtypeStruct((tokens, PAIR), BF16)] * 6,
        in_specs=[vmem()] * 11,
        out_specs=[vmem()] * 9,
        scratch_shapes=[pltpu.VMEM((width, 3 * PADDED), BF16)],
        cost_estimate=cost(16),
        compiler_params=limit(34),
        name="project",
    )(*x_tiles, mod, w, cos, sin, gq, gk, spread)


def attend_kernel(qin_ref, k_ref, v_ref, spread_ref, q_ref, mixedp_ref, mixed_ref):
    tokens = qin_ref.shape[0]
    block = 256
    for i in range(tokens // block):
        rows = slice(block * i, block * (i + 1))
        for head in range(2):
            at = slice(LANES * head, LANES * (head + 1))
            query = qin_ref[rows, at]
            terms = jnp.exp2(dot_nt(query, k_ref[:, at])).astype(BF16)
            result = dot(terms, v_ref[:, at])
            total = result[:, V_SPARE : V_SPARE + 1]
            mixedp_ref[rows, at] = (result * (1.0 / total)).astype(BF16)
            q_ref[rows, at] = put_lanes(query, QK_SPARE, three_parts(-jnp.log2(total)))
        mixed_ref[:, rows] = dot_nt(spread_ref[3, :PAIR_COLS, :PAIR], mixedp_ref[rows, :]).astype(BF16)


def attend(q, k, v, spread):
    tokens = q.shape[0]
    return pl.pallas_call(
        attend_kernel,
        out_shape=[
            jax.ShapeDtypeStruct((tokens, PAIR), BF16),
            jax.ShapeDtypeStruct((tokens, PAIR), BF16),
            jax.ShapeDtypeStruct((PAIR_COLS, tokens), BF16),
        ],
        in_specs=[vmem()] * 4,
        out_specs=[vmem()] * 3,
        cost_estimate=cost(4.1),
        compiler_params=limit(20),
        name="attend",
    )(q, k, v, spread)


def attention_back_kernel(
    g0_ref, g1_ref, g2_ref, g3_ref, wout_ref, qraw_ref, kraw_ref, q0_ref, q1_ref, k0_ref, k1_ref, v0_ref, v1_ref,
    m0_ref, m1_ref, cos_ref, sin_ref, gq_ref, gk_ref, spread_ref, out_ref, gains_ref, do_ref, dq_ref, dk_ref, pad_ref,
    *scratch
):
    sems = scratch[-1]
    late = (q0_ref, k0_ref, v0_ref, q1_ref, k1_ref, v1_ref, cos_ref, sin_ref, qraw_ref, kraw_ref)
    copies = [pltpu.make_async_copy(src, dst, sems.at[n]) for n, (src, dst) in enumerate(zip(late, scratch))]
    for copy in copies:
        copy.start()
    q0_ref, k0_ref, v0_ref, q1_ref, k1_ref, v1_ref, cos_ref, sin_ref, qraw_ref, kraw_ref = scratch[:-1]
    block = g0_ref.shape[0]
    tokens = 4 * block
    root = 1.0 / math.sqrt(HEAD)

    for place, g_ref in enumerate((g0_ref, g1_ref, g2_ref, g3_ref)):
        rows = slice(block * place, block * (place + 1))
        grad_mixed = dot(g_ref[...], wout_ref[...]).astype(BF16)
        wide = dot(grad_mixed, spread_ref[3, :COLS, :])
        mixed = jnp.concatenate([m0_ref[rows, :], m1_ref[rows, :]], axis=1).astype(F32)
        row_dot = head_sums(wide * mixed)
        for head in range(OWN):
            at = slice(LANES * head, LANES * (head + 1))
            do_ref[rows, at] = put_lanes(wide[:, at].astype(BF16), V_SPARE, three_parts(-row_dot[:, at]))

    for head in range(OWN):
        at = slice(LANES * head, LANES * (head + 1))
        pair_at = slice(LANES * (head % 2), LANES * (head % 2 + 1))
        q_ref, k_ref, v_ref = ((q0_ref, k0_ref, v0_ref), (q1_ref, k1_ref, v1_ref))[head // 2]
        if head % 2 == 0:
            for copy in copies[3 * (head // 2) : 3 * (head // 2) + 3]:
                copy.wait()
        dq_ref[at, :] = jnp.zeros((LANES, tokens), F32)

        for i in range(tokens // block):
            rows = slice(block * i, block * (i + 1))
            query, grad = q_ref[:, pair_at], do_ref[:, at]
            key = k_ref[rows, pair_at]
            probs = jnp.exp2(dot_nt(key, query))
            slope = (probs * dot_nt(v_ref[rows, pair_at], grad)).astype(BF16)
            pad_ref[rows, 2 * PADDED + LANES * head : 2 * PADDED + LANES * (head + 1)] = dot(
                probs.astype(BF16), grad
            ).astype(BF16)
            dk_ref[rows, at] = dot(slope, query) * LN2
            dq_ref[at, :] += dot(key.astype(F32).T.astype(BF16), slope)

    for copy in copies[6:]:
        copy.wait()
    gains_ref[...] = jnp.zeros_like(gains_ref)

    @pl.loop(0, tokens // block)
    def _(i):
        rows = pl.ds(pl.multiple_of(i * block, block), block)
        cos, sin = cos_ref[rows, :], sin_ref[rows, :]
        for which, raw_ref, gain_ref in ((0, qraw_ref, gq_ref), (1, kraw_ref, gk_ref)):
            raw = raw_ref[rows, :]
            inv = lax.rsqrt(head_sums(raw * raw) / HEAD + EPSILON)
            hat = raw * inv
            turned = []
            for head in range(OWN):
                at = slice(LANES * head, LANES * (head + 1))
                grad = dq_ref[at, rows].T * root if which == 0 else dk_ref[rows, at]
                turned.append(grad * cos - pltpu.roll(grad, 64, 1) * sin)
            gain = jnp.concatenate([gain_ref[...]] * OWN, axis=1)
            product = jnp.concatenate(turned, axis=1) * hat
            gained = jnp.sum(product, axis=0, keepdims=True)
            gains_ref[which : which + 1, :] += sum(
                gained[:, LANES * head : LANES * (head + 1)] for head in range(OWN)
            )
            mean = head_sums(product * gain) / HEAD
            pad_ref[rows, PADDED * which : PADDED * (which + 1)] = (
                inv * (jnp.concatenate(turned, axis=1) * gain - hat * mean)
            ).astype(BF16)
        compact = [
            dot_nt(pad_ref[rows, PADDED * w : PADDED * (w + 1)], spread_ref[w]).astype(BF16)
            for w in range(3)
        ]
        out_ref[rows, :] = jnp.concatenate(
            [
                compact[0][:, :256],
                compact[0][:, 256:] + compact[1][:, :128],
                compact[1][:, 128:256],
                compact[1][:, 256:] + compact[2][:, :128],
                compact[2][:, 128:],
            ],
            axis=1,
        )[:, : 3 * COLS]


def attention_backward(grads, w_rows, qraw, kraw, q, k, v, mixedp, cos, sin, gq, gk, spread):
    tokens = cos.shape[0]
    return pl.pallas_call(
        attention_back_kernel,
        out_shape=[
            jax.ShapeDtypeStruct((tokens, 3 * COLS), BF16),
            jax.ShapeDtypeStruct((8, LANES), F32),
        ],
        in_specs=[vmem()] * 5 + [hbm()] * 8 + [vmem()] * 2 + [hbm()] * 2 + [vmem()] * 3,
        out_specs=[vmem()] * 2,
        scratch_shapes=[
            pltpu.VMEM((tokens, PADDED), BF16),
            pltpu.VMEM((PADDED, tokens), F32),
            pltpu.VMEM((tokens, PADDED), F32),
            pltpu.VMEM((tokens, 3 * PADDED), BF16),
        ]
        + [pltpu.VMEM((tokens, PAIR), BF16)] * 6
        + [pltpu.VMEM((tokens, LANES), F32)] * 2
        + [pltpu.VMEM((tokens, PADDED), F32)] * 2
        + [pltpu.SemaphoreType.DMA((10,))],
        cost_estimate=cost(K5_COST),
        compiler_params=limit(58),
        name="attention_backward",
    )(*grads, w_rows, qraw, kraw, *q, *k, *v, *mixedp, cos, sin, gq, gk, spread)


def smem():
    return pl.BlockSpec(memory_space=pltpu.SMEM)


def out_weight_kernel(tile_ref, p0_ref, p1_ref, p2_ref, p3_ref, out_ref, own_ref):
    for place, piece in enumerate((p0_ref, p1_ref, p2_ref, p3_ref)):
        start = pl.multiple_of((tile_ref[0] ^ FLIPS[place]) * COLS, 16)
        out_ref[pl.ds(start, COLS), :] = piece[...]
    for tile in range(4):

        @pl.when(tile_ref[0] == tile)
        def _(tile=tile):
            own_ref[...] = out_ref[:, COLS * tile : COLS * (tile + 1)]


def out_weight(tile, pieces):
    width = pieces[0].shape[1]
    return pl.pallas_call(
        out_weight_kernel,
        out_shape=[
            jax.ShapeDtypeStruct((width, width), BF16),
            jax.ShapeDtypeStruct((width, COLS), BF16),
        ],
        in_specs=[smem()] + [vmem()] * 4,
        out_specs=[vmem()] * 2,
        cost_estimate=cost(3.8),
        compiler_params=limit(12),
        name="out_weight",
    )(tile, *pieces)


def residual_kernel(tile_ref, mod_ref, wout_ref, *refs):
    x_refs, mixed_refs = refs[:4], refs[4 : 4 + 4 * PAIRS]
    mlp_ref, attended_ref, mixed_ref = refs[4 + 4 * PAIRS :]
    block = x_refs[0].shape[0]
    for k, m_ref in enumerate(mixed_refs):
        pair, source = k // 4, k % 4
        start = pl.multiple_of((tile_ref[0] ^ FLIPS[source]) * COLS + PAIR_COLS * pair, 16)
        for place in range(4):
            at = block * (place ^ FLIPS[source])
            mixed_ref[pl.ds(start, PAIR_COLS), block * place : block * (place + 1)] = m_ref[:, at : at + block]
    for place, x_ref in enumerate(x_refs):
        here = slice(block * place, block * (place + 1))
        attended = lax.dot_general(
            mixed_ref[:, here], wout_ref[...], (((0,), (1,)), ((), ())), preferred_element_type=F32
        )
        if place == 2:
            attended_ref[...] = attended
        x_mid = x_ref[...].astype(F32) + mod_ref[2:3, :] * attended
        normed = x_mid * inverse_rms(x_mid)
        mlp_ref[here, :] = (normed * (1.0 + mod_ref[4:5, :]) + mod_ref[3:4, :]).astype(BF16)


def branch_kernel(mod_ref, dy0_ref, dy1_ref, dy2_ref, dy3_ref, out_ref):
    block = dy0_ref.shape[0]
    for place, dy_ref in enumerate((dy0_ref, dy1_ref, dy2_ref, dy3_ref)):
        out_ref[block * place : block * (place + 1), :] = (
            mod_ref[5:6, :] * (mod_ref[6:7, :] * dy_ref[...].astype(F32))
        ).astype(BF16)


def branch_grad(mod, dy_tiles):
    block, width = dy_tiles[0].shape
    return pl.pallas_call(
        branch_kernel,
        out_shape=jax.ShapeDtypeStruct((4 * block, width), BF16),
        in_specs=[vmem()] * 5,
        out_specs=vmem(),
        compiler_params=limit(12),
        cost_estimate=cost(3),
        name="branch_grad",
    )(mod, *dy_tiles)


def residual(tile, mod, w_out, x_tiles, mixed):
    block, width = x_tiles[0].shape
    return pl.pallas_call(
        residual_kernel,
        out_shape=[
            jax.ShapeDtypeStruct((4 * block, width), BF16),
            jax.ShapeDtypeStruct((block, width), F32),
        ],
        in_specs=[smem()] + [vmem()] * (6 + 4 * PAIRS),
        out_specs=[vmem()] * 2,
        scratch_shapes=[pltpu.VMEM((width, 4 * block), BF16)],
        compiler_params=limit(58),
        cost_estimate=cost(9),
        name="residual",
    )(tile, mod, w_out, *x_tiles, *mixed)


def mlp_kernel(places, wgu_ref, wdown_ref, in_ref, gbranch_ref, *refs):
    number = len(places)
    refs = refs[-(2 + 2 * number) :]
    hidden_ref, ggu_ref, branch_refs, gmlp_refs = refs[0], refs[1], refs[2 : 2 + number], refs[2 + number :]
    block = branch_refs[0].shape[0]
    half = wgu_ref.shape[1] // 2
    for place, branch_ref, gmlp_ref in zip(places, branch_refs, gmlp_refs):
        here = slice(0, block) if number == 1 else slice(block * place, block * (place + 1))
        mlp_in, grad_branch = in_ref[here, :], gbranch_ref[here, :]
        gate = dot(mlp_in, wgu_ref[:, :half])
        up = dot(mlp_in, wgu_ref[:, half:])
        grad_hidden = dot_nt(grad_branch, wdown_ref[...])
        sigmoid = jax.nn.sigmoid(gate)
        silu = gate * sigmoid
        hidden = (silu * up).astype(BF16)
        hidden_ref[here, :] = hidden
        branch_ref[...] = dot(hidden, wdown_ref[...]).astype(BF16)
        grad_gate = (grad_hidden * up * (sigmoid * (1.0 + gate * (1.0 - sigmoid)))).astype(BF16)
        grad_up = (grad_hidden * silu).astype(BF16)
        ggu_ref[here, :half] = grad_gate
        ggu_ref[here, half:] = grad_up
        gmlp_ref[...] = (
            dot_nt(grad_gate, wgu_ref[:, :half]) + dot_nt(grad_up, wgu_ref[:, half:])
        ).astype(BF16)


def mlp(places, w_gu, w_down, mlp_in, grad_branch, kept):
    number = len(places)
    tokens, width = mlp_in.shape
    block = tokens // 4
    hidden = w_down.shape[0]
    one = pl.Buffered(1)
    if number == 1:
        row_block = lambda cols: pl.BlockSpec((block, cols), lambda i: (places[0], 0), pipeline_mode=one)
    else:
        row_block = lambda cols: pl.BlockSpec((4 * block, cols), lambda i: (0, 0), pipeline_mode=one)
    whole = lambda rows, cols: pl.BlockSpec((rows, cols), lambda i: (0, 0), pipeline_mode=one)
    args = [w_gu, w_down, mlp_in, grad_branch, *kept]
    shapes = [(tokens, hidden), (tokens, 2 * hidden)]
    return pl.pallas_call(
        functools.partial(mlp_kernel, places),
        grid=(1,),
        out_shape=[jax.ShapeDtypeStruct(shape, BF16) for shape in shapes]
        + [jax.ShapeDtypeStruct((block, width), BF16)] * (2 * number),
        in_specs=[whole(*w_gu.shape), whole(*w_down.shape), row_block(width), row_block(width)]
        + [hbm()] * len(kept),
        out_specs=[row_block(shape[1]) for shape in shapes] + [whole(block, width)] * (2 * number),
        input_output_aliases={4 + k: k for k in range(len(kept))},
        compiler_params=limit(58),
        cost_estimate=cost(12 if number == 2 else 0.3),
        name="mlp",
    )(*args)


def middle_kernel(a_ref, b_ref, c_ref, attended_ref, x_ref, dy_ref, mod_ref, gatt_ref, gmid_ref, sums_ref):
    grad_in = a_ref[...].astype(F32) + b_ref[...].astype(F32) + c_ref[...].astype(F32)
    attended = attended_ref[...]
    x_mid = x_ref[...].astype(F32) + mod_ref[2:3, :] * attended
    inv = inverse_rms(x_mid)
    normed = x_mid * inv
    product = grad_in * normed
    grad_mid = mod_ref[6:7, :] * dy_ref[...].astype(F32) + inv * (
        grad_in * (1.0 + mod_ref[4:5, :])
        - normed * jnp.mean(product * (1.0 + mod_ref[4:5, :]), axis=-1, keepdims=True)
    )
    gmid_ref[...] = grad_mid
    gatt_ref[...] = (mod_ref[2:3, :] * grad_mid).astype(BF16)
    sums_ref[...] = jnp.zeros_like(sums_ref)
    sums_ref[0:1, :] = jnp.sum(grad_mid * attended, axis=0, keepdims=True)
    sums_ref[1:2, :] = jnp.sum(grad_in, axis=0, keepdims=True)
    sums_ref[2:3, :] = jnp.sum(product, axis=0, keepdims=True)


def middle(parts, attended, x, dy, mod):
    block, width = x.shape
    return pl.pallas_call(
        middle_kernel,
        out_shape=[
            jax.ShapeDtypeStruct((block, width), BF16),
            jax.ShapeDtypeStruct((block, width), F32),
            jax.ShapeDtypeStruct((8, width), F32),
        ],
        in_specs=[vmem()] * 7,
        out_specs=[vmem()] * 3,
        cost_estimate=cost(4.6),
        compiler_params=limit(14),
        name="middle",
    )(*parts, attended, x, dy, mod)


def output_kernel(a_ref, b_ref, c_ref, attended_ref, x_ref, dy_ref, mod_ref, out_ref, sums_ref):
    branch = a_ref[...].astype(F32) + b_ref[...].astype(F32) + c_ref[...].astype(F32)
    x_mid = x_ref[...].astype(F32) + mod_ref[2:3, :] * attended_ref[...]
    live = mod_ref[6:7, :]
    out_ref[...] = (live * (x_mid + mod_ref[5:6, :] * branch)).astype(BF16)
    sums_ref[...] = jnp.zeros_like(sums_ref)
    sums_ref[0:1, :] = jnp.sum(live * dy_ref[...].astype(F32) * branch, axis=0, keepdims=True)


def output_tile(parts, attended, x, dy, mod):
    block, width = x.shape
    return pl.pallas_call(
        output_kernel,
        out_shape=[
            jax.ShapeDtypeStruct((block, width), BF16),
            jax.ShapeDtypeStruct((8, width), F32),
        ],
        in_specs=[vmem()] * 7,
        out_specs=[vmem()] * 2,
        cost_estimate=cost(3.5),
        compiler_params=limit(12),
        name="output_tile",
    )(*parts, attended, x, dy, mod)


def tokens_kernel(a_ref, b_ref, c_ref, x_ref, gmid_ref, mod_ref, out_ref, sums_ref):
    grad_in = a_ref[...].astype(F32) + b_ref[...].astype(F32) + c_ref[...].astype(F32)
    x = x_ref[...].astype(F32)
    inv = inverse_rms(x)
    normed = x * inv
    product = grad_in * normed
    scale = 1.0 + mod_ref[1:2, :]
    out_ref[...] = (
        gmid_ref[...] + inv * (grad_in * scale - normed * jnp.mean(product * scale, axis=-1, keepdims=True))
    ).astype(BF16)
    sums_ref[...] = jnp.zeros_like(sums_ref)
    sums_ref[0:1, :] = jnp.sum(grad_in, axis=0, keepdims=True)
    sums_ref[1:2, :] = jnp.sum(product, axis=0, keepdims=True)


def tokens_back(parts, x, grad_mid, mod):
    block, width = x.shape
    return pl.pallas_call(
        tokens_kernel,
        out_shape=[
            jax.ShapeDtypeStruct((block, width), BF16),
            jax.ShapeDtypeStruct((8, width), F32),
        ],
        in_specs=[vmem()] * 6,
        out_specs=[vmem()] * 2,
        cost_estimate=cost(3.6),
        compiler_params=limit(14),
        name="tokens_back",
    )(*parts, x, grad_mid, mod)


def first_grad_kernel(tile_ref, g0_ref, g1_ref, g2_ref, g3_ref, *refs):
    mixed_refs, (attn_ref, qkv_ref, out_ref, cols_ref) = refs[: 4 * PAIRS], refs[4 * PAIRS :]
    block = g0_ref.shape[0]
    wide = qkv_ref.shape[1]
    for tile in range(4):

        @pl.when(tile_ref[0] == tile)
        def _(tile=tile):
            for place, g_ref in enumerate((g0_ref, g1_ref, g2_ref, g3_ref)):
                cols_ref[block * place : block * (place + 1), :] = g_ref[:, COLS * tile : COLS * (tile + 1)]

    for k in range(attn_ref.shape[1] // LANES):
        at = slice(LANES * k, LANES * (k + 1))
        out_ref[at, :wide] = dot_tn(attn_ref[:, at], qkv_ref[...]).astype(BF16)
    for k, m_ref in enumerate(mixed_refs):
        pair, source = k // 4, k % 4
        total = None
        for place in range(4):
            at = block * (place ^ FLIPS[source])
            term = dot(m_ref[:, at : at + block], cols_ref[block * place : block * (place + 1), :])
            total = term if total is None else total + term
        start = pl.multiple_of((tile_ref[0] ^ FLIPS[source]) * COLS + PAIR_COLS * pair, 16)
        out_ref[pl.ds(start, PAIR_COLS), wide:] = total.astype(BF16)


def first_grad(tile, grads, mixed, attn_in, grad_qkv):
    width = attn_in.shape[1]
    return pl.pallas_call(
        first_grad_kernel,
        out_shape=jax.ShapeDtypeStruct((width, grad_qkv.shape[1] + COLS), BF16),
        in_specs=[smem()] + [vmem()] * (6 + 4 * PAIRS),
        out_specs=vmem(),
        scratch_shapes=[pltpu.VMEM((grad_qkv.shape[0], COLS), BF16)],
        compiler_params=limit(58),
        cost_estimate=cost(FIRST_COST),
        name="first_grad",
    )(tile, *grads, *mixed, attn_in, grad_qkv)


def weight_grad_kernel(left_ref, right_ref, out_ref):
    for k in range(left_ref.shape[1] // LANES):
        at = slice(LANES * k, LANES * (k + 1))
        out_ref[at, :] = dot_tn(left_ref[:, at], right_ref[...]).astype(BF16)


def weight_grad(left, right, microseconds):
    return pl.pallas_call(
        weight_grad_kernel,
        out_shape=jax.ShapeDtypeStruct((left.shape[1], right.shape[1]), BF16),
        in_specs=[vmem()] * 2,
        out_specs=vmem(),
        compiler_params=limit(24),
        cost_estimate=cost(microseconds),
        name="weight_grad",
    )(left, right)


GU_AFTER = 5
K5_COST = 1
GU_BY = 3
TIE_BY = 1
FIRST_COST = 1
TO_TX = (1, 0, 2, 1)
TO_TY = (2, 2, 0, 0)
KEPT = (0, 1, 1, 2)
SLOTS = ((0, 1, 2), (2, 1, 0), (0, 1, 2), (2, 1, 0))


def pack_kernel(shard, ff_own, tile_ref, a_ref, b_ref, tx_ref, ty_ref, down_ref, unit_ref, out_ref):
    cut = a_ref.shape[0]

    def rows(first, last, lanes):
        pieces = []
        if first < cut:
            pieces.append(a_ref[first : min(last, cut), lanes])
        if last > cut:
            pieces.append(b_ref[max(first, cut) - cut : last - cut, lanes])
        return pieces[0] if len(pieces) == 1 else jnp.concatenate(pieces)

    def down(tile):
        return rows(shard, shard + ff_own, slice(COLS * tile, COLS * (tile + 1)))

    def unit(part):
        return rows(0, shard, slice(COLS * part, COLS * (part + 1)))

    out_ref[...] = unit(3)
    for tile in range(4):

        @pl.when(tile_ref[0] == tile)
        def _(tile=tile):
            for ref, pieces in (
                (tx_ref, (down(tile ^ 1), down(tile ^ 3), unit(TO_TX[tile]))),
                (ty_ref, (down(tile ^ 2), unit(TO_TY[tile]))),
            ):
                at = 0
                for piece in pieces:
                    ref[at : at + piece.shape[0], :COLS] = piece.astype(BF16)
                    at += piece.shape[0]
            down_ref[...] = down(tile)
            unit_ref[...] = unit(KEPT[tile])


def pack(tile, sums, shard, ff_own):
    return pl.pallas_call(
        functools.partial(pack_kernel, shard, ff_own),
        out_shape=[
            jax.ShapeDtypeStruct((shard + 2 * ff_own, WINDOW), BF16),
            jax.ShapeDtypeStruct((shard + ff_own, WINDOW), BF16),
            jax.ShapeDtypeStruct((ff_own, COLS), F32),
            jax.ShapeDtypeStruct((shard, COLS), F32),
            jax.ShapeDtypeStruct((shard, COLS), F32),
        ],
        in_specs=[smem()] + [vmem()] * 2,
        out_specs=[vmem()] * 5,
        compiler_params=limit(12),
        cost_estimate=cost(2),
        name="pack",
    )(tile, *sums)


def unpack_kernel(
    shard, ff_own, tile_ref, tx_ref, ty_ref, on_ref, down_ref, unit_ref, sgu_ref, gutx_ref, guty_ref,
    wgu_ref, wdown_ref, wqkv_ref,
):
    share = sgu_ref.shape[1] // 4
    groups = share // ff_own
    gus = [None, gutx_ref[:shard, :], guty_ref[:shard, :], guty_ref[shard:, :]]
    downs = [
        down_ref[...],
        tx_ref[:ff_own, :COLS].astype(F32),
        ty_ref[:ff_own, :COLS].astype(F32),
        on_ref[:, :COLS].astype(F32),
    ]
    units = [unit_ref[...], tx_ref[2 * ff_own :, :COLS].astype(F32), ty_ref[ff_own:, :COLS].astype(F32)]
    for tile in range(4):

        @pl.when(tile_ref[0] == tile)
        def _(tile=tile):
            for source in range(4):
                flip = source ^ tile
                wdown_ref[ff_own * source : ff_own * (source + 1), :] = downs[flip]
                piece = sgu_ref[:, share * tile : share * (tile + 1)] if flip == 0 else gus[flip]
                for group in range(groups):
                    at = share * group + ff_own * source
                    wgu_ref[:, at : at + ff_own] = piece[:, ff_own * group : ff_own * (group + 1)].astype(F32)
            for k in range(3):
                wqkv_ref[:, COLS * k : COLS * (k + 1)] = units[SLOTS[tile][k]]


def unpack(tile, from_tx, from_ty, passed_on, kept, gus, shard, ff_own):
    return pl.pallas_call(
        functools.partial(unpack_kernel, shard, ff_own),
        out_shape=[
            jax.ShapeDtypeStruct(gus[0].shape, F32),
            jax.ShapeDtypeStruct((4 * ff_own, COLS), F32),
            jax.ShapeDtypeStruct((shard, 3 * COLS), F32),
        ],
        in_specs=[smem()] + [vmem()] * 8,
        out_specs=[vmem()] * 3,
        compiler_params=limit(12),
        cost_estimate=cost(2),
        name="unpack",
    )(tile, from_tx, from_ty, passed_on, *kept, *gus)


def ada_kernel(tile_ref, mod_ref, w_ref, silu_ref, ada_ref, bias_ref, cond_ref):
    count, wide = mod_ref.shape
    width = w_ref.shape[1]
    share = width // 4
    for tile in range(4):

        @pl.when(tile_ref[0] == tile)
        def _(tile=tile):
            ada_ref[...] = dot_tn(silu_ref[...], mod_ref[:, share * tile : share * (tile + 1)])

    rows = [mod_ref[k : k + 1, :].astype(F32) for k in range(count)]
    while len(rows) > 1:
        rows = [rows[k] + rows[k + 1] for k in range(0, len(rows), 2)]
    bias_ref[...] = rows[0]
    cond_ref[...] = dot_nt(mod_ref[:, :width], w_ref[...])


def ada_back(tile, mod_all, w_ada, silu_rows):
    count, wide = mod_all.shape
    shard, width = w_ada.shape
    return pl.pallas_call(
        ada_kernel,
        out_shape=[
            jax.ShapeDtypeStruct((shard, width // 4), F32),
            jax.ShapeDtypeStruct((1, wide), F32),
            jax.ShapeDtypeStruct((count, shard), F32),
        ],
        in_specs=[smem()] + [vmem()] * 3,
        out_specs=[vmem()] * 3,
        cost_estimate=cost(3.5),
        compiler_params=limit(12),
        name="ada_back",
    )(tile, mod_all, w_ada, silu_rows)


def reorder_kernel(index_ref, rows_ref, out_ref):
    for k in range(rows_ref.shape[0]):
        out_ref[k : k + 1, :] = rows_ref[pl.ds(index_ref[k], 1), :]


def reorder(index, rows):
    return pl.pallas_call(
        reorder_kernel,
        out_shape=jax.ShapeDtypeStruct(rows.shape, rows.dtype),
        in_specs=[smem(), vmem()],
        out_specs=vmem(),
        cost_estimate=cost(1.3),
        compiler_params=limit(4),
        name="reorder",
    )(index, rows)


def lane_matrix():
    matrix = np.zeros((HEAD, LANES), np.float32)
    for index in range(HEAD):
        matrix[index, head_lane(index)] = 1.0
    return matrix


def rope_lanes(tile_rows, tile_cols):
    freqs = (10000.0 ** (-np.arange(QUARTER, dtype=np.float64) / QUARTER)).astype(np.float32)
    freq = np.zeros((LANES,), np.float32)
    part = np.zeros((LANES,), np.int32)
    sign = np.zeros((LANES,), np.float32)
    for index in range(HEAD):
        lane = head_lane(index)
        freq[lane] = freqs[index % QUARTER]
        part[lane] = index // 36
        sign[lane] = 1.0 if lane >= 64 else -1.0
    per_tile = tile_rows * tile_cols
    ids = np.arange(4 * per_tile)
    flips = np.array(FLIPS)[ids // per_tile]
    ty = lax.axis_index("ty") ^ jnp.asarray(flips >> 1, jnp.int32)
    tx = lax.axis_index("tx") ^ jnp.asarray(flips & 1, jnp.int32)
    rows = (ty * tile_rows + jnp.asarray(ids % per_tile // tile_cols, jnp.int32)).astype(F32)
    cols = (tx * tile_cols + jnp.asarray(ids % tile_cols, jnp.int32)).astype(F32)
    angle = jnp.where(jnp.asarray(part)[None] == 0, rows[:, None], cols[:, None]) * jnp.asarray(freq)[None]
    live = jnp.asarray((sign != 0).astype(np.float32))[None]
    return jnp.cos(angle) * live, jnp.sin(angle) * jnp.asarray(sign)[None]


def gain_lanes(gain):
    return jnp.sum(jnp.asarray(lane_matrix()) * gain[:, None], axis=0, keepdims=True)


def gain_back(lanes):
    return jnp.sum(jnp.asarray(lane_matrix()) * lanes[None, :], axis=1)


def tile_pair(far):
    return (far[0].astype(F32) + swap(far[1], "tx").astype(F32)).astype(BF16)


def tile_sum_parts(pair, near):
    return near[0], swap(near[1], "tx"), swap(pair, "ty")


def body(
    count, tokens, cond, live_count, w_qkv, w_out, w_gu, w_down, w_ada, ada_bias, q_gain, k_gain, cotangent
):
    _, tile_rows, tile_cols, width = tokens.shape
    per_tile = tile_rows * tile_cols
    img, ty, tx = lax.axis_index("img"), lax.axis_index("ty"), lax.axis_index("tx")
    tile = ty * 2 + tx
    tile_word = tile[None].astype(jnp.int32)
    live = (live_count[0] > 0).astype(F32)
    shard = width // count
    ff_shard = FF // count
    ff_own = ff_shard // TILES
    hidden_own = FF // TILES
    out_width = width // TILES
    spread = jnp.asarray(spread_matrices(), BF16)

    first = jnp.concatenate(
        [lax.dynamic_slice_in_dim(w_qkv, p * width + tile * COLS, COLS, 1) for p in range(3)]
        + [lax.dynamic_slice_in_dim(w_out, tile * out_width, out_width, 1)],
        axis=1,
    )
    down_own = lax.dynamic_slice_in_dim(w_down, tile * ff_own, ff_own, 0)
    gu_own = lax.dynamic_slice_in_dim(w_gu.reshape(shard, 2 * count, ff_shard), tile * ff_own, ff_own, 2)
    gu_own = gu_own.reshape(shard, 2 * hidden_own)

    x_own = tokens.reshape(per_tile, width)
    dy_own = cotangent.reshape(per_tile, width)
    x_tiles = gather_tiles(x_own)

    cond_float = cond.astype(F32)
    bits = [1 << k for k in range(count.bit_length() - 1)]
    store = {}

    def gather_step(v, bit):
        return jnp.concatenate([v, lax.ppermute(v, "img", flip_perm(count, bit))])

    def scatter_step(v, bit):
        return v[:bit] + lax.ppermute(v[bit:], "img", flip_perm(count, bit))

    silu_some = gather_step(jax.nn.silu(cond_float).astype(BF16), bits[0])

    def rows_step(v):
        store["silu_rows"] = lax.dynamic_slice_in_dim(gather_step(v, bits[-1]), img * shard, shard, 1)
        return store["silu_rows"]

    def dy_step(v):
        store["dy"] = gather_tiles(after(dy_own, v))
        return v

    beside = [lambda _, bit=bit: gather_step(silu_some if _ is None else _, bit) for bit in bits[1:-1]]
    beside += [rows_step, lambda v: scatter_step(dot(v, w_ada), bits[-1])]
    beside += [lambda v, bit=bit: scatter_step(v, bit) for bit in bits[-2::-1]]
    early, middle_step, late = beside[2], beside[3], beside[-1]
    beside[2] = lambda v: after(early(v), x_tiles)
    beside[3] = lambda v: middle_step(dy_step(v))
    beside.append(lambda v: after(v, store["dy"]))

    ring = use_ring(count, math.gcd(shard, ff_own))
    if ring:
        own = after(jnp.concatenate([first, down_own]), silu_some)
        pieces, modulation = ring_gather(own, count, beside)
        full_first, full_down, out_own = assemble(
            own,
            pieces,
            [(width, width), (hidden_own, width), (COLS, width)],
            [(0, shard, 0, shard, 0, 0, 0, width), (1, ff_own, shard, ff_own, 0, 0, 0, width)],
            count,
            True,
        )
        full_gu = lax.all_gather(after(gu_own, pieces[GU_AFTER]), "img", axis=0, tiled=True)
    else:
        full_first, full_down, full_gu = [
            lax.all_gather(a, "img", axis=0, tiled=True) for a in (first, down_own, gu_own)
        ]
        out_own = out_share(out_pick(), full_first)
        modulation = None
        for step in beside:
            modulation = step(modulation)
    silu_rows = store["silu_rows"]
    dy_tiles = store["dy"]
    modulation = modulation + ada_bias
    mod = jnp.concatenate([modulation.reshape(6, width), jnp.broadcast_to(live, (2, width))])

    cos, sin = rope_lanes(tile_rows, tile_cols)
    gq, gk = gain_lanes(q_gain), gain_lanes(k_gain)
    attn_in, qraw, kraw, q0, q1, k0, k1, v0, v1 = project(
        x_tiles, mod, full_first, cos, sin, gq, gk, spread
    )
    out_far = swap(out_own, "ty")
    out_far = after(out_far, attn_in)
    full_out, out_rows = out_weight(
        tile_word, [out_far, swap(out_far, "tx"), out_own, swap(out_own, "tx")]
    )
    q0, mixedp0, mixed0 = attend(q0, k0, v0, spread)
    mixed = gather_tiles(mixed0)
    q1, mixedp1, mixed1 = attend(after(q1, full_out, mixed0), k1, v1, spread)
    mixed += gather_tiles(mixed1)

    grad_branch = branch_grad(mod, after(dy_tiles, mixed1))
    mlp_in, attended = residual(tile_word, mod, full_out, after(x_tiles, grad_branch), mixed)
    weights = (full_gu, full_down, mlp_in, grad_branch)
    far = mlp((1, 0), *weights, ())
    grad_pair = tile_pair((far[5], far[4]))
    grad_far = swap(grad_pair, "ty")
    beside_tile = mlp((3,), *weights, after(far[:2], grad_pair))
    own_tile = mlp((2,), *weights, beside_tile[:2])
    hidden, grad_gu = own_tile[:2]

    grad_att, grad_mid, mid_sums = middle(
        (own_tile[3], swap(beside_tile[3], "tx"), grad_far), attended, x_own, dy_own, mod
    )
    g_gu = weight_grad(mlp_in, after(grad_gu, grad_att), 5)
    g_down = weight_grad(hidden, after(grad_branch, g_gu), 3)
    att_far = after(swap(grad_att, "ty"), g_gu, g_down)
    grad_att_tiles = [att_far, swap(att_far, "tx"), grad_att, swap(grad_att, "tx")]

    grad_qkv, gains = attention_backward(
        grad_att_tiles, out_rows, qraw, kraw, (q0, q1), (k0, k1), (v0, v1), (mixedp0, mixedp1),
        cos, sin, gq, gk, spread,
    )
    branch_parts = tile_sum_parts(tile_pair((far[3], far[2])), (own_tile[2], beside_tile[2]))
    grad_qkv = after(grad_qkv, branch_parts)
    w_back = full_first[:, : 3 * COLS]
    g_first = first_grad(tile_word, grad_att_tiles, mixed, attn_in, grad_qkv)
    back_qkv = after(grad_qkv, g_first)
    back_far = dot_nt(back_qkv[: 2 * per_tile], w_back).astype(BF16)
    halves = lambda rows: (rows[:per_tile], rows[per_tile:])
    back_pair = tile_pair(halves(back_far))
    back_near = dot_nt(after(back_qkv, back_pair)[2 * per_tile :], w_back).astype(BF16)

    wide = 6 * width

    def output_step():
        store["output"], store["out_sums"] = output_tile(
            branch_parts, attended, x_own, dy_own, mod
        )
        return store["out_sums"]

    def token_step():
        parts = tile_sum_parts(back_pair, halves(back_near))
        store["grad_tokens"], tok_sums = tokens_back(parts, x_own, grad_mid, mod)
        return jnp.concatenate(
            [tok_sums[0], tok_sums[1], mid_sums[0], mid_sums[1], mid_sums[2], store["out_sums"][0], gains[0], gains[1]]
        )[None]

    def low_step(grad_mod):
        return jnp.concatenate([grad_mod[:, :wide].astype(BF16), *three_parts(grad_mod[:, wide:])], axis=1)

    def ada_step(mod_all):
        store["grad_ada"], store["sums"], grad_silu = ada_back(tile_word, mod_all, w_ada, silu_rows)
        return grad_silu

    steps = [lambda _: output_step(), lambda _: token_step(), lambda v: low_step(sum_tiles(v))]
    steps += [lambda v, bit=bit: gather_step(v, bit) for bit in bits]
    steps.append(lambda v: flip_exchange(ada_step(v), count, bits[-1:]))

    if ring:
        s_gu = lax.psum_scatter(g_gu, "img", scatter_dimension=0, tiled=True)
        gu_cols = 2 * hidden_own // TILES

        def gu_piece(flip):
            return lax.dynamic_slice_in_dim(s_gu, tile_at(flip) * gu_cols, gu_cols, 1)

        def gu_tx_step(v):
            store["gu_tx"] = swap(jnp.concatenate([gu_piece(1), gu_piece(3)]), "tx")
            return after(v, store["gu_tx"])

        def gu_ty_step(v):
            store["gu_ty"] = swap(jnp.concatenate([gu_piece(2), store["gu_tx"][shard:]]), "ty")
            return after(v, store["gu_ty"])

        tied = steps[TIE_BY]
        steps[TIE_BY] = lambda v: after(tied(v), s_gu)
        first_half, second_half = steps[GU_BY], steps[GU_BY + 1]
        steps[GU_BY] = lambda v: gu_tx_step(first_half(v))
        steps[GU_BY + 1] = lambda v: gu_ty_step(second_half(v))
        s_all, grad_silu = ring_scatter([g_first, g_down], count, steps)
    else:
        grad_silu = None
        for step in steps:
            grad_silu = step(grad_silu) if step else None
    grad_tokens, grad_ada, sums = store["grad_tokens"], store["grad_ada"], store["sums"]
    grad_bias = sums[0, :wide]
    gain_sums = (sums[:, wide : wide + 256] + sums[:, wide + 256 : wide + 512]) + sums[:, wide + 512 :]
    if ring:
        to_tx, to_ty, *kept, grad_w_out = pack(tile_word, s_all, shard, ff_own)
        from_tx = swap(to_tx, "tx")
        passed_on = swap(from_tx[ff_own : 2 * ff_own], "ty")
        from_ty = swap(to_ty, "ty")
        grad_w_gu, grad_down, grad_w_qkv = unpack(
            tile_word, from_tx, from_ty, passed_on, kept, (s_gu, store["gu_tx"], store["gu_ty"]), shard, ff_own
        )
        grad_silu = after(grad_silu, from_tx)
    else:
        sums_of = lambda grad: lax.psum_scatter(grad, "img", scatter_dimension=0, tiled=True)
        s_first, s_down, s_gu = sums_of(g_first).astype(F32), sums_of(g_down), sums_of(g_gu)
        gu_cols = 2 * hidden_own // TILES
        got = exchange_tiles(lambda t: lax.dynamic_slice_in_dim(s_gu, t * gu_cols, gu_cols, 1))
        grad_w_out = s_first[:, 3 * COLS :].astype(F32)
        s_qkv = s_first.astype(BF16)

        grad_down = jnp.concatenate(
            exchange_tiles(lambda t: lax.dynamic_slice_in_dim(s_down, t * out_width, out_width, 1))
        ).astype(F32)
        grad_w_gu = jnp.concatenate(
            [got[s][:, ff_own * g : ff_own * (g + 1)] for g in range(gu_cols // ff_own) for s in range(4)],
            axis=1,
        ).astype(F32)
        units = [s_qkv[:, COLS * p : COLS * (p + 1)] for p in range(3)]

        def choose(options, table):
            result = options[table[0]]
            for t in range(1, 4):
                if table[t] != table[0]:
                    result = jnp.where(tile == t, options[table[t]], result)
            return result

        slots = [
            choose(units, KEPT),
            swap(choose(units, TO_TX), "tx"),
            swap(choose(units, TO_TY), "ty"),
        ]
        grad_w_qkv = jnp.concatenate(
            [choose(slots, [SLOTS[t][k] for t in range(4)]) for k in range(3)], axis=1
        ).astype(F32)

    flips = (jnp.arange(count, dtype=jnp.int32) ^ img).astype(jnp.int32)
    grad_silu = flip_exchange(grad_silu, count, bits[-2::-1])
    grad_silu = reorder(flips, grad_silu).reshape(1, width)
    sigmoid_c = jax.nn.sigmoid(cond_float)
    grad_cond = (grad_silu * sigmoid_c * (1.0 + cond_float * (1.0 - sigmoid_c))).astype(BF16)

    return (
        store["output"].reshape(tokens.shape),
        grad_tokens.reshape(tokens.shape),
        grad_cond,
        grad_w_qkv,
        grad_w_out,
        grad_w_gu,
        grad_down,
        grad_ada,
        gain_back(gain_sums[0, :LANES]),
        gain_back(gain_sums[0, LANES:]),
        grad_bias,
    )


def solution(mesh):
    tiled = P("img", "ty", "tx", None)
    rows = P("img", None)
    cut = P("img", ("ty", "tx"))
    in_specs = (tiled, rows, P("img"), rows, rows, rows, rows, rows, P(), P(), P(), tiled)
    out_specs = (tiled, tiled, rows, cut, cut, cut, cut, cut, P(), P(), P())
    return jax.shard_map(
        functools.partial(body, mesh.shape["img"]),
        mesh=mesh,
        in_specs=in_specs,
        out_specs=out_specs,
        check_vma=False,
    )
```

```python
import functools
import math

import jax
import jax.numpy as jnp
import numpy as np
from jax import lax
from jax.experimental import pallas as pl
from jax.experimental.pallas import tpu as pltpu
from jax.sharding import PartitionSpec as P

HEADS = 16
HEAD = 72
FF = 3072
TILES = 4
OWN = HEADS // TILES
LANES = 128
COLS = OWN * HEAD
PADDED = OWN * LANES
WINDOW = 384
QUARTER = HEAD // 4
EPSILON = 1e-06
LOG2E = math.log2(math.e)
LN2 = math.log(2.0)
BF16 = jnp.bfloat16
F32 = jnp.float32


def head_lane(index):
    part, half, freq = index // 36, (index % 36) // QUARTER, index % QUARTER
    return half * 64 + part * QUARTER + freq


def spread_matrices():
    spread = np.zeros((4, WINDOW, PADDED), np.float32)
    for which in range(4):
        base = (COLS - 256) * which if which < 3 else 0
        for head in range(OWN):
            for index in range(HEAD):
                lane = index if which >= 2 else head_lane(index)
                spread[which, base + HEAD * head + index, LANES * head + lane] = 1.0
    return spread


def dot(left, right):
    return jnp.dot(left, right, preferred_element_type=F32)


def dot_nt(left, right):
    return lax.dot_general(left, right, (((1,), (1,)), ((), ())), preferred_element_type=F32)


def dot_tn(left, right):
    return lax.dot_general(left, right, (((0,), (0,)), ((), ())), preferred_element_type=F32)


def inverse_rms(values):
    return lax.rsqrt(jnp.mean(values * values, axis=-1, keepdims=True) + EPSILON)


def norm_back(grad_out, normed, inv_scale):
    return inv_scale * (grad_out - normed * jnp.mean(grad_out * normed, axis=-1, keepdims=True))


def swap(values, axis):
    return lax.ppermute(values, axis, [(0, 1), (1, 0)])


FLIPS = (2, 3, 0, 1)


def tile_at(flip):
    return (lax.axis_index("ty") ^ (flip >> 1)) * 2 + (lax.axis_index("tx") ^ (flip & 1))


def gather_tiles(values):
    far = swap(values, "ty")
    return [far, swap(far, "tx"), values, swap(values, "tx")]


def sum_tiles(values):
    values = values + swap(values, "tx")
    return values + swap(values, "ty")


def absolute(pieces):
    ty, tx = lax.axis_index("ty"), lax.axis_index("tx")
    turned = [jnp.where(tx == 1, pieces[f ^ 1], pieces[f]) for f in range(4)]
    return [jnp.where(ty == 1, turned[f ^ 2], turned[f]) for f in range(4)]


def exchange_tiles(piece_for):
    across = [(a * 2 + b, (1 - a) * 2 + 1 - b) for a in range(2) for b in range(2)]
    return absolute(
        [
            piece_for(tile_at(0)),
            swap(piece_for(tile_at(1)), "tx"),
            swap(piece_for(tile_at(2)), "ty"),
            lax.ppermute(piece_for(tile_at(3)), ("ty", "tx"), across),
        ]
    )


def flip_perm(count, bit):
    return [(i, i ^ bit) for i in range(count)]


def flip_exchange(values, count, bits):
    rows = [values[k : k + 1] for k in range(count)]
    for bit in bits:
        sent = jnp.concatenate([rows[k] for k in range(count) if k & bit])
        got = lax.ppermute(sent, "img", flip_perm(count, bit))
        moved = [k for k in range(count) if k & bit]
        for place, k in enumerate(moved):
            rows[k] = got[place : place + 1]
    return jnp.concatenate(rows)


def ring_perm(count, step):
    order = list(range(0, count, 2)) + list(range(count - 1, 0, -2))
    return [(order[i], order[(i + step) % count]) for i in range(count)]


def ring_place(count):
    index = lax.axis_index("img")
    return jnp.where(index % 2 == 0, index // 2, count - 1 - index // 2)


def ring_owner(count, place):
    place = (place + count) % count
    return jnp.where(place < count // 2, 2 * place, 2 * (count - 1 - place) + 1)


def use_ring(count, rows):
    return 2 < count <= 16 and count % 2 == 0 and rows % 16 == 0


def split_rows(rows):
    return (rows // 2 + 15) // 16 * 16


def out_share(pick, first):
    return dot_nt(pick, first[:, first.shape[1] - WINDOW :]).astype(BF16)


def ring_gather(own, count, beside):
    cut = split_rows(own.shape[0])
    a, b = own[:cut], own[cut:]
    pieces, value = [], None
    for hop in range(count - 1):
        a = lax.ppermute(a, "img", ring_perm(count, 1))
        b = lax.ppermute(b, "img", ring_perm(count, -1))
        if hop < len(beside):
            value = beside[hop](value)
            a, b, value = lax.optimization_barrier((a, b, value))
        pieces.append((a, b))
    for step in beside[count - 1 :]:
        value = step(value)
    return pieces, value


def assemble_kernel(count, total, plan, shared, index_ref, pick_ref, *refs):
    cut = split_rows(total)
    own, pieces_a, pieces_b = refs[0], refs[1:count], refs[count : 2 * count - 1]
    outs, sems = refs[2 * count - 1 : -1], refs[-1]
    started = []
    for k, (src, first, size) in enumerate(
        [(own, 0, total)]
        + [(piece, 0, cut) for piece in pieces_a]
        + [(piece, cut, total - cut) for piece in pieces_b]
    ):
        for out, rows, base, count_rows, to_row, from_lane, to_lane, lanes in plan:
            low, high = max(first, base), min(first + size, base + count_rows)
            if low < high:
                start = pl.multiple_of(index_ref[k] * rows + to_row + low - base, 16)
                copy = pltpu.make_async_copy(
                    src.at[pl.ds(low - first, high - low), pl.ds(from_lane, lanes)],
                    outs[out].at[pl.ds(start, high - low), pl.ds(to_lane, lanes)],
                    sems.at[len(started)],
                )
                copy.start()
                started.append(copy)
    for copy in started:
        copy.wait()
    if shared:
        outs[-1][...] = out_share(pick_ref[...], outs[0])


def assemble(own, pieces, shapes, plan, count, shared):
    place = ring_place(count)
    steps = jnp.asarray([0] + [-k for k in range(1, count)] + list(range(1, count)), jnp.int32)
    index = ring_owner(count, place + steps).astype(jnp.int32)
    copies = 2 * count - 1
    shapes = [jax.ShapeDtypeStruct(shape, own.dtype) for shape in shapes]
    return pl.pallas_call(
        functools.partial(assemble_kernel, count, own.shape[0], plan, shared),
        out_shape=shapes,
        in_specs=[smem(), vmem()] + [pl.BlockSpec(memory_space=pltpu.HBM)] * copies,
        out_specs=[vmem() for _ in shapes],
        scratch_shapes=[pltpu.SemaphoreType.DMA((2 * len(plan) * copies,))],
        compiler_params=limit(58),
        cost_estimate=cost(5),
        name="assemble_first" if shared else "assemble_gu",
    )(index, out_pick(), own, *[a for a, _ in pieces], *[b for _, b in pieces])


def out_pick():
    pick = np.zeros((COLS, WINDOW), np.float32)
    pick[np.arange(COLS), WINDOW - COLS + np.arange(COLS)] = 1.0
    return jnp.asarray(pick, BF16)


def after(value, *others):
    return lax.optimization_barrier((value, others))[0]


def ring_scatter(grads, count, beside):
    sizes = [grad.shape[0] // count for grad in grads]
    total = sum(sizes)
    cut = split_rows(total)
    place = ring_place(count)
    value = None

    def part(sign, step):
        owner = ring_owner(count, place - sign * step)
        first, last = (0, cut) if sign > 0 else (cut, total)
        found, base = [], 0
        for grad, rows in zip(grads, sizes):
            low, high = max(first, base), min(last, base + rows)
            if low < high:
                found.append(lax.dynamic_slice_in_dim(grad, owner * rows + low - base, high - low, 0))
            base += rows
        return jnp.concatenate(found)

    sums = [part(1, 1), part(-1, 1)]
    for step in range(2, count + 1):
        kind = BF16 if step < count else F32
        got = [lax.ppermute(sums[k], "img", ring_perm(count, sign)) for k, sign in enumerate((1, -1))]
        if step - 2 < len(beside) and beside[step - 2]:
            value = beside[step - 2](value)
            got, value = lax.optimization_barrier((got, value))
        for k, sign in enumerate((1, -1)):
            sums[k] = (got[k].astype(F32) + part(sign, step).astype(F32)).astype(kind)
    for step in beside[count - 1 :]:
        value = step(value)
    return sums, value


def vmem():
    return pl.BlockSpec(memory_space=pltpu.VMEM)


def limit(megabytes):
    return pltpu.CompilerParams(vmem_limit_bytes=megabytes * 1024 * 1024)


def cost(microseconds):
    return pl.CostEstimate(
        flops=int(microseconds * 1.1e9), bytes_accessed=int(microseconds * 3e6), transcendentals=0
    )


def hbm():
    return pl.BlockSpec(memory_space=pltpu.HBM)


def lane_ids(rows):
    return lax.broadcasted_iota(jnp.int32, (rows, LANES), 1)


def three_parts(column):
    high = column.astype(BF16)
    rest = column - high.astype(F32)
    mid = rest.astype(BF16)
    return high, mid, (rest - mid.astype(F32)).astype(BF16)


def head_sums(values):
    lanes = values.shape[1]
    row = lax.broadcasted_iota(jnp.int32, (PAIR, PAIR), 0) // LANES
    col = lax.broadcasted_iota(jnp.int32, (PAIR, PAIR), 1) // LANES
    ones = jnp.where(row == col, 1.0, 0.0).astype(BF16)
    high = values.astype(BF16)
    rest = (values - high.astype(F32)).astype(BF16)
    return jnp.concatenate(
        [
            dot(high[:, at : at + PAIR], ones) + dot(rest[:, at : at + PAIR], ones)
            for at in range(0, lanes, PAIR)
        ],
        axis=1,
    )


def put_lanes(values, first, parts):
    lanes = lane_ids(values.shape[0])
    for k, part in enumerate(parts):
        values = jnp.where(lanes == first + k, part.astype(values.dtype), values)
    return values


QK_SPARE = 100
V_SPARE = HEAD


PAIRS = OWN // 2
PAIR = 2 * LANES
PAIR_COLS = 2 * HEAD


def project_kernel(
    x0_ref, x1_ref, x2_ref, x3_ref, mod_ref, w_ref, cos_ref, sin_ref, gq_ref, gk_ref, spread_ref,
    attn_ref, qraw_ref, kraw_ref, q0_ref, q1_ref, k0_ref, k1_ref, v0_ref, v1_ref, wpad_ref,
):
    block = x0_ref.shape[0]
    tokens = 4 * block
    factor = LOG2E / math.sqrt(HEAD)

    for place, x_ref in enumerate((x0_ref, x1_ref, x2_ref, x3_ref)):
        x = x_ref[...].astype(F32)
        normed = x * inverse_rms(x)
        attn_ref[block * place : block * (place + 1), :] = (
            normed * (1.0 + mod_ref[1:2, :]) + mod_ref[0:1, :]
        ).astype(BF16)

    @pl.loop(0, w_ref.shape[0] // 128)
    def _(i):
        rows = pl.ds(pl.multiple_of(i * 128, 128), 128)
        for w in range(3):
            wpad_ref[rows, PADDED * w : PADDED * (w + 1)] = dot(
                w_ref[rows, 256 * w : 256 * w + WINDOW], spread_ref[w]
            ).astype(BF16)

    @pl.loop(0, tokens // block)
    def _(i):
        rows = pl.ds(pl.multiple_of(i * block, block), block)
        attn_in = attn_ref[rows, :]
        cos, sin = cos_ref[rows, :], sin_ref[rows, :]
        lanes = lane_ids(block)
        spare = (lanes >= QK_SPARE) & (lanes < QK_SPARE + 3)
        for which, raw_ref, out_refs, gain_ref in (
            (0, qraw_ref, (q0_ref, q1_ref), gq_ref),
            (1, kraw_ref, (k0_ref, k1_ref), gk_ref),
        ):
            raw = dot(attn_in, wpad_ref[:, PADDED * which : PADDED * (which + 1)])
            raw_ref[rows, :] = raw
            for head in range(OWN):
                part = raw[:, LANES * head : LANES * (head + 1)]
                inv = lax.rsqrt(jnp.sum(part * part, axis=-1, keepdims=True) / HEAD + EPSILON)
                scaled = part * inv * gain_ref[...]
                turned = scaled * cos + pltpu.roll(scaled, 64, 1) * sin
                turned = turned * factor if which == 0 else jnp.where(spare, 1.0, turned)
                at = slice(LANES * (head % 2), LANES * (head % 2 + 1))
                out_refs[head // 2][rows, at] = turned.astype(BF16)
        value = dot(attn_in, wpad_ref[:, PADDED * 2 : PADDED * 3])
        ones = (lanes >= V_SPARE) & (lanes < V_SPARE + 3)
        for head in range(OWN):
            at = slice(LANES * (head % 2), LANES * (head % 2 + 1))
            part = value[:, LANES * head : LANES * (head + 1)]
            (v0_ref, v1_ref)[head // 2][rows, at] = jnp.where(ones, 1.0, part).astype(BF16)


def project(x_tiles, mod, w, cos, sin, gq, gk, spread):
    width = w.shape[0]
    tokens = cos.shape[0]
    return pl.pallas_call(
        project_kernel,
        out_shape=[
            jax.ShapeDtypeStruct((tokens, width), BF16),
            jax.ShapeDtypeStruct((tokens, PADDED), F32),
            jax.ShapeDtypeStruct((tokens, PADDED), F32),
        ]
        + [jax.ShapeDtypeStruct((tokens, PAIR), BF16)] * 6,
        in_specs=[vmem()] * 11,
        out_specs=[vmem()] * 9,
        scratch_shapes=[pltpu.VMEM((width, 3 * PADDED), BF16)],
        cost_estimate=cost(16),
        compiler_params=limit(34),
        name="project",
    )(*x_tiles, mod, w, cos, sin, gq, gk, spread)


def attend_kernel(qin_ref, k_ref, v_ref, spread_ref, q_ref, mixedp_ref, mixed_ref):
    tokens = qin_ref.shape[0]
    block = 256
    for i in range(tokens // block):
        rows = slice(block * i, block * (i + 1))
        for head in range(2):
            at = slice(LANES * head, LANES * (head + 1))
            query = qin_ref[rows, at]
            terms = jnp.exp2(dot_nt(query, k_ref[:, at])).astype(BF16)
            result = dot(terms, v_ref[:, at])
            total = result[:, V_SPARE : V_SPARE + 1]
            mixedp_ref[rows, at] = (result * (1.0 / total)).astype(BF16)
            q_ref[rows, at] = put_lanes(query, QK_SPARE, three_parts(-jnp.log2(total)))
        mixed_ref[:, rows] = dot_nt(spread_ref[3, :PAIR_COLS, :PAIR], mixedp_ref[rows, :]).astype(BF16)


def attend(q, k, v, spread):
    tokens = q.shape[0]
    return pl.pallas_call(
        attend_kernel,
        out_shape=[
            jax.ShapeDtypeStruct((tokens, PAIR), BF16),
            jax.ShapeDtypeStruct((tokens, PAIR), BF16),
            jax.ShapeDtypeStruct((PAIR_COLS, tokens), BF16),
        ],
        in_specs=[vmem()] * 4,
        out_specs=[vmem()] * 3,
        cost_estimate=cost(4.1),
        compiler_params=limit(20),
        name="attend",
    )(q, k, v, spread)


def attention_back_kernel(
    g0_ref, g1_ref, g2_ref, g3_ref, wout_ref, qraw_ref, kraw_ref, q0_ref, q1_ref, k0_ref, k1_ref, v0_ref, v1_ref,
    m0_ref, m1_ref, cos_ref, sin_ref, gq_ref, gk_ref, spread_ref, out_ref, gains_ref, do_ref, dq_ref, dk_ref, pad_ref,
    *scratch
):
    sems = scratch[-1]
    late = (q0_ref, k0_ref, v0_ref, q1_ref, k1_ref, v1_ref, cos_ref, sin_ref, qraw_ref, kraw_ref)
    copies = [pltpu.make_async_copy(src, dst, sems.at[n]) for n, (src, dst) in enumerate(zip(late, scratch))]
    for copy in copies:
        copy.start()
    q0_ref, k0_ref, v0_ref, q1_ref, k1_ref, v1_ref, cos_ref, sin_ref, qraw_ref, kraw_ref = scratch[:-1]
    block = g0_ref.shape[0]
    tokens = 4 * block
    root = 1.0 / math.sqrt(HEAD)

    for place, g_ref in enumerate((g0_ref, g1_ref, g2_ref, g3_ref)):
        rows = slice(block * place, block * (place + 1))
        grad_mixed = dot(g_ref[...], wout_ref[...]).astype(BF16)
        wide = dot(grad_mixed, spread_ref[3, :COLS, :])
        mixed = jnp.concatenate([m0_ref[rows, :], m1_ref[rows, :]], axis=1).astype(F32)
        row_dot = head_sums(wide * mixed)
        for head in range(OWN):
            at = slice(LANES * head, LANES * (head + 1))
            do_ref[rows, at] = put_lanes(wide[:, at].astype(BF16), V_SPARE, three_parts(-row_dot[:, at]))

    for head in range(OWN):
        at = slice(LANES * head, LANES * (head + 1))
        pair_at = slice(LANES * (head % 2), LANES * (head % 2 + 1))
        q_ref, k_ref, v_ref = ((q0_ref, k0_ref, v0_ref), (q1_ref, k1_ref, v1_ref))[head // 2]
        if head % 2 == 0:
            for copy in copies[3 * (head // 2) : 3 * (head // 2) + 3]:
                copy.wait()
        dq_ref[at, :] = jnp.zeros((LANES, tokens), F32)

        for i in range(tokens // block):
            rows = slice(block * i, block * (i + 1))
            query, grad = q_ref[:, pair_at], do_ref[:, at]
            key = k_ref[rows, pair_at]
            probs = jnp.exp2(dot_nt(key, query))
            slope = (probs * dot_nt(v_ref[rows, pair_at], grad)).astype(BF16)
            pad_ref[rows, 2 * PADDED + LANES * head : 2 * PADDED + LANES * (head + 1)] = dot(
                probs.astype(BF16), grad
            ).astype(BF16)
            dk_ref[rows, at] = dot(slope, query) * LN2
            dq_ref[at, :] += dot(key.astype(F32).T.astype(BF16), slope)

    for copy in copies[6:]:
        copy.wait()
    gains_ref[...] = jnp.zeros_like(gains_ref)

    @pl.loop(0, tokens // block)
    def _(i):
        rows = pl.ds(pl.multiple_of(i * block, block), block)
        cos, sin = cos_ref[rows, :], sin_ref[rows, :]
        for which, raw_ref, gain_ref in ((0, qraw_ref, gq_ref), (1, kraw_ref, gk_ref)):
            raw = raw_ref[rows, :]
            inv = lax.rsqrt(head_sums(raw * raw) / HEAD + EPSILON)
            hat = raw * inv
            turned = []
            for head in range(OWN):
                at = slice(LANES * head, LANES * (head + 1))
                grad = dq_ref[at, rows].T * root if which == 0 else dk_ref[rows, at]
                turned.append(grad * cos - pltpu.roll(grad, 64, 1) * sin)
            gain = jnp.concatenate([gain_ref[...]] * OWN, axis=1)
            product = jnp.concatenate(turned, axis=1) * hat
            gained = jnp.sum(product, axis=0, keepdims=True)
            gains_ref[which : which + 1, :] += sum(
                gained[:, LANES * head : LANES * (head + 1)] for head in range(OWN)
            )
            mean = head_sums(product * gain) / HEAD
            pad_ref[rows, PADDED * which : PADDED * (which + 1)] = (
                inv * (jnp.concatenate(turned, axis=1) * gain - hat * mean)
            ).astype(BF16)
        compact = [
            dot_nt(pad_ref[rows, PADDED * w : PADDED * (w + 1)], spread_ref[w]).astype(BF16)
            for w in range(3)
        ]
        out_ref[rows, :] = jnp.concatenate(
            [
                compact[0][:, :256],
                compact[0][:, 256:] + compact[1][:, :128],
                compact[1][:, 128:256],
                compact[1][:, 256:] + compact[2][:, :128],
                compact[2][:, 128:],
            ],
            axis=1,
        )[:, : 3 * COLS]


def attention_backward(grads, w_rows, qraw, kraw, q, k, v, mixedp, cos, sin, gq, gk, spread):
    tokens = cos.shape[0]
    return pl.pallas_call(
        attention_back_kernel,
        out_shape=[
            jax.ShapeDtypeStruct((tokens, 3 * COLS), BF16),
            jax.ShapeDtypeStruct((8, LANES), F32),
        ],
        in_specs=[vmem()] * 5 + [hbm()] * 8 + [vmem()] * 2 + [hbm()] * 2 + [vmem()] * 3,
        out_specs=[vmem()] * 2,
        scratch_shapes=[
            pltpu.VMEM((tokens, PADDED), BF16),
            pltpu.VMEM((PADDED, tokens), F32),
            pltpu.VMEM((tokens, PADDED), F32),
            pltpu.VMEM((tokens, 3 * PADDED), BF16),
        ]
        + [pltpu.VMEM((tokens, PAIR), BF16)] * 6
        + [pltpu.VMEM((tokens, LANES), F32)] * 2
        + [pltpu.VMEM((tokens, PADDED), F32)] * 2
        + [pltpu.SemaphoreType.DMA((10,))],
        cost_estimate=cost(K5_COST),
        compiler_params=limit(58),
        name="attention_backward",
    )(*grads, w_rows, qraw, kraw, *q, *k, *v, *mixedp, cos, sin, gq, gk, spread)


def smem():
    return pl.BlockSpec(memory_space=pltpu.SMEM)


def out_weight_kernel(tile_ref, p0_ref, p1_ref, p2_ref, p3_ref, out_ref, own_ref):
    for place, piece in enumerate((p0_ref, p1_ref, p2_ref, p3_ref)):
        start = pl.multiple_of((tile_ref[0] ^ FLIPS[place]) * COLS, 16)
        out_ref[pl.ds(start, COLS), :] = piece[...]
    for tile in range(4):

        @pl.when(tile_ref[0] == tile)
        def _(tile=tile):
            own_ref[...] = out_ref[:, COLS * tile : COLS * (tile + 1)]


def out_weight(tile, pieces):
    width = pieces[0].shape[1]
    return pl.pallas_call(
        out_weight_kernel,
        out_shape=[
            jax.ShapeDtypeStruct((width, width), BF16),
            jax.ShapeDtypeStruct((width, COLS), BF16),
        ],
        in_specs=[smem()] + [vmem()] * 4,
        out_specs=[vmem()] * 2,
        cost_estimate=cost(3.8),
        compiler_params=limit(12),
        name="out_weight",
    )(tile, *pieces)


def residual_kernel(tile_ref, mod_ref, wout_ref, *refs):
    x_refs, mixed_refs = refs[:4], refs[4 : 4 + 4 * PAIRS]
    mlp_ref, attended_ref, mixed_ref = refs[4 + 4 * PAIRS :]
    block = x_refs[0].shape[0]
    for k, m_ref in enumerate(mixed_refs):
        pair, source = k // 4, k % 4
        start = pl.multiple_of((tile_ref[0] ^ FLIPS[source]) * COLS + PAIR_COLS * pair, 16)
        for place in range(4):
            at = block * (place ^ FLIPS[source])
            mixed_ref[pl.ds(start, PAIR_COLS), block * place : block * (place + 1)] = m_ref[:, at : at + block]
    for place, x_ref in enumerate(x_refs):
        here = slice(block * place, block * (place + 1))
        attended = lax.dot_general(
            mixed_ref[:, here], wout_ref[...], (((0,), (1,)), ((), ())), preferred_element_type=F32
        )
        if place == 2:
            attended_ref[...] = attended
        x_mid = x_ref[...].astype(F32) + mod_ref[2:3, :] * attended
        normed = x_mid * inverse_rms(x_mid)
        mlp_ref[here, :] = (normed * (1.0 + mod_ref[4:5, :]) + mod_ref[3:4, :]).astype(BF16)


def branch_kernel(mod_ref, dy0_ref, dy1_ref, dy2_ref, dy3_ref, out_ref):
    block = dy0_ref.shape[0]
    for place, dy_ref in enumerate((dy0_ref, dy1_ref, dy2_ref, dy3_ref)):
        out_ref[block * place : block * (place + 1), :] = (
            mod_ref[5:6, :] * (mod_ref[6:7, :] * dy_ref[...].astype(F32))
        ).astype(BF16)


def branch_grad(mod, dy_tiles):
    block, width = dy_tiles[0].shape
    return pl.pallas_call(
        branch_kernel,
        out_shape=jax.ShapeDtypeStruct((4 * block, width), BF16),
        in_specs=[vmem()] * 5,
        out_specs=vmem(),
        compiler_params=limit(12),
        cost_estimate=cost(3),
        name="branch_grad",
    )(mod, *dy_tiles)


def residual(tile, mod, w_out, x_tiles, mixed):
    block, width = x_tiles[0].shape
    return pl.pallas_call(
        residual_kernel,
        out_shape=[
            jax.ShapeDtypeStruct((4 * block, width), BF16),
            jax.ShapeDtypeStruct((block, width), F32),
        ],
        in_specs=[smem()] + [vmem()] * (6 + 4 * PAIRS),
        out_specs=[vmem()] * 2,
        scratch_shapes=[pltpu.VMEM((width, 4 * block), BF16)],
        compiler_params=limit(58),
        cost_estimate=cost(9),
        name="residual",
    )(tile, mod, w_out, *x_tiles, *mixed)


def mlp_kernel(places, wgu_ref, wdown_ref, in_ref, gbranch_ref, *refs):
    number = len(places)
    refs = refs[-(2 + 2 * number) :]
    hidden_ref, ggu_ref, branch_refs, gmlp_refs = refs[0], refs[1], refs[2 : 2 + number], refs[2 + number :]
    block = branch_refs[0].shape[0]
    half = wgu_ref.shape[1] // 2
    for place, branch_ref, gmlp_ref in zip(places, branch_refs, gmlp_refs):
        here = slice(0, block) if number == 1 else slice(block * place, block * (place + 1))
        mlp_in, grad_branch = in_ref[here, :], gbranch_ref[here, :]
        gate = dot(mlp_in, wgu_ref[:, :half])
        up = dot(mlp_in, wgu_ref[:, half:])
        grad_hidden = dot_nt(grad_branch, wdown_ref[...])
        sigmoid = jax.nn.sigmoid(gate)
        silu = gate * sigmoid
        hidden = (silu * up).astype(BF16)
        hidden_ref[here, :] = hidden
        branch_ref[...] = dot(hidden, wdown_ref[...]).astype(BF16)
        grad_gate = (grad_hidden * up * (sigmoid * (1.0 + gate * (1.0 - sigmoid)))).astype(BF16)
        grad_up = (grad_hidden * silu).astype(BF16)
        ggu_ref[here, :half] = grad_gate
        ggu_ref[here, half:] = grad_up
        gmlp_ref[...] = (
            dot_nt(grad_gate, wgu_ref[:, :half]) + dot_nt(grad_up, wgu_ref[:, half:])
        ).astype(BF16)


def mlp(places, w_gu, w_down, mlp_in, grad_branch, kept):
    number = len(places)
    tokens, width = mlp_in.shape
    block = tokens // 4
    hidden = w_down.shape[0]
    one = pl.Buffered(1)
    if number == 1:
        row_block = lambda cols: pl.BlockSpec((block, cols), lambda i: (places[0], 0), pipeline_mode=one)
    else:
        row_block = lambda cols: pl.BlockSpec((4 * block, cols), lambda i: (0, 0), pipeline_mode=one)
    whole = lambda rows, cols: pl.BlockSpec((rows, cols), lambda i: (0, 0), pipeline_mode=one)
    args = [w_gu, w_down, mlp_in, grad_branch, *kept]
    shapes = [(tokens, hidden), (tokens, 2 * hidden)]
    return pl.pallas_call(
        functools.partial(mlp_kernel, places),
        grid=(1,),
        out_shape=[jax.ShapeDtypeStruct(shape, BF16) for shape in shapes]
        + [jax.ShapeDtypeStruct((block, width), BF16)] * (2 * number),
        in_specs=[whole(*w_gu.shape), whole(*w_down.shape), row_block(width), row_block(width)]
        + [hbm()] * len(kept),
        out_specs=[row_block(shape[1]) for shape in shapes] + [whole(block, width)] * (2 * number),
        input_output_aliases={4 + k: k for k in range(len(kept))},
        compiler_params=limit(58),
        cost_estimate=cost(12 if number == 2 else 0.3),
        name="mlp",
    )(*args)


def middle_kernel(a_ref, b_ref, c_ref, attended_ref, x_ref, dy_ref, mod_ref, gatt_ref, gmid_ref, sums_ref):
    grad_in = a_ref[...].astype(F32) + b_ref[...].astype(F32) + c_ref[...].astype(F32)
    attended = attended_ref[...]
    x_mid = x_ref[...].astype(F32) + mod_ref[2:3, :] * attended
    inv = inverse_rms(x_mid)
    normed = x_mid * inv
    product = grad_in * normed
    grad_mid = mod_ref[6:7, :] * dy_ref[...].astype(F32) + inv * (
        grad_in * (1.0 + mod_ref[4:5, :])
        - normed * jnp.mean(product * (1.0 + mod_ref[4:5, :]), axis=-1, keepdims=True)
    )
    gmid_ref[...] = grad_mid
    gatt_ref[...] = (mod_ref[2:3, :] * grad_mid).astype(BF16)
    sums_ref[...] = jnp.zeros_like(sums_ref)
    sums_ref[0:1, :] = jnp.sum(grad_mid * attended, axis=0, keepdims=True)
    sums_ref[1:2, :] = jnp.sum(grad_in, axis=0, keepdims=True)
    sums_ref[2:3, :] = jnp.sum(product, axis=0, keepdims=True)


def middle(parts, attended, x, dy, mod):
    block, width = x.shape
    return pl.pallas_call(
        middle_kernel,
        out_shape=[
            jax.ShapeDtypeStruct((block, width), BF16),
            jax.ShapeDtypeStruct((block, width), F32),
            jax.ShapeDtypeStruct((8, width), F32),
        ],
        in_specs=[vmem()] * 7,
        out_specs=[vmem()] * 3,
        cost_estimate=cost(4.6),
        compiler_params=limit(14),
        name="middle",
    )(*parts, attended, x, dy, mod)


def output_kernel(a_ref, b_ref, c_ref, attended_ref, x_ref, dy_ref, mod_ref, out_ref, sums_ref):
    branch = a_ref[...].astype(F32) + b_ref[...].astype(F32) + c_ref[...].astype(F32)
    x_mid = x_ref[...].astype(F32) + mod_ref[2:3, :] * attended_ref[...]
    live = mod_ref[6:7, :]
    out_ref[...] = (live * (x_mid + mod_ref[5:6, :] * branch)).astype(BF16)
    sums_ref[...] = jnp.zeros_like(sums_ref)
    sums_ref[0:1, :] = jnp.sum(live * dy_ref[...].astype(F32) * branch, axis=0, keepdims=True)


def output_tile(parts, attended, x, dy, mod):
    block, width = x.shape
    return pl.pallas_call(
        output_kernel,
        out_shape=[
            jax.ShapeDtypeStruct((block, width), BF16),
            jax.ShapeDtypeStruct((8, width), F32),
        ],
        in_specs=[vmem()] * 7,
        out_specs=[vmem()] * 2,
        cost_estimate=cost(3.5),
        compiler_params=limit(12),
        name="output_tile",
    )(*parts, attended, x, dy, mod)


def tokens_kernel(a_ref, b_ref, c_ref, x_ref, gmid_ref, mod_ref, out_ref, sums_ref):
    grad_in = a_ref[...].astype(F32) + b_ref[...].astype(F32) + c_ref[...].astype(F32)
    x = x_ref[...].astype(F32)
    inv = inverse_rms(x)
    normed = x * inv
    product = grad_in * normed
    scale = 1.0 + mod_ref[1:2, :]
    out_ref[...] = (
        gmid_ref[...] + inv * (grad_in * scale - normed * jnp.mean(product * scale, axis=-1, keepdims=True))
    ).astype(BF16)
    sums_ref[...] = jnp.zeros_like(sums_ref)
    sums_ref[0:1, :] = jnp.sum(grad_in, axis=0, keepdims=True)
    sums_ref[1:2, :] = jnp.sum(product, axis=0, keepdims=True)


def tokens_back(parts, x, grad_mid, mod):
    block, width = x.shape
    return pl.pallas_call(
        tokens_kernel,
        out_shape=[
            jax.ShapeDtypeStruct((block, width), BF16),
            jax.ShapeDtypeStruct((8, width), F32),
        ],
        in_specs=[vmem()] * 6,
        out_specs=[vmem()] * 2,
        cost_estimate=cost(3.6),
        compiler_params=limit(14),
        name="tokens_back",
    )(*parts, x, grad_mid, mod)


def first_grad_kernel(tile_ref, g0_ref, g1_ref, g2_ref, g3_ref, *refs):
    mixed_refs, (attn_ref, qkv_ref, out_ref, cols_ref) = refs[: 4 * PAIRS], refs[4 * PAIRS :]
    block = g0_ref.shape[0]
    wide = qkv_ref.shape[1]
    for tile in range(4):

        @pl.when(tile_ref[0] == tile)
        def _(tile=tile):
            for place, g_ref in enumerate((g0_ref, g1_ref, g2_ref, g3_ref)):
                cols_ref[block * place : block * (place + 1), :] = g_ref[:, COLS * tile : COLS * (tile + 1)]

    for k in range(attn_ref.shape[1] // LANES):
        at = slice(LANES * k, LANES * (k + 1))
        out_ref[at, :wide] = dot_tn(attn_ref[:, at], qkv_ref[...]).astype(BF16)
    for k, m_ref in enumerate(mixed_refs):
        pair, source = k // 4, k % 4
        total = None
        for place in range(4):
            at = block * (place ^ FLIPS[source])
            term = dot(m_ref[:, at : at + block], cols_ref[block * place : block * (place + 1), :])
            total = term if total is None else total + term
        start = pl.multiple_of((tile_ref[0] ^ FLIPS[source]) * COLS + PAIR_COLS * pair, 16)
        out_ref[pl.ds(start, PAIR_COLS), wide:] = total.astype(BF16)


def first_grad(tile, grads, mixed, attn_in, grad_qkv):
    width = attn_in.shape[1]
    return pl.pallas_call(
        first_grad_kernel,
        out_shape=jax.ShapeDtypeStruct((width, grad_qkv.shape[1] + COLS), BF16),
        in_specs=[smem()] + [vmem()] * (6 + 4 * PAIRS),
        out_specs=vmem(),
        scratch_shapes=[pltpu.VMEM((grad_qkv.shape[0], COLS), BF16)],
        compiler_params=limit(58),
        cost_estimate=cost(FIRST_COST),
        name="first_grad",
    )(tile, *grads, *mixed, attn_in, grad_qkv)


def weight_grad_kernel(left_ref, right_ref, out_ref):
    for k in range(left_ref.shape[1] // LANES):
        at = slice(LANES * k, LANES * (k + 1))
        out_ref[at, :] = dot_tn(left_ref[:, at], right_ref[...]).astype(BF16)


def weight_grad(left, right, microseconds):
    return pl.pallas_call(
        weight_grad_kernel,
        out_shape=jax.ShapeDtypeStruct((left.shape[1], right.shape[1]), BF16),
        in_specs=[vmem()] * 2,
        out_specs=vmem(),
        compiler_params=limit(24),
        cost_estimate=cost(microseconds),
        name="weight_grad",
    )(left, right)


GU_AFTER = 5
K5_COST = 1
GU_BY = 3
TIE_BY = 1
FIRST_COST = 1
TO_TX = (1, 0, 2, 1)
TO_TY = (2, 2, 0, 0)
KEPT = (0, 1, 1, 2)
SLOTS = ((0, 1, 2), (2, 1, 0), (0, 1, 2), (2, 1, 0))


def pack_kernel(shard, ff_own, tile_ref, a_ref, b_ref, tx_ref, ty_ref, down_ref, unit_ref, out_ref):
    cut = a_ref.shape[0]

    def rows(first, last, lanes):
        pieces = []
        if first < cut:
            pieces.append(a_ref[first : min(last, cut), lanes])
        if last > cut:
            pieces.append(b_ref[max(first, cut) - cut : last - cut, lanes])
        return pieces[0] if len(pieces) == 1 else jnp.concatenate(pieces)

    def down(tile):
        return rows(shard, shard + ff_own, slice(COLS * tile, COLS * (tile + 1)))

    def unit(part):
        return rows(0, shard, slice(COLS * part, COLS * (part + 1)))

    out_ref[...] = unit(3)
    for tile in range(4):

        @pl.when(tile_ref[0] == tile)
        def _(tile=tile):
            for ref, pieces in (
                (tx_ref, (down(tile ^ 1), down(tile ^ 3), unit(TO_TX[tile]))),
                (ty_ref, (down(tile ^ 2), unit(TO_TY[tile]))),
            ):
                at = 0
                for piece in pieces:
                    ref[at : at + piece.shape[0], :COLS] = piece.astype(BF16)
                    at += piece.shape[0]
            down_ref[...] = down(tile)
            unit_ref[...] = unit(KEPT[tile])


def pack(tile, sums, shard, ff_own):
    return pl.pallas_call(
        functools.partial(pack_kernel, shard, ff_own),
        out_shape=[
            jax.ShapeDtypeStruct((shard + 2 * ff_own, WINDOW), BF16),
            jax.ShapeDtypeStruct((shard + ff_own, WINDOW), BF16),
            jax.ShapeDtypeStruct((ff_own, COLS), F32),
            jax.ShapeDtypeStruct((shard, COLS), F32),
            jax.ShapeDtypeStruct((shard, COLS), F32),
        ],
        in_specs=[smem()] + [vmem()] * 2,
        out_specs=[vmem()] * 5,
        compiler_params=limit(12),
        cost_estimate=cost(2),
        name="pack",
    )(tile, *sums)


def unpack_kernel(
    shard, ff_own, tile_ref, tx_ref, ty_ref, on_ref, down_ref, unit_ref, sgu_ref, gutx_ref, guty_ref,
    wgu_ref, wdown_ref, wqkv_ref,
):
    share = sgu_ref.shape[1] // 4
    groups = share // ff_own
    gus = [None, gutx_ref[:shard, :], guty_ref[:shard, :], guty_ref[shard:, :]]
    downs = [
        down_ref[...],
        tx_ref[:ff_own, :COLS].astype(F32),
        ty_ref[:ff_own, :COLS].astype(F32),
        on_ref[:, :COLS].astype(F32),
    ]
    units = [unit_ref[...], tx_ref[2 * ff_own :, :COLS].astype(F32), ty_ref[ff_own:, :COLS].astype(F32)]
    for tile in range(4):

        @pl.when(tile_ref[0] == tile)
        def _(tile=tile):
            for source in range(4):
                flip = source ^ tile
                wdown_ref[ff_own * source : ff_own * (source + 1), :] = downs[flip]
                piece = sgu_ref[:, share * tile : share * (tile + 1)] if flip == 0 else gus[flip]
                for group in range(groups):
                    at = share * group + ff_own * source
                    wgu_ref[:, at : at + ff_own] = piece[:, ff_own * group : ff_own * (group + 1)].astype(F32)
            for k in range(3):
                wqkv_ref[:, COLS * k : COLS * (k + 1)] = units[SLOTS[tile][k]]


def unpack(tile, from_tx, from_ty, passed_on, kept, gus, shard, ff_own):
    return pl.pallas_call(
        functools.partial(unpack_kernel, shard, ff_own),
        out_shape=[
            jax.ShapeDtypeStruct(gus[0].shape, F32),
            jax.ShapeDtypeStruct((4 * ff_own, COLS), F32),
            jax.ShapeDtypeStruct((shard, 3 * COLS), F32),
        ],
        in_specs=[smem()] + [vmem()] * 8,
        out_specs=[vmem()] * 3,
        compiler_params=limit(12),
        cost_estimate=cost(2),
        name="unpack",
    )(tile, from_tx, from_ty, passed_on, *kept, *gus)


def ada_kernel(tile_ref, mod_ref, w_ref, silu_ref, ada_ref, bias_ref, cond_ref):
    count, wide = mod_ref.shape
    width = w_ref.shape[1]
    share = width // 4
    for tile in range(4):

        @pl.when(tile_ref[0] == tile)
        def _(tile=tile):
            ada_ref[...] = dot_tn(silu_ref[...], mod_ref[:, share * tile : share * (tile + 1)])

    rows = [mod_ref[k : k + 1, :].astype(F32) for k in range(count)]
    while len(rows) > 1:
        rows = [rows[k] + rows[k + 1] for k in range(0, len(rows), 2)]
    bias_ref[...] = rows[0]
    cond_ref[...] = dot_nt(mod_ref[:, :width], w_ref[...])


def ada_back(tile, mod_all, w_ada, silu_rows):
    count, wide = mod_all.shape
    shard, width = w_ada.shape
    return pl.pallas_call(
        ada_kernel,
        out_shape=[
            jax.ShapeDtypeStruct((shard, width // 4), F32),
            jax.ShapeDtypeStruct((1, wide), F32),
            jax.ShapeDtypeStruct((count, shard), F32),
        ],
        in_specs=[smem()] + [vmem()] * 3,
        out_specs=[vmem()] * 3,
        cost_estimate=cost(3.5),
        compiler_params=limit(12),
        name="ada_back",
    )(tile, mod_all, w_ada, silu_rows)


def reorder_kernel(index_ref, rows_ref, out_ref):
    for k in range(rows_ref.shape[0]):
        out_ref[k : k + 1, :] = rows_ref[pl.ds(index_ref[k], 1), :]


def reorder(index, rows):
    return pl.pallas_call(
        reorder_kernel,
        out_shape=jax.ShapeDtypeStruct(rows.shape, rows.dtype),
        in_specs=[smem(), vmem()],
        out_specs=vmem(),
        cost_estimate=cost(1.3),
        compiler_params=limit(4),
        name="reorder",
    )(index, rows)


def lane_matrix():
    matrix = np.zeros((HEAD, LANES), np.float32)
    for index in range(HEAD):
        matrix[index, head_lane(index)] = 1.0
    return matrix


def rope_lanes(tile_rows, tile_cols):
    freqs = (10000.0 ** (-np.arange(QUARTER, dtype=np.float64) / QUARTER)).astype(np.float32)
    freq = np.zeros((LANES,), np.float32)
    part = np.zeros((LANES,), np.int32)
    sign = np.zeros((LANES,), np.float32)
    for index in range(HEAD):
        lane = head_lane(index)
        freq[lane] = freqs[index % QUARTER]
        part[lane] = index // 36
        sign[lane] = 1.0 if lane >= 64 else -1.0
    per_tile = tile_rows * tile_cols
    ids = np.arange(4 * per_tile)
    flips = np.array(FLIPS)[ids // per_tile]
    ty = lax.axis_index("ty") ^ jnp.asarray(flips >> 1, jnp.int32)
    tx = lax.axis_index("tx") ^ jnp.asarray(flips & 1, jnp.int32)
    rows = (ty * tile_rows + jnp.asarray(ids % per_tile // tile_cols, jnp.int32)).astype(F32)
    cols = (tx * tile_cols + jnp.asarray(ids % tile_cols, jnp.int32)).astype(F32)
    angle = jnp.where(jnp.asarray(part)[None] == 0, rows[:, None], cols[:, None]) * jnp.asarray(freq)[None]
    live = jnp.asarray((sign != 0).astype(np.float32))[None]
    return jnp.cos(angle) * live, jnp.sin(angle) * jnp.asarray(sign)[None]


def gain_lanes(gain):
    return jnp.sum(jnp.asarray(lane_matrix()) * gain[:, None], axis=0, keepdims=True)


def gain_back(lanes):
    return jnp.sum(jnp.asarray(lane_matrix()) * lanes[None, :], axis=1)


def tile_pair(far):
    return (far[0].astype(F32) + swap(far[1], "tx").astype(F32)).astype(BF16)


def tile_sum_parts(pair, near):
    return near[0], swap(near[1], "tx"), swap(pair, "ty")


def body(
    count, tokens, cond, live_count, w_qkv, w_out, w_gu, w_down, w_ada, ada_bias, q_gain, k_gain, cotangent
):
    _, tile_rows, tile_cols, width = tokens.shape
    per_tile = tile_rows * tile_cols
    img, ty, tx = lax.axis_index("img"), lax.axis_index("ty"), lax.axis_index("tx")
    tile = ty * 2 + tx
    tile_word = tile[None].astype(jnp.int32)
    live = (live_count[0] > 0).astype(F32)
    shard = width // count
    ff_shard = FF // count
    ff_own = ff_shard // TILES
    hidden_own = FF // TILES
    out_width = width // TILES
    spread = jnp.asarray(spread_matrices(), BF16)

    first = jnp.concatenate(
        [lax.dynamic_slice_in_dim(w_qkv, p * width + tile * COLS, COLS, 1) for p in range(3)]
        + [lax.dynamic_slice_in_dim(w_out, tile * out_width, out_width, 1)],
        axis=1,
    )
    down_own = lax.dynamic_slice_in_dim(w_down, tile * ff_own, ff_own, 0)
    gu_own = lax.dynamic_slice_in_dim(w_gu.reshape(shard, 2 * count, ff_shard), tile * ff_own, ff_own, 2)
    gu_own = gu_own.reshape(shard, 2 * hidden_own)

    x_own = tokens.reshape(per_tile, width)
    dy_own = cotangent.reshape(per_tile, width)
    x_tiles = gather_tiles(x_own)

    cond_float = cond.astype(F32)
    bits = [1 << k for k in range(count.bit_length() - 1)]
    store = {}

    def gather_step(v, bit):
        return jnp.concatenate([v, lax.ppermute(v, "img", flip_perm(count, bit))])

    def scatter_step(v, bit):
        return v[:bit] + lax.ppermute(v[bit:], "img", flip_perm(count, bit))

    silu_some = gather_step(jax.nn.silu(cond_float).astype(BF16), bits[0])

    def rows_step(v):
        store["silu_rows"] = lax.dynamic_slice_in_dim(gather_step(v, bits[-1]), img * shard, shard, 1)
        return store["silu_rows"]

    def dy_step(v):
        store["dy"] = gather_tiles(after(dy_own, v))
        return v

    beside = [lambda _, bit=bit: gather_step(silu_some if _ is None else _, bit) for bit in bits[1:-1]]
    beside += [rows_step, lambda v: scatter_step(dot(v, w_ada), bits[-1])]
    beside += [lambda v, bit=bit: scatter_step(v, bit) for bit in bits[-2::-1]]
    early, middle_step, late = beside[2], beside[3], beside[-1]
    beside[2] = lambda v: after(early(v), x_tiles)
    beside[3] = lambda v: middle_step(dy_step(v))
    beside.append(lambda v: after(v, store["dy"]))

    ring = use_ring(count, math.gcd(shard, ff_own))
    if ring:
        own = after(jnp.concatenate([first, down_own]), silu_some)
        pieces, modulation = ring_gather(own, count, beside)
        full_first, full_down, out_own = assemble(
            own,
            pieces,
            [(width, width), (hidden_own, width), (COLS, width)],
            [(0, shard, 0, shard, 0, 0, 0, width), (1, ff_own, shard, ff_own, 0, 0, 0, width)],
            count,
            True,
        )
        full_gu = lax.all_gather(after(gu_own, pieces[GU_AFTER]), "img", axis=0, tiled=True)
    else:
        full_first, full_down, full_gu = [
            lax.all_gather(a, "img", axis=0, tiled=True) for a in (first, down_own, gu_own)
        ]
        out_own = out_share(out_pick(), full_first)
        modulation = None
        for step in beside:
            modulation = step(modulation)
    silu_rows = store["silu_rows"]
    dy_tiles = store["dy"]
    modulation = modulation + ada_bias
    mod = jnp.concatenate([modulation.reshape(6, width), jnp.broadcast_to(live, (2, width))])

    cos, sin = rope_lanes(tile_rows, tile_cols)
    gq, gk = gain_lanes(q_gain), gain_lanes(k_gain)
    attn_in, qraw, kraw, q0, q1, k0, k1, v0, v1 = project(
        x_tiles, mod, full_first, cos, sin, gq, gk, spread
    )
    out_far = swap(out_own, "ty")
    out_far = after(out_far, attn_in)
    full_out, out_rows = out_weight(
        tile_word, [out_far, swap(out_far, "tx"), out_own, swap(out_own, "tx")]
    )
    q0, mixedp0, mixed0 = attend(q0, k0, v0, spread)
    mixed = gather_tiles(mixed0)
    q1, mixedp1, mixed1 = attend(after(q1, full_out, mixed0), k1, v1, spread)
    mixed += gather_tiles(mixed1)

    grad_branch = branch_grad(mod, after(dy_tiles, mixed1))
    mlp_in, attended = residual(tile_word, mod, full_out, after(x_tiles, grad_branch), mixed)
    weights = (full_gu, full_down, mlp_in, grad_branch)
    far = mlp((1, 0), *weights, ())
    grad_pair = tile_pair((far[5], far[4]))
    grad_far = swap(grad_pair, "ty")
    beside_tile = mlp((3,), *weights, after(far[:2], grad_pair))
    own_tile = mlp((2,), *weights, beside_tile[:2])
    hidden, grad_gu = own_tile[:2]

    grad_att, grad_mid, mid_sums = middle(
        (own_tile[3], swap(beside_tile[3], "tx"), grad_far), attended, x_own, dy_own, mod
    )
    g_gu = weight_grad(mlp_in, after(grad_gu, grad_att), 5)
    g_down = weight_grad(hidden, after(grad_branch, g_gu), 3)
    branch_pair = tile_pair((far[3], far[2]))
    att_far = after(swap(grad_att, "ty"), g_gu, g_down, branch_pair)
    grad_att_tiles = [att_far, swap(att_far, "tx"), grad_att, swap(grad_att, "tx")]

    grad_qkv, gains = attention_backward(
        grad_att_tiles, out_rows, qraw, kraw, (q0, q1), (k0, k1), (v0, v1), (mixedp0, mixedp1),
        cos, sin, gq, gk, spread,
    )
    branch_parts = tile_sum_parts(branch_pair, (own_tile[2], beside_tile[2]))
    grad_qkv = after(grad_qkv, branch_parts)
    w_back = full_first[:, : 3 * COLS]
    g_first = first_grad(tile_word, grad_att_tiles, mixed, attn_in, grad_qkv)
    back_qkv = after(grad_qkv, g_first)
    back_far = dot_nt(back_qkv[: 2 * per_tile], w_back).astype(BF16)
    halves = lambda rows: (rows[:per_tile], rows[per_tile:])
    back_pair = tile_pair(halves(back_far))
    back_near = dot_nt(after(back_qkv, back_pair)[2 * per_tile :], w_back).astype(BF16)

    wide = 6 * width

    def output_step():
        store["output"], store["out_sums"] = output_tile(
            branch_parts, attended, x_own, dy_own, mod
        )
        return store["out_sums"]

    def token_step():
        parts = tile_sum_parts(back_pair, halves(back_near))
        store["grad_tokens"], tok_sums = tokens_back(parts, x_own, grad_mid, mod)
        return jnp.concatenate(
            [tok_sums[0], tok_sums[1], mid_sums[0], mid_sums[1], mid_sums[2], store["out_sums"][0], gains[0], gains[1]]
        )[None]

    def low_step(grad_mod):
        return jnp.concatenate([grad_mod[:, :wide].astype(BF16), *three_parts(grad_mod[:, wide:])], axis=1)

    def ada_step(mod_all):
        store["grad_ada"], store["sums"], grad_silu = ada_back(tile_word, mod_all, w_ada, silu_rows)
        return grad_silu

    steps = [lambda _: output_step(), lambda _: token_step(), lambda v: low_step(sum_tiles(v))]
    steps += [lambda v, bit=bit: gather_step(v, bit) for bit in bits]
    steps.append(lambda v: flip_exchange(ada_step(v), count, bits[-1:]))

    if ring:
        s_gu = lax.psum_scatter(g_gu, "img", scatter_dimension=0, tiled=True)
        gu_cols = 2 * hidden_own // TILES

        def gu_piece(flip):
            return lax.dynamic_slice_in_dim(s_gu, tile_at(flip) * gu_cols, gu_cols, 1)

        def gu_tx_step(v):
            store["gu_tx"] = swap(jnp.concatenate([gu_piece(1), gu_piece(3)]), "tx")
            return after(v, store["gu_tx"])

        def gu_ty_step(v):
            store["gu_ty"] = swap(jnp.concatenate([gu_piece(2), store["gu_tx"][shard:]]), "ty")
            return after(v, store["gu_ty"])

        tied = steps[TIE_BY]
        steps[TIE_BY] = lambda v: after(tied(v), s_gu)
        first_half, second_half = steps[GU_BY], steps[GU_BY + 1]
        steps[GU_BY] = lambda v: gu_tx_step(first_half(v))
        steps[GU_BY + 1] = lambda v: gu_ty_step(second_half(v))
        s_all, grad_silu = ring_scatter([g_first, g_down], count, steps)
    else:
        grad_silu = None
        for step in steps:
            grad_silu = step(grad_silu) if step else None
    grad_tokens, grad_ada, sums = store["grad_tokens"], store["grad_ada"], store["sums"]
    grad_bias = sums[0, :wide]
    gain_sums = (sums[:, wide : wide + 256] + sums[:, wide + 256 : wide + 512]) + sums[:, wide + 512 :]
    if ring:
        to_tx, to_ty, *kept, grad_w_out = pack(tile_word, s_all, shard, ff_own)
        from_tx = swap(to_tx, "tx")
        passed_on = swap(from_tx[ff_own : 2 * ff_own], "ty")
        from_ty = swap(to_ty, "ty")
        grad_w_gu, grad_down, grad_w_qkv = unpack(
            tile_word, from_tx, from_ty, passed_on, kept, (s_gu, store["gu_tx"], store["gu_ty"]), shard, ff_own
        )
        grad_silu = after(grad_silu, from_tx)
    else:
        sums_of = lambda grad: lax.psum_scatter(grad, "img", scatter_dimension=0, tiled=True)
        s_first, s_down, s_gu = sums_of(g_first).astype(F32), sums_of(g_down), sums_of(g_gu)
        gu_cols = 2 * hidden_own // TILES
        got = exchange_tiles(lambda t: lax.dynamic_slice_in_dim(s_gu, t * gu_cols, gu_cols, 1))
        grad_w_out = s_first[:, 3 * COLS :].astype(F32)
        s_qkv = s_first.astype(BF16)

        grad_down = jnp.concatenate(
            exchange_tiles(lambda t: lax.dynamic_slice_in_dim(s_down, t * out_width, out_width, 1))
        ).astype(F32)
        grad_w_gu = jnp.concatenate(
            [got[s][:, ff_own * g : ff_own * (g + 1)] for g in range(gu_cols // ff_own) for s in range(4)],
            axis=1,
        ).astype(F32)
        units = [s_qkv[:, COLS * p : COLS * (p + 1)] for p in range(3)]

        def choose(options, table):
            result = options[table[0]]
            for t in range(1, 4):
                if table[t] != table[0]:
                    result = jnp.where(tile == t, options[table[t]], result)
            return result

        slots = [
            choose(units, KEPT),
            swap(choose(units, TO_TX), "tx"),
            swap(choose(units, TO_TY), "ty"),
        ]
        grad_w_qkv = jnp.concatenate(
            [choose(slots, [SLOTS[t][k] for t in range(4)]) for k in range(3)], axis=1
        ).astype(F32)

    flips = (jnp.arange(count, dtype=jnp.int32) ^ img).astype(jnp.int32)
    grad_silu = flip_exchange(grad_silu, count, bits[-2::-1])
    grad_silu = reorder(flips, grad_silu).reshape(1, width)
    sigmoid_c = jax.nn.sigmoid(cond_float)
    grad_cond = (grad_silu * sigmoid_c * (1.0 + cond_float * (1.0 - sigmoid_c))).astype(BF16)

    return (
        store["output"].reshape(tokens.shape),
        grad_tokens.reshape(tokens.shape),
        grad_cond,
        grad_w_qkv,
        grad_w_out,
        grad_w_gu,
        grad_down,
        grad_ada,
        gain_back(gain_sums[0, :LANES]),
        gain_back(gain_sums[0, LANES:]),
        grad_bias,
    )


def solution(mesh):
    tiled = P("img", "ty", "tx", None)
    rows = P("img", None)
    cut = P("img", ("ty", "tx"))
    in_specs = (tiled, rows, P("img"), rows, rows, rows, rows, rows, P(), P(), P(), tiled)
    out_specs = (tiled, tiled, rows, cut, cut, cut, cut, cut, P(), P(), P())
    return jax.shard_map(
        functools.partial(body, mesh.shape["img"]),
        mesh=mesh,
        in_specs=in_specs,
        out_specs=out_specs,
        check_vma=False,
    )
```
